32 devices in a mesh: groups: 2 (over y), chain: 4 (over z), clus: 4 (over x, core).
Axes of the slice: x: 2, y: 2, z: 4, core: 2. Of those that a mesh axis runs over, the one named last changes fastest.
Arguments:
- embeddings: bfloat16 [16384, 768], P(('groups', 'chain', 'clus')), parts along dimension 0
- dest: int32 [16384], P(('groups', 'chain', 'clus')), parts along dimension 0, may hold values from 0 to 8191, as said below
- sizes: int32 [8], P('groups'), parts along dimension 0, may hold values from 256 to 2048, as said below
Outputs:
- best: float32 [8, 2048], P(('groups', 'clus'), 'chain'), parts along dimension 0
The draws below stay inside these ranges and needn't reach their ends.
There are 2 independent parts, one for each index of `groups`. The reference program is written for one: setup_inputs(seed, part) draws one part's arguments, and reference() takes and returns one part's arrays. A program takes and returns all parts, laid end to end along the dimension named above; each array names one. Nothing has to cross between parts.
Inputs may be any that keep to these rules, and one draw needn't show every extreme that they name: `dest`: a permutation of the slots of the group; every data shard of 512 rows holds exactly 16 rows for each aligned run of 256 slots. `sizes`: some cluster has exactly 2048 members.
All inputs are finite; a program needn't handle non-finite values.
Results may differ from the reference program's by a relative error of at most 0.00054.
Values may be sent and summed in bfloat16 or wider, within the bound.
No kernel may reach another device: no remote copies, remote signals or barrier semaphores. Data moves between devices by JAX's collectives and lax.ppermute only.
A program may use at most 64 MiB of HBM per device.

```python
import math
import jax
import jax.numpy as jnp
from jax import lax

D = 768
ROWS_DEV = 512
SHARDS = 16
CLUSTER_ROWS = 2048
CLUSTERS = 4


def shuffle_positions(key):
    half = ROWS_DEV // 2
    blocks = CLUSTERS * (2 * CLUSTER_ROWS // ROWS_DEV)
    each = half // SHARDS
    first_key, second_key = jax.random.split(jax.random.fold_in(key, 11))
    base = jnp.tile(jnp.arange(half, dtype=jnp.int32), (blocks, 1))
    within = jax.random.permutation(first_key, base, axis=1, independent=True)
    positions = within + (jnp.arange(blocks, dtype=jnp.int32) * half)[:, None]
    positions = positions.reshape(blocks, SHARDS, each).transpose(1, 0, 2).reshape(SHARDS, ROWS_DEV)
    positions = jax.random.permutation(second_key, positions, axis=1, independent=True)
    return positions.reshape(-1)


def draw_dest(key, part):
    return shuffle_positions(key)


def draw_embeddings(key, part):
    positions = shuffle_positions(key)
    key = jax.random.fold_in(key, 5)
    key_topic, key_center, key_strength, key_noise = jax.random.split(key, 4)
    total = CLUSTERS * CLUSTER_ROWS
    topics_count = CLUSTER_ROWS // 8
    topic_of = jax.random.randint(key_topic, (total,), 0, topics_count)
    centers = jax.random.normal(key_center, (CLUSTERS, topics_count, D), jnp.float32)
    strength = jnp.exp(jax.random.uniform(key_strength, (total, 1), jnp.float32, math.log(0.3), math.log(3.0)))
    cluster = positions // CLUSTER_ROWS
    center = centers[cluster, topic_of[positions]]
    noise = jax.random.normal(key_noise, (total, D), jnp.float32)
    values = noise + strength * center
    return values.astype(jnp.bfloat16)


def draw_sizes(key, part):
    key = jax.random.fold_in(key, 7)
    key_sizes, key_full = jax.random.split(key)
    counts = jax.random.randint(key_sizes, (CLUSTERS,), CLUSTER_ROWS // 8, CLUSTER_ROWS + 1)
    full_one = jax.random.randint(key_full, (), 0, CLUSTERS)
    return jnp.where(jnp.arange(CLUSTERS, dtype=jnp.int32) == full_one, CLUSTER_ROWS, counts).astype(jnp.int32)


def setup_inputs(seed: int = 0, part: int = 0) -> dict:
    seeds = jax.random.split(jax.random.key(seed), 4)
    part_keys = jax.random.split(jax.random.fold_in(seeds[3], part), 4)
    return {
        "embeddings": draw_embeddings(jax.random.fold_in(jax.random.fold_in(seeds[3], part), 71), part),
        "dest": draw_dest(jax.random.fold_in(jax.random.fold_in(seeds[3], part), 71), part),
        "sizes": draw_sizes(jax.random.fold_in(jax.random.fold_in(seeds[3], part), 71), part),
    }


block_rows = 256

def block_best(units, index):
    rows_start = index * block_rows
    queries = lax.dynamic_slice_in_dim(units, rows_start, block_rows, 0)
    query_pos = rows_start + jnp.arange(block_rows, dtype=jnp.int32)

    def step(kblock, current):
        keys = lax.dynamic_slice_in_dim(units, kblock * block_rows, block_rows, 0)
        scores = jnp.dot(queries, keys.T, preferred_element_type=jnp.float32)
        key_pos = kblock * block_rows + jnp.arange(block_rows, dtype=jnp.int32)
        masked = jnp.where(key_pos[None, :] < query_pos[:, None], scores, -2.0)
        return jnp.maximum(current, lax.optimization_barrier(jnp.max(masked, axis=1)))
    start_best = jnp.full((block_rows,), -1.0, jnp.float32)
    return lax.fori_loop(jnp.int32(0), index + 1, step, start_best)

def cluster_best(pair):
    units, count = pair
    blocks = jnp.arange(CLUSTER_ROWS // block_rows, dtype=jnp.int32)
    values = lax.map(lambda index: block_best(units, index), blocks).reshape(CLUSTER_ROWS)
    where_pos = jnp.arange(CLUSTER_ROWS, dtype=jnp.int32)
    return jnp.where(where_pos < count, values, jnp.zeros_like(values))

def reference(embeddings, dest, sizes):
    clustered = jnp.zeros((CLUSTERS * CLUSTER_ROWS, D), embeddings.dtype).at[dest].set(embeddings)
    floats = clustered.astype(jnp.float32)
    units = (floats * lax.rsqrt(lax.optimization_barrier(jnp.sum(floats * floats, axis=1, keepdims=True)) + 1e-06)).astype(jnp.bfloat16)
    units = units.reshape(CLUSTERS, CLUSTER_ROWS, D)
    return lax.map(cluster_best, (units, sizes))
```

```python
import functools

import jax
import jax.numpy as jnp
from jax import lax
from jax.experimental import pallas as pl
from jax.experimental.pallas import tpu as pltpu
from jax.sharding import PartitionSpec as P

PIECE = 16
VMEM = pl.BlockSpec(memory_space=pltpu.VMEM)
SMEM = pl.BlockSpec(memory_space=pltpu.SMEM)


def sort_kernel(run_slots, dest_ref, rows_ref, units_ref, slots_ref):
    rows = rows_ref.shape[0]
    runs = rows // PIECE
    dest = dest_ref[...]
    run = dest // run_slots
    within = dest % run_slots
    member = lax.broadcasted_iota(jnp.int32, (runs, rows), 0) == run
    before = lax.broadcasted_iota(jnp.int32, (rows, rows), 0) < lax.broadcasted_iota(
        jnp.int32, (rows, rows), 1
    )
    earlier = jnp.dot(
        member.astype(jnp.float32).astype(jnp.bfloat16),
        before.astype(jnp.float32).astype(jnp.bfloat16),
        preferred_element_type=jnp.float32,
    )
    rank = jnp.sum(jnp.where(member, earlier, 0.0), axis=0, keepdims=True).astype(jnp.int32)
    placed = run * PIECE + rank
    hot = (lax.broadcasted_iota(jnp.int32, (rows, rows), 0) == placed).astype(jnp.float32)
    hot = hot.astype(jnp.bfloat16)
    x = rows_ref[...].astype(jnp.float32)
    units = (x * lax.rsqrt(jnp.sum(x * x, axis=1, keepdims=True) + 1e-06)).astype(jnp.bfloat16)
    units_ref[...] = jnp.dot(hot, units, preferred_element_type=jnp.float32).astype(jnp.bfloat16)
    halves = jnp.concatenate(
        [jnp.broadcast_to(within // 256, (8, rows)), jnp.broadcast_to(within % 256, (8, rows))], axis=0
    )
    moved = lax.dot_general(
        halves.astype(jnp.float32).astype(jnp.bfloat16),
        hot,
        (((1,), (1,)), ((), ())),
        preferred_element_type=jnp.float32,
    )
    slots_ref[...] = (moved[0:1, :] * 256.0 + moved[8:9, :]).astype(jnp.int32)


def best_kernel(info_ref, slots_ref, keys_ref, out_ref, query_ref):
    shards, depth, width = keys_ref.shape
    queries = out_ref.shape[1]
    run_slots = shards * PIECE
    unit = min(run_slots, queries)
    first = info_ref[0]
    members = info_ref[1]
    first_run = first // run_slots

    def run_rows(run):
        start = pl.multiple_of(run * PIECE, PIECE)
        return keys_ref[:, pl.ds(start, PIECE), :].reshape(run_slots, width)

    def run_positions(run):
        start = pl.multiple_of(run * PIECE, PIECE)
        tile = slots_ref[pl.ds(start, PIECE), :]
        wide = jnp.broadcast_to(tile[None], (shards, PIECE, shards)).reshape(run_slots, shards)
        lane = lax.broadcasted_iota(jnp.int32, (run_slots, shards), 1)
        row = lax.broadcasted_iota(jnp.int32, (run_slots, shards), 0)
        picked = jnp.sum(jnp.where(lane == row // PIECE, wide, 0), axis=1, keepdims=True)
        return picked + run * run_slots

    for index in range(queries // unit):
        run = first_run + index
        lanes = lax.broadcasted_iota(jnp.int32, (run_slots, unit), 1) + (first + index * unit)
        hot = (run_positions(run) == lanes).astype(jnp.float32).astype(jnp.bfloat16)
        query_ref[:, index * unit : (index + 1) * unit] = lax.dot_general(
            run_rows(run), hot, (((0,), (0,)), ((), ())), preferred_element_type=jnp.float32
        ).astype(jnp.bfloat16)

    def fold(scores):
        return jnp.max(scores.reshape(run_slots // 8, 8, queries), axis=0)

    def step(run, running):
        scores = jnp.dot(run_rows(run), query_ref[...], preferred_element_type=jnp.float32)
        return jnp.maximum(running, fold(scores))

    running = lax.fori_loop(0, first_run, step, jnp.full((8, queries), -1.0, jnp.float32))
    position = first + lax.broadcasted_iota(jnp.int32, (1, queries), 1)
    for index in range(queries // unit):
        run = first_run + index
        scores = jnp.dot(run_rows(run), query_ref[...], preferred_element_type=jnp.float32)
        masked = jnp.where(run_positions(run) < position, scores, -2.0)
        running = jnp.maximum(running, fold(masked))
    found = jnp.max(running, axis=0, keepdims=True)
    out_ref[...] = jnp.where(position < members, found, 0.0)


def local(embeddings, dest, sizes):
    chain_len = lax.axis_size("chain")
    clus_len = lax.axis_size("clus")
    shards = chain_len * clus_len
    rows, width = embeddings.shape
    clusters = sizes.shape[0]
    parts = chain_len // clusters
    run_slots = shards * PIECE
    depth = rows // chain_len
    my_chain = lax.axis_index("chain")
    my_clus = lax.axis_index("clus")
    cluster = my_chain // parts
    part = my_chain % parts

    units, slots = pl.pallas_call(
        functools.partial(sort_kernel, run_slots),
        out_shape=(
            jax.ShapeDtypeStruct((rows, width), jnp.bfloat16),
            jax.ShapeDtypeStruct((1, rows), jnp.int32),
        ),
        in_specs=[VMEM, VMEM],
        out_specs=(VMEM, VMEM),
        compiler_params=pltpu.CompilerParams(vmem_limit_bytes=32 * 2**20),
        name="sort_units",
    )(dest.reshape(1, rows), embeddings)

    slots = lax.all_gather(slots, ("chain", "clus"), axis=0, tiled=True)
    slots = slots.reshape(chain_len, clus_len, clusters, -1, PIECE)
    slots = lax.dynamic_index_in_dim(slots, cluster, 2, keepdims=False)
    slots = slots.transpose(2, 3, 1, 0).reshape(-1, shards)

    got = lax.all_to_all(units, "chain", split_axis=0, concat_axis=0, tiled=True)
    keys = lax.all_gather(got, "clus", axis=0, tiled=True).reshape(shards, depth, width)
    if parts > 1:
        pieces = []
        for wanted in range(parts):
            block = keys
            for other in range(parts):
                if other != wanted:
                    pairs = [(c * parts + wanted, c * parts + other) for c in range(clusters)]
                    came = lax.ppermute(keys, "chain", pairs)
                    block = jnp.where(part == other, came, block)
            pieces.append(block)
        keys = jnp.concatenate(pieces, axis=1)

    first = (part * clus_len + my_clus) * rows
    ids = jnp.arange(clusters, dtype=jnp.int32)
    members = jnp.sum(jnp.where(ids == cluster, sizes, 0))
    info = jnp.stack([first, members]).astype(jnp.int32)
    found = pl.pallas_call(
        best_kernel,
        out_shape=jax.ShapeDtypeStruct((1, rows), jnp.float32),
        in_specs=[SMEM, VMEM, VMEM],
        out_specs=VMEM,
        scratch_shapes=[pltpu.VMEM((width, rows), jnp.bfloat16)],
        compiler_params=pltpu.CompilerParams(vmem_limit_bytes=48 * 2**20),
        name="best_of_earlier",
    )(info, slots, keys)

    pairs = []
    for z in range(chain_len):
        for k in range(clus_len):
            pairs.append((z * clus_len + k, ((z % parts) * clus_len + k) * clus_len + z // parts))
    return lax.ppermute(found, ("chain", "clus"), pairs)


def solution(mesh):
    return jax.shard_map(
        local,
        mesh=mesh,
        in_specs=(
            P(("groups", "chain", "clus"), None),
            P(("groups", "chain", "clus")),
            P("groups"),
        ),
        out_specs=P(("groups", "clus"), "chain"),
        check_vma=False,
    )
```

```python
import functools

import jax
import jax.numpy as jnp
from jax import lax
from jax.experimental import pallas as pl
from jax.experimental.pallas import tpu as pltpu
from jax.sharding import PartitionSpec as P

PIECE = 16
VMEM = pl.BlockSpec(memory_space=pltpu.VMEM)
SMEM = pl.BlockSpec(memory_space=pltpu.SMEM)
HBM = pl.BlockSpec(memory_space=pltpu.HBM)


def as_bf16(mask):
    return mask.astype(jnp.float32).astype(jnp.bfloat16)


def sort_kernel(run_slots, dest_ref, rows_ref, units_ref, slots_ref):
    rows = rows_ref.shape[0]
    runs = rows // PIECE
    dest = dest_ref[...]
    run = dest // run_slots
    within = dest % run_slots
    member = lax.broadcasted_iota(jnp.int32, (runs, rows), 0) == run
    before = lax.broadcasted_iota(jnp.int32, (rows, rows), 0) < lax.broadcasted_iota(
        jnp.int32, (rows, rows), 1
    )
    earlier = jnp.dot(
        member.astype(jnp.float32).astype(jnp.bfloat16),
        before.astype(jnp.float32).astype(jnp.bfloat16),
        preferred_element_type=jnp.float32,
    )
    rank = jnp.sum(jnp.where(member, earlier, 0.0), axis=0, keepdims=True).astype(jnp.int32)
    placed = run * PIECE + rank
    hot = (lax.broadcasted_iota(jnp.int32, (rows, rows), 0) == placed).astype(jnp.float32)
    hot = hot.astype(jnp.bfloat16)
    x = rows_ref[...].astype(jnp.float32)
    units = (x * lax.rsqrt(jnp.sum(x * x, axis=1, keepdims=True) + 1e-06)).astype(jnp.bfloat16)
    units_ref[...] = jnp.dot(hot, units, preferred_element_type=jnp.float32).astype(jnp.bfloat16)
    halves = jnp.concatenate(
        [jnp.broadcast_to(within // 256, (8, rows)), jnp.broadcast_to(within % 256, (8, rows))], axis=0
    )
    moved = lax.dot_general(
        halves.astype(jnp.float32).astype(jnp.bfloat16),
        hot,
        (((1,), (1,)), ((), ())),
        preferred_element_type=jnp.float32,
    )
    slots_ref[...] = (moved[0:1, :] * 256.0 + moved[8:9, :]).astype(jnp.int32)


def best_kernel(info_ref, slots_ref, keys_ref, out_ref, query_ref):
    shards, depth, width = keys_ref.shape
    queries = out_ref.shape[1]
    run_slots = shards * PIECE
    unit = min(run_slots, queries)
    first = info_ref[0]
    members = info_ref[1]
    first_run = first // run_slots

    def run_rows(run):
        start = pl.multiple_of(run * PIECE, PIECE)
        return keys_ref[:, pl.ds(start, PIECE), :].reshape(run_slots, width)

    def run_positions(run):
        start = pl.multiple_of(run * PIECE, PIECE)
        tile = slots_ref[pl.ds(start, PIECE), :]
        wide = jnp.broadcast_to(tile[None], (shards, PIECE, shards)).reshape(run_slots, shards)
        lane = lax.broadcasted_iota(jnp.int32, (run_slots, shards), 1)
        row = lax.broadcasted_iota(jnp.int32, (run_slots, shards), 0)
        picked = jnp.sum(jnp.where(lane == row // PIECE, wide, 0), axis=1, keepdims=True)
        return picked + run * run_slots

    for index in range(queries // unit):
        run = first_run + index
        lanes = lax.broadcasted_iota(jnp.int32, (run_slots, unit), 1) + (first + index * unit)
        hot = (run_positions(run) == lanes).astype(jnp.float32).astype(jnp.bfloat16)
        query_ref[:, index * unit : (index + 1) * unit] = lax.dot_general(
            run_rows(run), hot, (((0,), (0,)), ((), ())), preferred_element_type=jnp.float32
        ).astype(jnp.bfloat16)

    def fold(scores):
        return jnp.max(scores.reshape(run_slots // 8, 8, queries), axis=0)

    def step(run, running):
        scores = jnp.dot(run_rows(run), query_ref[...], preferred_element_type=jnp.float32)
        return jnp.maximum(running, fold(scores))

    running = lax.fori_loop(0, first_run, step, jnp.full((8, queries), -1.0, jnp.float32))
    position = first + lax.broadcasted_iota(jnp.int32, (1, queries), 1)
    for index in range(queries // unit):
        run = first_run + index
        scores = jnp.dot(run_rows(run), query_ref[...], preferred_element_type=jnp.float32)
        masked = jnp.where(run_positions(run) < position, scores, -2.0)
        running = jnp.maximum(running, fold(masked))
    found = jnp.max(running, axis=0, keepdims=True)
    out_ref[...] = jnp.where(position < members, found, 0.0)


def local_plane(embeddings, dest, sizes):
    chain_len = lax.axis_size("chain")
    clus_len = lax.axis_size("clus")
    shards = chain_len * clus_len
    rows, width = embeddings.shape
    clusters = sizes.shape[0]
    parts = chain_len // clusters
    run_slots = shards * PIECE
    depth = rows // chain_len
    my_chain = lax.axis_index("chain")
    my_clus = lax.axis_index("clus")
    cluster = my_chain // parts
    part = my_chain % parts

    units, slots = pl.pallas_call(
        functools.partial(sort_kernel, run_slots),
        out_shape=(
            jax.ShapeDtypeStruct((rows, width), jnp.bfloat16),
            jax.ShapeDtypeStruct((1, rows), jnp.int32),
        ),
        in_specs=[VMEM, VMEM],
        out_specs=(VMEM, VMEM),
        compiler_params=pltpu.CompilerParams(vmem_limit_bytes=32 * 2**20),
        name="sort_units",
    )(dest.reshape(1, rows), embeddings)

    slots = lax.all_gather(slots, ("chain", "clus"), axis=0, tiled=True)
    slots = slots.reshape(chain_len, clus_len, clusters, -1, PIECE)
    slots = lax.dynamic_index_in_dim(slots, cluster, 2, keepdims=False)
    slots = slots.transpose(2, 3, 1, 0).reshape(-1, shards)

    got = lax.all_to_all(units, "chain", split_axis=0, concat_axis=0, tiled=True)
    keys = lax.all_gather(got, "clus", axis=0, tiled=True).reshape(shards, depth, width)
    if parts > 1:
        pieces = []
        for wanted in range(parts):
            block = keys
            for other in range(parts):
                if other != wanted:
                    pairs = [(c * parts + wanted, c * parts + other) for c in range(clusters)]
                    came = lax.ppermute(keys, "chain", pairs)
                    block = jnp.where(part == other, came, block)
            pieces.append(block)
        keys = jnp.concatenate(pieces, axis=1)

    first = (part * clus_len + my_clus) * rows
    ids = jnp.arange(clusters, dtype=jnp.int32)
    members = jnp.sum(jnp.where(ids == cluster, sizes, 0))
    info = jnp.stack([first, members]).astype(jnp.int32)
    found = pl.pallas_call(
        best_kernel,
        out_shape=jax.ShapeDtypeStruct((1, rows), jnp.float32),
        in_specs=[SMEM, VMEM, VMEM],
        out_specs=VMEM,
        scratch_shapes=[pltpu.VMEM((width, rows), jnp.bfloat16)],
        compiler_params=pltpu.CompilerParams(vmem_limit_bytes=48 * 2**20),
        name="best_of_earlier",
    )(info, slots, keys)

    pairs = []
    for z in range(chain_len):
        for k in range(clus_len):
            pairs.append((z * clus_len + k, ((z % parts) * clus_len + k) * clus_len + z // parts))
    return lax.ppermute(found, ("chain", "clus"), pairs)


def lengths(embeddings):
    chain_len = lax.axis_size("chain")
    clus_len = lax.axis_size("clus")
    return chain_len, clus_len, embeddings.shape[0], embeddings.shape[1]


def send_kernel(run_slots, cluster_runs, dest_ref, rows_ref, *rest):
    block_refs, (x_ref, sem) = rest[:-2], rest[-2:]
    copy = pltpu.make_async_copy(rows_ref, x_ref, sem)
    copy.start()
    my_clus = lax.axis_index("clus")
    rows, width = x_ref.shape
    runs = rows // PIECE
    depth = rows // len(block_refs)
    dest = dest_ref[...]
    run = lax.div(dest, run_slots)
    within = lax.rem(dest, run_slots)
    run = (lax.div(run, cluster_runs) ^ my_clus) * cluster_runs + lax.rem(run, cluster_runs)
    member = lax.broadcasted_iota(jnp.int32, (runs, rows), 0) == run
    before = lax.broadcasted_iota(jnp.int32, (rows, rows), 0) < lax.broadcasted_iota(
        jnp.int32, (rows, rows), 1
    )
    earlier = jnp.dot(as_bf16(member), as_bf16(before), preferred_element_type=jnp.float32)
    rank = jnp.sum(jnp.where(member, earlier, 0.0), axis=0, keepdims=True).astype(jnp.int32)
    hot = as_bf16(lax.broadcasted_iota(jnp.int32, (rows, rows), 0) == run * PIECE + rank)
    moved = lax.dot_general(
        jnp.broadcast_to(within, (8, rows)).astype(jnp.float32).astype(jnp.bfloat16),
        hot,
        (((1,), (1,)), ((), ())),
        preferred_element_type=jnp.float32,
    ).astype(jnp.bfloat16)
    copy.wait()
    x = x_ref[...].astype(jnp.float32)
    units = (x * lax.rsqrt(jnp.sum(x * x, axis=1, keepdims=True) + 1e-06)).astype(jnp.bfloat16)
    for index, block_ref in enumerate(block_refs):
        low = index * depth
        block_ref[0:depth, :] = jnp.dot(
            hot[low : low + depth], units, preferred_element_type=jnp.float32
        ).astype(jnp.bfloat16)
        block_ref[depth : depth + 8, :] = jnp.zeros((8, width), jnp.bfloat16)
        block_ref[depth : depth + 8, 0:depth] = moved[:, low : low + depth]


def home_kernel(sizes_ref, *rest):
    chain_len = lax.axis_size("chain")
    chunk_refs = rest[-1 - chain_len : -1]
    keys_ref = rest[-1]
    blocks = rest[: -1 - chain_len]
    count = len(blocks)
    width = keys_ref.shape[1]
    run_slots = count * PIECE
    depth = blocks[0].shape[0] - 8
    runs = depth // PIECE
    chunk = chunk_refs[0].shape[1]
    my_clus = lax.axis_index("clus")
    my_chain = lax.axis_index("chain")
    home = home_of(chain_len, my_clus)
    members = sizes_ref[my_clus]

    @pl.when(my_chain != home)
    def _():
        for ref in chunk_refs:
            ref[...] = jnp.zeros_like(ref)

    @pl.when(my_chain == home)
    def _():
        slots = jnp.concatenate([ref[depth : depth + 8, 0:depth][0:1] for ref in blocks], axis=0)
        lane = lax.broadcasted_iota(jnp.int32, (count, run_slots), 1)
        mine = lax.div(lane, PIECE) == lax.broadcasted_iota(jnp.int32, (count, run_slots), 0)
        from_lane = lax.broadcasted_iota(jnp.int32, (depth, run_slots), 0)
        to_lane = lax.rem(lax.broadcasted_iota(jnp.int32, (depth, run_slots), 1), PIECE)
        place = lax.broadcasted_iota(jnp.int32, (run_slots, run_slots), 0)
        key_at = lax.broadcasted_iota(jnp.int32, (run_slots, run_slots), 0)
        query_at = lax.broadcasted_iota(jnp.int32, (run_slots, run_slots), 1)
        results = []
        for run in range(runs):
            low = run * PIECE
            spread = jnp.dot(
                slots, as_bf16(from_lane == to_lane + low), preferred_element_type=jnp.float32
            )
            slot = jnp.sum(jnp.where(mine, spread, 0.0), axis=0, keepdims=True).astype(jnp.int32)
            rows = jnp.concatenate([ref[low : low + PIECE, :] for ref in blocks], axis=0)
            base = run * run_slots
            keys_ref[base : base + run_slots, :] = jnp.dot(
                as_bf16(place == slot), rows, preferred_element_type=jnp.float32
            ).astype(jnp.bfloat16)
            scores = lax.dot_general(
                keys_ref[0 : base + run_slots, :],
                keys_ref[base : base + run_slots, :],
                (((1,), (1,)), ((), ())),
                preferred_element_type=jnp.float32,
            )
            best = jnp.where(key_at < query_at, scores[base:], -2.0)
            best = jnp.max(best.reshape(run_slots // 8, 8, run_slots), axis=0)
            if run:
                best = jnp.maximum(best, jnp.max(scores[:base].reshape(base // 8, 8, run_slots), axis=0))
            best = jnp.maximum(jnp.max(best, axis=0, keepdims=True), -1.0)
            position = base + lax.broadcasted_iota(jnp.int32, (1, run_slots), 1)
            results.append(jnp.where(position < members, best, 0.0))
        whole = jnp.concatenate(results, axis=1)
        for step, ref in enumerate(chunk_refs):
            for place_of in range(chain_len):
                @pl.when(lax.rem(home + step, chain_len) == place_of)
                def _():
                    ref[...] = whole[:, place_of * chunk : (place_of + 1) * chunk]


def home_of(chain_len, clus):
    return chain_len // 2 - 1 + clus % 2


def local_home(embeddings, dest, sizes):
    chain_len, clus_len, rows, width = lengths(embeddings)
    shards = chain_len * clus_len
    run_slots = shards * PIECE
    depth = rows // clus_len
    block = jax.ShapeDtypeStruct((depth + 8, width), jnp.bfloat16)
    blocks = pl.pallas_call(
        functools.partial(send_kernel, run_slots, depth // PIECE),
        out_shape=(block,) * clus_len,
        in_specs=[VMEM, HBM],
        out_specs=(VMEM,) * clus_len,
        scratch_shapes=[pltpu.VMEM((rows, width), jnp.bfloat16), pltpu.SemaphoreType.DMA],
        compiler_params=pltpu.CompilerParams(vmem_limit_bytes=32 * 2**20),
        name="send_blocks",
    )(dest.reshape(1, rows), embeddings)

    def at(chain, clus):
        return chain * clus_len + clus

    def to_home(block, step, flip):
        pairs = []
        for k in range(clus_len):
            home = home_of(chain_len, k)
            source = home + step if k % 2 else home - step
            pairs.append((at(source % chain_len, k ^ flip), at(home, k)))
        return lax.ppermute(block, ("chain", "clus"), pairs)

    def across(block, flip):
        pairs = [(at(z, k), at(z, k ^ flip)) for z in range(chain_len) for k in range(clus_len)]
        return lax.ppermute(block, ("chain", "clus"), pairs)

    crossed = [across(blocks[flip], flip) for flip in range(2, clus_len)]
    keys = [blocks[0]]
    for step in range(1, chain_len):
        keys.append(to_home(blocks[0], step, 0))
        keys.append(to_home(blocks[1], step, 1))
    keys.append(across(blocks[1], 1))
    for came in crossed:
        keys.append(came)
        for step in range(1, chain_len):
            keys.append(to_home(came, step, 0))

    chunk = rows
    chunks = pl.pallas_call(
        home_kernel,
        out_shape=(jax.ShapeDtypeStruct((1, chunk), jnp.float32),) * chain_len,
        in_specs=[SMEM] + [VMEM] * len(keys),
        out_specs=(VMEM,) * chain_len,
        scratch_shapes=[pltpu.VMEM((chain_len * chunk, width), jnp.bfloat16)],
        compiler_params=pltpu.CompilerParams(vmem_limit_bytes=40 * 2**20),
        name="best_at_home",
    )(sizes, *keys)
    found = chunks[0]
    for step in range(1, chain_len):
        pairs = []
        for k in range(clus_len):
            home = home_of(chain_len, k)
            pairs.append((at(home, k), at((home + step) % chain_len, k)))
        found = found + lax.ppermute(chunks[step], ("chain", "clus"), pairs)
    return found


def solution(mesh):
    return jax.shard_map(
        local_home if mesh.shape["chain"] == mesh.shape["clus"] == 4 else local_plane,
        mesh=mesh,
        in_specs=(
            P(("groups", "chain", "clus"), None),
            P(("groups", "chain", "clus")),
            P("groups"),
        ),
        out_specs=P(("groups", "clus"), "chain"),
        check_vma=False,
    )
```

```python
import functools

import jax
import jax.numpy as jnp
from jax import lax
from jax.experimental import pallas as pl
from jax.experimental.pallas import tpu as pltpu
from jax.sharding import PartitionSpec as P

PIECE = 16
VMEM = pl.BlockSpec(memory_space=pltpu.VMEM)
SMEM = pl.BlockSpec(memory_space=pltpu.SMEM)
HBM = pl.BlockSpec(memory_space=pltpu.HBM)


def as_bf16(mask):
    return mask.astype(jnp.float32).astype(jnp.bfloat16)


def sort_kernel(run_slots, dest_ref, rows_ref, units_ref, slots_ref):
    rows = rows_ref.shape[0]
    runs = rows // PIECE
    dest = dest_ref[...]
    run = dest // run_slots
    within = dest % run_slots
    member = lax.broadcasted_iota(jnp.int32, (runs, rows), 0) == run
    before = lax.broadcasted_iota(jnp.int32, (rows, rows), 0) < lax.broadcasted_iota(
        jnp.int32, (rows, rows), 1
    )
    earlier = jnp.dot(
        member.astype(jnp.float32).astype(jnp.bfloat16),
        before.astype(jnp.float32).astype(jnp.bfloat16),
        preferred_element_type=jnp.float32,
    )
    rank = jnp.sum(jnp.where(member, earlier, 0.0), axis=0, keepdims=True).astype(jnp.int32)
    placed = run * PIECE + rank
    hot = (lax.broadcasted_iota(jnp.int32, (rows, rows), 0) == placed).astype(jnp.float32)
    hot = hot.astype(jnp.bfloat16)
    x = rows_ref[...].astype(jnp.float32)
    units = (x * lax.rsqrt(jnp.sum(x * x, axis=1, keepdims=True) + 1e-06)).astype(jnp.bfloat16)
    units_ref[...] = jnp.dot(hot, units, preferred_element_type=jnp.float32).astype(jnp.bfloat16)
    halves = jnp.concatenate(
        [jnp.broadcast_to(within // 256, (8, rows)), jnp.broadcast_to(within % 256, (8, rows))], axis=0
    )
    moved = lax.dot_general(
        halves.astype(jnp.float32).astype(jnp.bfloat16),
        hot,
        (((1,), (1,)), ((), ())),
        preferred_element_type=jnp.float32,
    )
    slots_ref[...] = (moved[0:1, :] * 256.0 + moved[8:9, :]).astype(jnp.int32)


def best_kernel(info_ref, slots_ref, keys_ref, out_ref, query_ref):
    shards, depth, width = keys_ref.shape
    queries = out_ref.shape[1]
    run_slots = shards * PIECE
    unit = min(run_slots, queries)
    first = info_ref[0]
    members = info_ref[1]
    first_run = first // run_slots

    def run_rows(run):
        start = pl.multiple_of(run * PIECE, PIECE)
        return keys_ref[:, pl.ds(start, PIECE), :].reshape(run_slots, width)

    def run_positions(run):
        start = pl.multiple_of(run * PIECE, PIECE)
        tile = slots_ref[pl.ds(start, PIECE), :]
        wide = jnp.broadcast_to(tile[None], (shards, PIECE, shards)).reshape(run_slots, shards)
        lane = lax.broadcasted_iota(jnp.int32, (run_slots, shards), 1)
        row = lax.broadcasted_iota(jnp.int32, (run_slots, shards), 0)
        picked = jnp.sum(jnp.where(lane == row // PIECE, wide, 0), axis=1, keepdims=True)
        return picked + run * run_slots

    for index in range(queries // unit):
        run = first_run + index
        lanes = lax.broadcasted_iota(jnp.int32, (run_slots, unit), 1) + (first + index * unit)
        hot = (run_positions(run) == lanes).astype(jnp.float32).astype(jnp.bfloat16)
        query_ref[:, index * unit : (index + 1) * unit] = lax.dot_general(
            run_rows(run), hot, (((0,), (0,)), ((), ())), preferred_element_type=jnp.float32
        ).astype(jnp.bfloat16)

    def fold(scores):
        return jnp.max(scores.reshape(run_slots // 8, 8, queries), axis=0)

    def step(run, running):
        scores = jnp.dot(run_rows(run), query_ref[...], preferred_element_type=jnp.float32)
        return jnp.maximum(running, fold(scores))

    running = lax.fori_loop(0, first_run, step, jnp.full((8, queries), -1.0, jnp.float32))
    position = first + lax.broadcasted_iota(jnp.int32, (1, queries), 1)
    for index in range(queries // unit):
        run = first_run + index
        scores = jnp.dot(run_rows(run), query_ref[...], preferred_element_type=jnp.float32)
        masked = jnp.where(run_positions(run) < position, scores, -2.0)
        running = jnp.maximum(running, fold(masked))
    found = jnp.max(running, axis=0, keepdims=True)
    out_ref[...] = jnp.where(position < members, found, 0.0)


def local_plane(embeddings, dest, sizes):
    chain_len = lax.axis_size("chain")
    clus_len = lax.axis_size("clus")
    shards = chain_len * clus_len
    rows, width = embeddings.shape
    clusters = sizes.shape[0]
    parts = chain_len // clusters
    run_slots = shards * PIECE
    depth = rows // chain_len
    my_chain = lax.axis_index("chain")
    my_clus = lax.axis_index("clus")
    cluster = my_chain // parts
    part = my_chain % parts

    units, slots = pl.pallas_call(
        functools.partial(sort_kernel, run_slots),
        out_shape=(
            jax.ShapeDtypeStruct((rows, width), jnp.bfloat16),
            jax.ShapeDtypeStruct((1, rows), jnp.int32),
        ),
        in_specs=[VMEM, VMEM],
        out_specs=(VMEM, VMEM),
        compiler_params=pltpu.CompilerParams(vmem_limit_bytes=32 * 2**20),
        name="sort_units",
    )(dest.reshape(1, rows), embeddings)

    slots = lax.all_gather(slots, ("chain", "clus"), axis=0, tiled=True)
    slots = slots.reshape(chain_len, clus_len, clusters, -1, PIECE)
    slots = lax.dynamic_index_in_dim(slots, cluster, 2, keepdims=False)
    slots = slots.transpose(2, 3, 1, 0).reshape(-1, shards)

    got = lax.all_to_all(units, "chain", split_axis=0, concat_axis=0, tiled=True)
    keys = lax.all_gather(got, "clus", axis=0, tiled=True).reshape(shards, depth, width)
    if parts > 1:
        pieces = []
        for wanted in range(parts):
            block = keys
            for other in range(parts):
                if other != wanted:
                    pairs = [(c * parts + wanted, c * parts + other) for c in range(clusters)]
                    came = lax.ppermute(keys, "chain", pairs)
                    block = jnp.where(part == other, came, block)
            pieces.append(block)
        keys = jnp.concatenate(pieces, axis=1)

    first = (part * clus_len + my_clus) * rows
    ids = jnp.arange(clusters, dtype=jnp.int32)
    members = jnp.sum(jnp.where(ids == cluster, sizes, 0))
    info = jnp.stack([first, members]).astype(jnp.int32)
    found = pl.pallas_call(
        best_kernel,
        out_shape=jax.ShapeDtypeStruct((1, rows), jnp.float32),
        in_specs=[SMEM, VMEM, VMEM],
        out_specs=VMEM,
        scratch_shapes=[pltpu.VMEM((width, rows), jnp.bfloat16)],
        compiler_params=pltpu.CompilerParams(vmem_limit_bytes=48 * 2**20),
        name="best_of_earlier",
    )(info, slots, keys)

    pairs = []
    for z in range(chain_len):
        for k in range(clus_len):
            pairs.append((z * clus_len + k, ((z % parts) * clus_len + k) * clus_len + z // parts))
    return lax.ppermute(found, ("chain", "clus"), pairs)


def send_kernel(run_slots, cluster_runs, dest_hbm, rows_hbm, *rest):
    block_refs, (dest_ref, rows_ref, sems) = rest[:-3], rest[-3:]
    dest_copy = pltpu.make_async_copy(dest_hbm, dest_ref, sems.at[0])
    rows_copy = pltpu.make_async_copy(rows_hbm, rows_ref, sems.at[1])
    dest_copy.start()
    rows_copy.start()
    rows, width = rows_ref.shape
    runs = rows // PIECE
    depth = rows // len(block_refs)
    upper = lax.axis_index("chain") >= lax.axis_size("chain") // 2
    code = lax.axis_index("clus") // 2 * 2 + upper.astype(jnp.int32)
    before = lax.broadcasted_iota(jnp.int32, (rows, rows), 0) < lax.broadcasted_iota(
        jnp.int32, (rows, rows), 1
    )
    dest_copy.wait()
    dest = dest_ref[...]
    run = lax.div(dest, run_slots)
    within = lax.rem(dest, run_slots)
    run = (lax.div(run, cluster_runs) ^ code) * cluster_runs + lax.rem(run, cluster_runs)
    member = lax.broadcasted_iota(jnp.int32, (runs, rows), 0) == run
    earlier = jnp.dot(as_bf16(member), as_bf16(before), preferred_element_type=jnp.float32)
    rank = jnp.sum(jnp.where(member, earlier, 0.0), axis=0, keepdims=True).astype(jnp.int32)
    hot = as_bf16(lax.broadcasted_iota(jnp.int32, (rows, rows), 0) == run * PIECE + rank)
    moved = lax.dot_general(
        jnp.broadcast_to(within, (8, rows)).astype(jnp.float32).astype(jnp.bfloat16),
        hot,
        (((1,), (1,)), ((), ())),
        preferred_element_type=jnp.float32,
    ).astype(jnp.bfloat16)
    rows_copy.wait()
    x = rows_ref[...].astype(jnp.float32)
    units = (x * lax.rsqrt(jnp.sum(x * x, axis=1, keepdims=True) + 1e-06)).astype(jnp.bfloat16)
    for index, block_ref in enumerate(block_refs):
        low = index * depth
        block_ref[0:depth, :] = jnp.dot(
            hot[low : low + depth], units, preferred_element_type=jnp.float32
        ).astype(jnp.bfloat16)
        block_ref[depth : depth + 8, :] = jnp.zeros((8, width), jnp.bfloat16)
        block_ref[depth : depth + 8, 0:depth] = moved[:, low : low + depth]


def home_kernel(height, sizes_ref, *rest):
    refs, (first_ref, second_ref, keys_ref) = rest[:-3], rest[-3:]
    blocks = []
    for ref in refs:
        blocks += [(ref, low) for low in range(0, ref.shape[0], height)]
    count = len(blocks)
    run_slots = count * PIECE
    depth = height - 8
    runs = depth // PIECE
    chunk = first_ref.shape[1]
    chunk_runs = chunk // run_slots
    clus = lax.axis_index("clus")
    chain = lax.axis_index("chain")
    half = lax.axis_size("chain") // 2
    is_home = jnp.logical_or(chain == half - 1, chain == half)
    members = sizes_ref[clus // 2 * 2 + (chain >= half).astype(jnp.int32)]

    @pl.when(jnp.logical_not(is_home))
    def _():
        first_ref[...] = jnp.zeros_like(first_ref)
        second_ref[...] = jnp.zeros_like(second_ref)

    @pl.when(is_home)
    def _():
        for index, (ref, low) in enumerate(blocks):
            for run in range(runs):
                at = run * run_slots + index * PIECE
                keys_ref[at : at + PIECE, :] = ref[low + run * PIECE : low + (run + 1) * PIECE, :]

    def answer(wanted, out_ref):
        slots = jnp.concatenate(
            [ref[low + depth : low + depth + 8, 0:depth][0:1] for ref, low in blocks], axis=0
        )
        block_of = lax.broadcasted_iota(jnp.int32, (run_slots, count), 0) // PIECE
        mine = block_of == lax.broadcasted_iota(jnp.int32, (run_slots, count), 1)
        in_block = lax.broadcasted_iota(jnp.int32, (run_slots, depth), 0) % PIECE
        lane = lax.broadcasted_iota(jnp.int32, (run_slots, depth), 1)
        query_at = lax.broadcasted_iota(jnp.int32, (run_slots, run_slots), 1)
        for index in range(chunk_runs):
            run = wanted * chunk_runs + index
            base = run * run_slots
            spread = lax.dot_general(
                as_bf16(lane == in_block + run * PIECE),
                slots,
                (((1,), (1,)), ((), ())),
                preferred_element_type=jnp.float32,
            )
            slot = jnp.sum(jnp.where(mine, spread, 0.0), axis=1, keepdims=True).astype(jnp.int32)
            queries = lax.dot_general(
                keys_ref[base : base + run_slots, :],
                as_bf16(slot == query_at),
                (((0,), (0,)), ((), ())),
                preferred_element_type=jnp.float32,
            ).astype(jnp.bfloat16)
            scores = jnp.dot(
                keys_ref[0 : base + run_slots, :], queries, preferred_element_type=jnp.float32
            )
            best = jnp.where(slot < query_at, scores[base:], -2.0)
            best = jnp.max(best.reshape(run_slots // 8, 8, run_slots), axis=0)
            if run:
                best = jnp.maximum(best, jnp.max(scores[:base].reshape(base // 8, 8, run_slots), axis=0))
            best = jnp.maximum(jnp.max(best, axis=0, keepdims=True), -1.0)
            position = base + lax.broadcasted_iota(jnp.int32, (1, run_slots), 1)
            out_ref[:, index * run_slots : (index + 1) * run_slots] = jnp.where(
                position < members, best, 0.0
            )

    for core in range(2):
        @pl.when(jnp.logical_and(is_home, clus % 2 == core))
        def _():
            answer(core, first_ref)
            answer(2 * half - 1 - core, second_ref)


def local_home(embeddings, dest, sizes):
    chain_len = lax.axis_size("chain")
    clus_len = lax.axis_size("clus")
    rows, width = embeddings.shape
    run_slots = chain_len * clus_len * PIECE
    depth = rows // clus_len
    height = depth + 8
    block = jax.ShapeDtypeStruct((height, width), jnp.bfloat16)
    blocks = pl.pallas_call(
        functools.partial(send_kernel, run_slots, depth // PIECE),
        out_shape=(block,) * clus_len,
        in_specs=[HBM, HBM],
        out_specs=(VMEM,) * clus_len,
        scratch_shapes=[
            pltpu.VMEM((1, rows), jnp.int32),
            pltpu.VMEM((rows, width), jnp.bfloat16),
            pltpu.SemaphoreType.DMA((2,)),
        ],
        compiler_params=pltpu.CompilerParams(vmem_limit_bytes=58 * 2**20),
        name="send_blocks",
    )(dest.reshape(1, rows), embeddings)

    def permute(value, moves):
        pairs = [(a * clus_len + b, c * clus_len + d) for a, b, c, d in moves]
        return lax.ppermute(value, ("chain", "clus"), pairs)

    def to_home(value, moves, flip):
        return permute(value, [(a, k, b, k ^ flip) for a, b in moves for k in range(clus_len)])

    low, high, top = chain_len // 2 - 1, chain_len // 2, chain_len - 1
    near = [(0, low), (top, high)]
    far = [(0, high), (top, low)]
    middle = [(low, high), (high, low)]
    stay = [(low, low), (high, high)]

    def swap(values):
        value = jnp.concatenate(values, axis=0)
        return permute(value, [(z, k, z, k ^ 1) for z in (low, high) for k in range(clus_len)])

    far_across = to_home(blocks[3], far, 2)
    far_along = to_home(blocks[1], far, 0)
    stay_across = to_home(blocks[2], stay, 2)
    near_across = to_home(blocks[2], near, 2)
    middle_across = to_home(blocks[3], middle, 2)
    near_along = to_home(blocks[0], near, 0)
    middle_along = to_home(blocks[1], middle, 0)
    batches = [
        [blocks[0], stay_across, far_across],
        [far_along, near_across, middle_across],
        [near_along, middle_along],
    ]
    keys = []
    for batch in batches:
        keys.append(swap(batch))
        keys += batch

    answers = pl.pallas_call(
        functools.partial(home_kernel, height),
        out_shape=(jax.ShapeDtypeStruct((1, rows), jnp.float32),) * 2,
        in_specs=[SMEM] + [VMEM] * len(keys),
        out_specs=(VMEM, VMEM),
        scratch_shapes=[pltpu.VMEM((chain_len * rows, width), jnp.bfloat16)],
        compiler_params=pltpu.CompilerParams(vmem_limit_bytes=40 * 2**20),
        name="best_at_home",
    )(sizes, *keys)
    moves = [[], []]
    for k in range(clus_len):
        for core in range(2):
            source = (low + k % 2, k // 2 * 2 + core)
            moves[0].append(source + (core, k))
            moves[1].append(source + (top - core, k))
    return permute(answers[0], moves[0]) + permute(answers[1], moves[1])


def solution(mesh):
    return jax.shard_map(
        local_home if mesh.shape["chain"] == mesh.shape["clus"] == 4 else local_plane,
        mesh=mesh,
        in_specs=(
            P(("groups", "chain", "clus"), None),
            P(("groups", "chain", "clus")),
            P("groups"),
        ),
        out_specs=P(("groups", "clus"), "chain"),
        check_vma=False,
    )
```

```python
import functools

import jax
import jax.numpy as jnp
from jax import lax
from jax.experimental import pallas as pl
from jax.experimental.pallas import tpu as pltpu
from jax.sharding import PartitionSpec as P

TILE = 8
PIECE = 16
VMEM = pl.BlockSpec(memory_space=pltpu.VMEM)
SMEM = pl.BlockSpec(memory_space=pltpu.SMEM)
HBM = pl.BlockSpec(memory_space=pltpu.HBM)


def as_bf16(mask):
    return mask.astype(jnp.float32).astype(jnp.bfloat16)


def sort_kernel(run_slots, dest_ref, rows_ref, units_ref, slots_ref):
    rows = rows_ref.shape[0]
    runs = rows // PIECE
    dest = dest_ref[...]
    run = dest // run_slots
    within = dest % run_slots
    member = lax.broadcasted_iota(jnp.int32, (runs, rows), 0) == run
    before = lax.broadcasted_iota(jnp.int32, (rows, rows), 0) < lax.broadcasted_iota(
        jnp.int32, (rows, rows), 1
    )
    earlier = jnp.dot(
        member.astype(jnp.float32).astype(jnp.bfloat16),
        before.astype(jnp.float32).astype(jnp.bfloat16),
        preferred_element_type=jnp.float32,
    )
    rank = jnp.sum(jnp.where(member, earlier, 0.0), axis=0, keepdims=True).astype(jnp.int32)
    placed = run * PIECE + rank
    hot = (lax.broadcasted_iota(jnp.int32, (rows, rows), 0) == placed).astype(jnp.float32)
    hot = hot.astype(jnp.bfloat16)
    x = rows_ref[...].astype(jnp.float32)
    units = (x * lax.rsqrt(jnp.sum(x * x, axis=1, keepdims=True) + 1e-06)).astype(jnp.bfloat16)
    units_ref[...] = jnp.dot(hot, units, preferred_element_type=jnp.float32).astype(jnp.bfloat16)
    halves = jnp.concatenate(
        [jnp.broadcast_to(within // 256, (8, rows)), jnp.broadcast_to(within % 256, (8, rows))], axis=0
    )
    moved = lax.dot_general(
        halves.astype(jnp.float32).astype(jnp.bfloat16),
        hot,
        (((1,), (1,)), ((), ())),
        preferred_element_type=jnp.float32,
    )
    slots_ref[...] = (moved[0:1, :] * 256.0 + moved[8:9, :]).astype(jnp.int32)


def best_kernel(info_ref, slots_ref, keys_ref, out_ref, query_ref):
    shards, depth, width = keys_ref.shape
    queries = out_ref.shape[1]
    run_slots = shards * PIECE
    unit = min(run_slots, queries)
    first = info_ref[0]
    members = info_ref[1]
    first_run = first // run_slots

    def run_rows(run):
        start = pl.multiple_of(run * PIECE, PIECE)
        return keys_ref[:, pl.ds(start, PIECE), :].reshape(run_slots, width)

    def run_positions(run):
        start = pl.multiple_of(run * PIECE, PIECE)
        tile = slots_ref[pl.ds(start, PIECE), :]
        wide = jnp.broadcast_to(tile[None], (shards, PIECE, shards)).reshape(run_slots, shards)
        lane = lax.broadcasted_iota(jnp.int32, (run_slots, shards), 1)
        row = lax.broadcasted_iota(jnp.int32, (run_slots, shards), 0)
        picked = jnp.sum(jnp.where(lane == row // PIECE, wide, 0), axis=1, keepdims=True)
        return picked + run * run_slots

    for index in range(queries // unit):
        run = first_run + index
        lanes = lax.broadcasted_iota(jnp.int32, (run_slots, unit), 1) + (first + index * unit)
        hot = (run_positions(run) == lanes).astype(jnp.float32).astype(jnp.bfloat16)
        query_ref[:, index * unit : (index + 1) * unit] = lax.dot_general(
            run_rows(run), hot, (((0,), (0,)), ((), ())), preferred_element_type=jnp.float32
        ).astype(jnp.bfloat16)

    def fold(scores):
        return jnp.max(scores.reshape(run_slots // 8, 8, queries), axis=0)

    def step(run, running):
        scores = jnp.dot(run_rows(run), query_ref[...], preferred_element_type=jnp.float32)
        return jnp.maximum(running, fold(scores))

    running = lax.fori_loop(0, first_run, step, jnp.full((8, queries), -1.0, jnp.float32))
    position = first + lax.broadcasted_iota(jnp.int32, (1, queries), 1)
    for index in range(queries // unit):
        run = first_run + index
        scores = jnp.dot(run_rows(run), query_ref[...], preferred_element_type=jnp.float32)
        masked = jnp.where(run_positions(run) < position, scores, -2.0)
        running = jnp.maximum(running, fold(masked))
    found = jnp.max(running, axis=0, keepdims=True)
    out_ref[...] = jnp.where(position < members, found, 0.0)


def local_plane(embeddings, dest, sizes):
    chain_len = lax.axis_size("chain")
    clus_len = lax.axis_size("clus")
    shards = chain_len * clus_len
    rows, width = embeddings.shape
    clusters = sizes.shape[0]
    parts = chain_len // clusters
    run_slots = shards * PIECE
    depth = rows // chain_len
    my_chain = lax.axis_index("chain")
    my_clus = lax.axis_index("clus")
    cluster = my_chain // parts
    part = my_chain % parts

    units, slots = pl.pallas_call(
        functools.partial(sort_kernel, run_slots),
        out_shape=(
            jax.ShapeDtypeStruct((rows, width), jnp.bfloat16),
            jax.ShapeDtypeStruct((1, rows), jnp.int32),
        ),
        in_specs=[VMEM, VMEM],
        out_specs=(VMEM, VMEM),
        compiler_params=pltpu.CompilerParams(vmem_limit_bytes=32 * 2**20),
        name="sort_units",
    )(dest.reshape(1, rows), embeddings)

    slots = lax.all_gather(slots, ("chain", "clus"), axis=0, tiled=True)
    slots = slots.reshape(chain_len, clus_len, clusters, -1, PIECE)
    slots = lax.dynamic_index_in_dim(slots, cluster, 2, keepdims=False)
    slots = slots.transpose(2, 3, 1, 0).reshape(-1, shards)

    got = lax.all_to_all(units, "chain", split_axis=0, concat_axis=0, tiled=True)
    keys = lax.all_gather(got, "clus", axis=0, tiled=True).reshape(shards, depth, width)
    if parts > 1:
        pieces = []
        for wanted in range(parts):
            block = keys
            for other in range(parts):
                if other != wanted:
                    pairs = [(c * parts + wanted, c * parts + other) for c in range(clusters)]
                    came = lax.ppermute(keys, "chain", pairs)
                    block = jnp.where(part == other, came, block)
            pieces.append(block)
        keys = jnp.concatenate(pieces, axis=1)

    first = (part * clus_len + my_clus) * rows
    ids = jnp.arange(clusters, dtype=jnp.int32)
    members = jnp.sum(jnp.where(ids == cluster, sizes, 0))
    info = jnp.stack([first, members]).astype(jnp.int32)
    found = pl.pallas_call(
        best_kernel,
        out_shape=jax.ShapeDtypeStruct((1, rows), jnp.float32),
        in_specs=[SMEM, VMEM, VMEM],
        out_specs=VMEM,
        scratch_shapes=[pltpu.VMEM((width, rows), jnp.bfloat16)],
        compiler_params=pltpu.CompilerParams(vmem_limit_bytes=48 * 2**20),
        name="best_of_earlier",
    )(info, slots, keys)

    pairs = []
    for z in range(chain_len):
        for k in range(clus_len):
            pairs.append((z * clus_len + k, ((z % parts) * clus_len + k) * clus_len + z // parts))
    return lax.ppermute(found, ("chain", "clus"), pairs)


def send_kernel(run_slots, cluster_runs, dest_hbm, rows_hbm, kept_ref, given_ref, *scratch):
    dest_ref, rows_ref, sems = scratch
    dest_copy = pltpu.make_async_copy(dest_hbm, dest_ref, sems.at[0])
    rows_copy = pltpu.make_async_copy(rows_hbm, rows_ref, sems.at[1])
    dest_copy.start()
    rows_copy.start()
    rows, width = rows_ref.shape
    runs = rows // PIECE
    half = rows // 2
    depth = half // 2
    clus = lax.axis_index("clus")
    core = clus % 2
    upper = lax.axis_index("chain") >= lax.axis_size("chain") // 2
    code = (clus // 2 ^ core) * 2 + upper.astype(jnp.int32)
    before = lax.broadcasted_iota(jnp.int32, (rows, rows), 0) < lax.broadcasted_iota(
        jnp.int32, (rows, rows), 1
    )
    dest_copy.wait()
    dest = dest_ref[...]
    run = lax.div(dest, run_slots)
    within = lax.rem(dest, run_slots)
    run = (lax.div(run, cluster_runs) ^ code) * cluster_runs + lax.rem(run, cluster_runs)
    member = lax.broadcasted_iota(jnp.int32, (runs, rows), 0) == run
    earlier = jnp.dot(as_bf16(member), as_bf16(before), preferred_element_type=jnp.float32)
    rank = jnp.sum(jnp.where(member, earlier, 0.0), axis=0, keepdims=True).astype(jnp.int32)
    hot = as_bf16(lax.broadcasted_iota(jnp.int32, (rows, rows), 0) == run * PIECE + rank)
    moved = lax.dot_general(
        jnp.broadcast_to(within, (TILE, rows)).astype(jnp.float32).astype(jnp.bfloat16),
        hot,
        (((1,), (1,)), ((), ())),
        preferred_element_type=jnp.float32,
    )
    rows_copy.wait()
    x = rows_ref[...].astype(jnp.float32)
    units = (x * lax.rsqrt(jnp.sum(x * x, axis=1, keepdims=True) + 1e-06)).astype(jnp.bfloat16)
    for index, ref in enumerate((kept_ref, given_ref)):
        low = index * half
        ref[0:half, :] = jnp.dot(
            hot[low : low + half], units, preferred_element_type=jnp.float32
        ).astype(jnp.bfloat16)
        line = lax.broadcasted_iota(jnp.int32, (TILE, half), 0) == index
        ref[half : half + TILE, :] = jnp.zeros((TILE, width), jnp.bfloat16)
        ref[half : half + TILE, 0:half] = jnp.where(line, moved[:, low : low + half], 0.0).astype(
            jnp.bfloat16
        )


def merge_kernel(kept_ref, came_ref, near_ref, far_ref):
    half = kept_ref.shape[0] - TILE
    depth = half // 2
    slots = kept_ref[half : half + TILE, 0:half].astype(jnp.float32)
    slots = (slots + came_ref[half : half + TILE, 0:half].astype(jnp.float32)).astype(jnp.bfloat16)
    for index, ref in enumerate((near_ref, far_ref)):
        low = index * depth
        ref[0:depth, :] = kept_ref[low : low + depth, :]
        ref[depth:half, :] = came_ref[low : low + depth, :]
        ref[half : half + TILE, :] = jnp.zeros((TILE, ref.shape[1]), jnp.bfloat16)
        ref[half : half + TILE, 0:depth] = slots[:, low : low + depth]


def home_kernel(height, sizes_ref, *rest):
    refs, (first_ref, second_ref, keys_ref) = rest[:-3], rest[-3:]
    blocks = []
    depth = (height - TILE) // 2
    for ref in refs:
        for low in range(0, ref.shape[0], height):
            blocks += [(ref, low, low + 2 * depth, 0), (ref, low + depth, low + 2 * depth, 1)]
    count = len(blocks)
    run_slots = count * PIECE
    runs = depth // PIECE
    chunk = first_ref.shape[1]
    chunk_runs = chunk // run_slots
    clus = lax.axis_index("clus")
    chain = lax.axis_index("chain")
    half = lax.axis_size("chain") // 2
    is_home = jnp.logical_or(chain == half - 1, chain == half)
    members = sizes_ref[clus // 2 * 2 + (chain >= half).astype(jnp.int32)]

    @pl.when(jnp.logical_not(is_home))
    def _():
        first_ref[...] = jnp.zeros_like(first_ref)
        second_ref[...] = jnp.zeros_like(second_ref)

    @pl.when(is_home)
    def _():
        for index, (ref, low, _, _) in enumerate(blocks):
            for run in range(runs):
                at = run * run_slots + index * PIECE
                keys_ref[at : at + PIECE, :] = ref[low + run * PIECE : low + (run + 1) * PIECE, :]

    def answer(wanted, out_ref):
        slots = jnp.concatenate(
            [ref[at : at + TILE, 0:depth][line : line + 1] for ref, _, at, line in blocks], axis=0
        )
        block_of = lax.broadcasted_iota(jnp.int32, (run_slots, count), 0) // PIECE
        mine = block_of == lax.broadcasted_iota(jnp.int32, (run_slots, count), 1)
        in_block = lax.broadcasted_iota(jnp.int32, (run_slots, depth), 0) % PIECE
        lane = lax.broadcasted_iota(jnp.int32, (run_slots, depth), 1)
        query_at = lax.broadcasted_iota(jnp.int32, (run_slots, run_slots), 1)
        for index in range(chunk_runs):
            run = wanted * chunk_runs + index
            base = run * run_slots
            spread = lax.dot_general(
                as_bf16(lane == in_block + run * PIECE),
                slots,
                (((1,), (1,)), ((), ())),
                preferred_element_type=jnp.float32,
            )
            slot = jnp.sum(jnp.where(mine, spread, 0.0), axis=1, keepdims=True).astype(jnp.int32)
            queries = lax.dot_general(
                keys_ref[base : base + run_slots, :],
                as_bf16(slot == query_at),
                (((0,), (0,)), ((), ())),
                preferred_element_type=jnp.float32,
            ).astype(jnp.bfloat16)
            scores = jnp.dot(
                keys_ref[0 : base + run_slots, :], queries, preferred_element_type=jnp.float32
            )
            best = jnp.where(slot < query_at, scores[base:], -2.0)
            best = jnp.max(best.reshape(run_slots // 8, 8, run_slots), axis=0)
            if run:
                best = jnp.maximum(best, jnp.max(scores[:base].reshape(base // 8, 8, run_slots), axis=0))
            best = jnp.maximum(jnp.max(best, axis=0, keepdims=True), -1.0)
            position = base + lax.broadcasted_iota(jnp.int32, (1, run_slots), 1)
            out_ref[:, index * run_slots : (index + 1) * run_slots] = jnp.where(
                position < members, best, 0.0
            )

    for core in range(2):
        @pl.when(jnp.logical_and(is_home, clus % 2 == core))
        def _():
            answer(core, first_ref)
            answer(2 * half - 1 - core, second_ref)


def local_home(embeddings, dest, sizes):
    chain_len = lax.axis_size("chain")
    clus_len = lax.axis_size("clus")
    rows, width = embeddings.shape
    run_slots = chain_len * clus_len * PIECE
    height = rows // 2 + TILE
    block = jax.ShapeDtypeStruct((height, width), jnp.bfloat16)
    kept, given = pl.pallas_call(
        functools.partial(send_kernel, run_slots, rows // clus_len // PIECE),
        out_shape=(block, block),
        in_specs=[HBM, HBM],
        out_specs=(VMEM, VMEM),
        scratch_shapes=[
            pltpu.VMEM((1, rows), jnp.int32),
            pltpu.VMEM((rows, width), jnp.bfloat16),
            pltpu.SemaphoreType.DMA((2,)),
        ],
        compiler_params=pltpu.CompilerParams(vmem_limit_bytes=62_400_000),
        name="send_blocks",
    )(dest.reshape(1, rows), embeddings)

    def permute(value, moves):
        pairs = [(a * clus_len + b, c * clus_len + d) for a, b, c, d in moves]
        return lax.ppermute(value, ("chain", "clus"), pairs)

    def to_home(value, moves):
        columns = range(clus_len)
        return permute(value, [(a, k, b, k ^ (2 * (k % 2))) for a, b in moves for k in columns])

    low, high, top = chain_len // 2 - 1, chain_len // 2, chain_len - 1

    def swap(values, planes):
        value = jnp.concatenate(values, axis=0) if len(values) > 1 else values[0]
        return permute(value, [(z, k, z, k ^ 1) for z in planes for k in range(clus_len)])

    near, far = pl.pallas_call(
        merge_kernel,
        out_shape=(block, block),
        in_specs=[VMEM, VMEM],
        out_specs=(VMEM, VMEM),
        compiler_params=pltpu.CompilerParams(vmem_limit_bytes=16 * 2**20),
        name="merge_blocks",
    )(kept, swap([given], range(chain_len)))

    from_far = to_home(far, [(0, high), (top, low)])
    from_middle = to_home(far, [(low, high), (high, low)])
    from_near = to_home(near, [(0, low), (top, high)])
    from_plane = to_home(near, [(low, low), (high, high)])
    keys = []
    for batch in ([from_plane, from_far], [from_near], [from_middle]):
        keys += batch + [swap(batch, (low, high))]

    answers = pl.pallas_call(
        functools.partial(home_kernel, height),
        out_shape=(jax.ShapeDtypeStruct((1, rows), jnp.float32),) * 2,
        in_specs=[SMEM] + [VMEM] * len(keys),
        out_specs=(VMEM, VMEM),
        scratch_shapes=[pltpu.VMEM((chain_len * rows, width), jnp.bfloat16)],
        compiler_params=pltpu.CompilerParams(vmem_limit_bytes=40 * 2**20),
        name="best_at_home",
    )(sizes, *keys)
    moves = [[], []]
    for k in range(clus_len):
        for core in range(2):
            source = (low + k % 2, k // 2 * 2 + core)
            moves[0].append(source + (core, k))
            moves[1].append(source + (top - core, k))
    return permute(answers[0], moves[0]) + permute(answers[1], moves[1])


def solution(mesh):
    return jax.shard_map(
        local_home if mesh.shape["chain"] == mesh.shape["clus"] == 4 else local_plane,
        mesh=mesh,
        in_specs=(
            P(("groups", "chain", "clus"), None),
            P(("groups", "chain", "clus")),
            P("groups"),
        ),
        out_specs=P(("groups", "clus"), "chain"),
        check_vma=False,
    )
```

```python
import functools

import jax
import jax.numpy as jnp
from jax import lax
from jax.experimental import pallas as pl
from jax.experimental.pallas import tpu as pltpu
from jax.sharding import PartitionSpec as P

TILE = 8
LANES = 128
PIECE = 16
VMEM = pl.BlockSpec(memory_space=pltpu.VMEM)
SMEM = pl.BlockSpec(memory_space=pltpu.SMEM)
HBM = pl.BlockSpec(memory_space=pltpu.HBM)


def as_bf16(mask):
    return mask.astype(jnp.float32).astype(jnp.bfloat16)


def sort_kernel(run_slots, dest_ref, rows_ref, units_ref, slots_ref):
    rows = rows_ref.shape[0]
    runs = rows // PIECE
    dest = dest_ref[...]
    run = dest // run_slots
    within = dest % run_slots
    member = lax.broadcasted_iota(jnp.int32, (runs, rows), 0) == run
    before = lax.broadcasted_iota(jnp.int32, (rows, rows), 0) < lax.broadcasted_iota(
        jnp.int32, (rows, rows), 1
    )
    earlier = jnp.dot(
        member.astype(jnp.float32).astype(jnp.bfloat16),
        before.astype(jnp.float32).astype(jnp.bfloat16),
        preferred_element_type=jnp.float32,
    )
    rank = jnp.sum(jnp.where(member, earlier, 0.0), axis=0, keepdims=True).astype(jnp.int32)
    placed = run * PIECE + rank
    hot = (lax.broadcasted_iota(jnp.int32, (rows, rows), 0) == placed).astype(jnp.float32)
    hot = hot.astype(jnp.bfloat16)
    x = rows_ref[...].astype(jnp.float32)
    units = (x * lax.rsqrt(jnp.sum(x * x, axis=1, keepdims=True) + 1e-06)).astype(jnp.bfloat16)
    units_ref[...] = jnp.dot(hot, units, preferred_element_type=jnp.float32).astype(jnp.bfloat16)
    halves = jnp.concatenate(
        [jnp.broadcast_to(within // 256, (8, rows)), jnp.broadcast_to(within % 256, (8, rows))], axis=0
    )
    moved = lax.dot_general(
        halves.astype(jnp.float32).astype(jnp.bfloat16),
        hot,
        (((1,), (1,)), ((), ())),
        preferred_element_type=jnp.float32,
    )
    slots_ref[...] = (moved[0:1, :] * 256.0 + moved[8:9, :]).astype(jnp.int32)


def best_kernel(info_ref, slots_ref, keys_ref, out_ref, query_ref):
    shards, depth, width = keys_ref.shape
    queries = out_ref.shape[1]
    run_slots = shards * PIECE
    unit = min(run_slots, queries)
    first = info_ref[0]
    members = info_ref[1]
    first_run = first // run_slots

    def run_rows(run):
        start = pl.multiple_of(run * PIECE, PIECE)
        return keys_ref[:, pl.ds(start, PIECE), :].reshape(run_slots, width)

    def run_positions(run):
        start = pl.multiple_of(run * PIECE, PIECE)
        tile = slots_ref[pl.ds(start, PIECE), :]
        wide = jnp.broadcast_to(tile[None], (shards, PIECE, shards)).reshape(run_slots, shards)
        lane = lax.broadcasted_iota(jnp.int32, (run_slots, shards), 1)
        row = lax.broadcasted_iota(jnp.int32, (run_slots, shards), 0)
        picked = jnp.sum(jnp.where(lane == row // PIECE, wide, 0), axis=1, keepdims=True)
        return picked + run * run_slots

    for index in range(queries // unit):
        run = first_run + index
        lanes = lax.broadcasted_iota(jnp.int32, (run_slots, unit), 1) + (first + index * unit)
        hot = (run_positions(run) == lanes).astype(jnp.float32).astype(jnp.bfloat16)
        query_ref[:, index * unit : (index + 1) * unit] = lax.dot_general(
            run_rows(run), hot, (((0,), (0,)), ((), ())), preferred_element_type=jnp.float32
        ).astype(jnp.bfloat16)

    def fold(scores):
        return jnp.max(scores.reshape(run_slots // 8, 8, queries), axis=0)

    def step(run, running):
        scores = jnp.dot(run_rows(run), query_ref[...], preferred_element_type=jnp.float32)
        return jnp.maximum(running, fold(scores))

    running = lax.fori_loop(0, first_run, step, jnp.full((8, queries), -1.0, jnp.float32))
    position = first + lax.broadcasted_iota(jnp.int32, (1, queries), 1)
    for index in range(queries // unit):
        run = first_run + index
        scores = jnp.dot(run_rows(run), query_ref[...], preferred_element_type=jnp.float32)
        masked = jnp.where(run_positions(run) < position, scores, -2.0)
        running = jnp.maximum(running, fold(masked))
    found = jnp.max(running, axis=0, keepdims=True)
    out_ref[...] = jnp.where(position < members, found, 0.0)


def local_plane(embeddings, dest, sizes):
    chain_len = lax.axis_size("chain")
    clus_len = lax.axis_size("clus")
    shards = chain_len * clus_len
    rows, width = embeddings.shape
    clusters = sizes.shape[0]
    parts = chain_len // clusters
    run_slots = shards * PIECE
    depth = rows // chain_len
    my_chain = lax.axis_index("chain")
    my_clus = lax.axis_index("clus")
    cluster = my_chain // parts
    part = my_chain % parts

    units, slots = pl.pallas_call(
        functools.partial(sort_kernel, run_slots),
        out_shape=(
            jax.ShapeDtypeStruct((rows, width), jnp.bfloat16),
            jax.ShapeDtypeStruct((1, rows), jnp.int32),
        ),
        in_specs=[VMEM, VMEM],
        out_specs=(VMEM, VMEM),
        compiler_params=pltpu.CompilerParams(vmem_limit_bytes=32 * 2**20),
        name="sort_units",
    )(dest.reshape(1, rows), embeddings)

    slots = lax.all_gather(slots, ("chain", "clus"), axis=0, tiled=True)
    slots = slots.reshape(chain_len, clus_len, clusters, -1, PIECE)
    slots = lax.dynamic_index_in_dim(slots, cluster, 2, keepdims=False)
    slots = slots.transpose(2, 3, 1, 0).reshape(-1, shards)

    got = lax.all_to_all(units, "chain", split_axis=0, concat_axis=0, tiled=True)
    keys = lax.all_gather(got, "clus", axis=0, tiled=True).reshape(shards, depth, width)
    if parts > 1:
        pieces = []
        for wanted in range(parts):
            block = keys
            for other in range(parts):
                if other != wanted:
                    pairs = [(c * parts + wanted, c * parts + other) for c in range(clusters)]
                    came = lax.ppermute(keys, "chain", pairs)
                    block = jnp.where(part == other, came, block)
            pieces.append(block)
        keys = jnp.concatenate(pieces, axis=1)

    first = (part * clus_len + my_clus) * rows
    ids = jnp.arange(clusters, dtype=jnp.int32)
    members = jnp.sum(jnp.where(ids == cluster, sizes, 0))
    info = jnp.stack([first, members]).astype(jnp.int32)
    found = pl.pallas_call(
        best_kernel,
        out_shape=jax.ShapeDtypeStruct((1, rows), jnp.float32),
        in_specs=[SMEM, VMEM, VMEM],
        out_specs=VMEM,
        scratch_shapes=[pltpu.VMEM((width, rows), jnp.bfloat16)],
        compiler_params=pltpu.CompilerParams(vmem_limit_bytes=48 * 2**20),
        name="best_of_earlier",
    )(info, slots, keys)

    pairs = []
    for z in range(chain_len):
        for k in range(clus_len):
            pairs.append((z * clus_len + k, ((z % parts) * clus_len + k) * clus_len + z // parts))
    return lax.ppermute(found, ("chain", "clus"), pairs)


def send_kernel(run_slots, cluster_runs, dest_hbm, rows_hbm, kept_ref, slots_ref, given_ref, *scratch):
    dest_ref, rows_ref, sems = scratch
    dest_copy = pltpu.make_async_copy(dest_hbm, dest_ref, sems.at[0])
    rows_copy = pltpu.make_async_copy(rows_hbm, rows_ref, sems.at[1])
    dest_copy.start()
    rows_copy.start()
    rows, width = rows_ref.shape
    runs = rows // PIECE
    half = rows // 2
    depth = half // 2
    clus = lax.axis_index("clus")
    upper = (lax.axis_index("chain") >= lax.axis_size("chain") // 2).astype(jnp.int32)
    code = (clus // 2 ^ clus % 2 ^ upper) * 2 + upper
    before = lax.broadcasted_iota(jnp.int32, (rows, rows), 0) < lax.broadcasted_iota(
        jnp.int32, (rows, rows), 1
    )
    dest_copy.wait()
    dest = dest_ref[...]
    run = lax.div(dest, run_slots)
    within = lax.rem(dest, run_slots)
    run = (lax.div(run, cluster_runs) ^ code) * cluster_runs + lax.rem(run, cluster_runs)
    member = lax.broadcasted_iota(jnp.int32, (runs, rows), 0) == run
    earlier = jnp.dot(as_bf16(member), as_bf16(before), preferred_element_type=jnp.float32)
    rank = jnp.sum(jnp.where(member, earlier, 0.0), axis=0, keepdims=True).astype(jnp.int32)
    hot = as_bf16(lax.broadcasted_iota(jnp.int32, (rows, rows), 0) == run * PIECE + rank)
    moved = lax.dot_general(
        jnp.broadcast_to(within, (TILE, rows)).astype(jnp.float32).astype(jnp.bfloat16),
        hot,
        (((1,), (1,)), ((), ())),
        preferred_element_type=jnp.float32,
    )
    rows_copy.wait()
    x = rows_ref[...].astype(jnp.float32)
    units = (x * lax.rsqrt(jnp.sum(x * x, axis=1, keepdims=True) + 1e-06)).astype(jnp.bfloat16)
    for low, ref in ((0, kept_ref), (half, given_ref)):
        ref[0:half, :] = jnp.dot(
            hot[low : low + half], units, preferred_element_type=jnp.float32
        ).astype(jnp.bfloat16)
    line = lax.broadcasted_iota(jnp.int32, (TILE, half), 0)
    slots_ref[...] = jnp.where(line == 0, moved[:, 0:half], 0.0)
    given_ref[half : half + TILE, :] = jnp.zeros((TILE, width), jnp.bfloat16)
    given_ref[half : half + TILE, 0:half] = jnp.where(line == 1, moved[:, half:rows], 0.0).astype(
        jnp.bfloat16
    )


def merge_kernel(kept_ref, slots_ref, came_ref, near_ref, far_ref):
    half, width = kept_ref.shape
    depth = half // 2
    slots = slots_ref[...] + came_ref[half : half + TILE, 0:half].astype(jnp.float32)
    for low, ref in ((0, near_ref), (depth, far_ref)):
        ref[0:depth, :] = kept_ref[low : low + depth, :]
        ref[depth:half, :] = came_ref[low : low + depth, :]
        ref[half : half + TILE, :] = jnp.zeros((TILE, width), jnp.bfloat16)
        ref[half : half + TILE, 0:depth] = slots[:, low : low + depth].astype(jnp.bfloat16)


def home_chain():
    return lax.axis_size("chain") // 2 - 1 + lax.axis_index("clus") % 2


def stage_kernel(run_slots, old, new, last, *rest):
    sizes_ref, rest = (rest[0], rest[1:]) if last else (None, rest)
    refs, rest = rest[: old + new], rest[old + new :]
    old_states, rest = rest[: 2 * old], rest[2 * old :]
    outs = rest[: 1 if last else 2 * (old + new)]
    states = rest[len(outs) :] if last else outs
    rows = refs[0].shape[0] - TILE
    depth = rows // 2
    runs = depth // PIECE
    is_home = lax.axis_index("chain") == home_chain()

    def halves(value):
        best = value[:, 0:LANES]
        for low in range(LANES, value.shape[1], LANES):
            best = jnp.maximum(best, value[:, low : low + LANES])
        return best

    @pl.when(is_home)
    def _():
        for index in range(old):
            states[2 * index][...] = old_states[2 * index][...]
            states[2 * index + 1][...] = old_states[2 * index + 1][...]
        diagonal = lax.broadcasted_iota(jnp.int32, (rows, rows), 0) == lax.broadcasted_iota(
            jnp.int32, (rows, rows), 1
        )
        run_of = lax.broadcasted_iota(jnp.int32, (1, depth), 1) // PIECE
        for index in range(old, old + new):
            slots = refs[index][rows : rows + TILE, 0:depth].astype(jnp.float32)
            start = (run_of * run_slots).astype(jnp.float32)
            line = jnp.concatenate([slots[0:1] + start, slots[1:2] + start], axis=1)
            column = jnp.sum(jnp.where(diagonal, line, 0.0), axis=1, keepdims=True)
            states[2 * index][...] = jnp.broadcast_to(column, (rows, LANES))
            block = refs[index][0:rows, :]
            best = jnp.full((8, rows), -1.0, jnp.float32)
            for other in range(index + 1):
                scores = lax.dot_general(
                    refs[other][0:rows, :],
                    block,
                    (((1,), (1,)), ((), ())),
                    preferred_element_type=jnp.float32,
                )
                place = states[2 * other][...]
                earlier = jnp.concatenate([place] * (rows // LANES), axis=1) < line
                kept = jnp.where(earlier, scores, -2.0)
                best = jnp.maximum(best, jnp.max(kept.reshape(rows // 8, 8, rows), axis=0))
                if other < index:
                    given = halves(jnp.where(earlier, -2.0, scores))
                    states[2 * other + 1][...] = jnp.maximum(states[2 * other + 1][...], given)
            best = jnp.max(best, axis=0, keepdims=True)
            states[2 * index + 1][...] = halves(jnp.where(diagonal, best, -2.0))

    if last:
        (out_ref,) = outs
        chunk = out_ref.shape[1]

        @pl.when(jnp.logical_not(is_home))
        def _():
            out_ref[...] = jnp.zeros_like(out_ref)

        @pl.when(is_home)
        def _():
            members = sizes_ref[lax.axis_index("clus")]
            lane = lax.broadcasted_iota(jnp.int32, (run_slots, run_slots), 1)
            for run in range(runs):
                where = [
                    (index, low + run * PIECE) for index in range(old + new) for low in (0, depth)
                ]
                place, best = (
                    jnp.concatenate([states[2 * n + kind][at : at + PIECE, :] for n, at in where])
                    for kind in range(2)
                )
                best = jnp.max(best, axis=1, keepdims=True)
                place = jnp.concatenate([place] * (run_slots // LANES), axis=1)
                base = run * run_slots
                found = jnp.where(place == (lane + base).astype(jnp.float32), best, 0.0)
                found = jnp.sum(found, axis=0, keepdims=True)
                position = base + lax.broadcasted_iota(jnp.int32, (1, run_slots), 1)
                found = jnp.where(position < members, found, 0.0)
                row, low = base // chunk, base % chunk
                out_ref[row : row + 1, low : low + run_slots] = found


def local_home(embeddings, dest, sizes):
    chain_len = lax.axis_size("chain")
    clus_len = lax.axis_size("clus")
    rows, width = embeddings.shape
    half = rows // 2
    run_slots = chain_len * clus_len * PIECE
    block = jax.ShapeDtypeStruct((half + TILE, width), jnp.bfloat16)
    kept, slots, given = pl.pallas_call(
        functools.partial(send_kernel, run_slots, rows // clus_len // PIECE),
        out_shape=(
            jax.ShapeDtypeStruct((half, width), jnp.bfloat16),
            jax.ShapeDtypeStruct((TILE, half), jnp.float32),
            block,
        ),
        in_specs=[HBM, HBM],
        out_specs=(VMEM, VMEM, VMEM),
        scratch_shapes=[
            pltpu.VMEM((1, rows), jnp.int32),
            pltpu.VMEM((rows, width), jnp.bfloat16),
            pltpu.SemaphoreType.DMA((2,)),
        ],
        compiler_params=pltpu.CompilerParams(vmem_limit_bytes=32 * 2**20),
        name="send_blocks",
    )(dest.reshape(1, rows), embeddings)

    def permute(value, moves):
        pairs = [(a * clus_len + b, c * clus_len + d) for a, b, c, d in moves]
        return lax.ppermute(value, ("chain", "clus"), pairs)

    low, high, top = chain_len // 2 - 1, chain_len // 2, chain_len - 1
    swap = [(z, k, z, k ^ 1) for z in range(chain_len) for k in range(clus_len)]
    near, far = pl.pallas_call(
        merge_kernel,
        out_shape=(block, block),
        in_specs=[VMEM, VMEM, VMEM],
        out_specs=(VMEM, VMEM),
        compiler_params=pltpu.CompilerParams(vmem_limit_bytes=16 * 2**20),
        name="merge_blocks",
    )(kept, slots, permute(given, swap))

    def to_home(value, moves, across):
        pairs = []
        for a, b in moves:
            for x in range(clus_len // 2):
                source = 2 * x + (across ^ (a >= high))
                pairs.append((a, source, b, 2 * (x ^ across) + (b - low)))
        return permute(value, pairs)

    nearer, farther = [(0, low), (top, high)], [(0, high), (top, low)]
    middle, plane = [(low, high), (high, low)], [(low, low), (high, high)]
    stages = [
        [near, to_home(near, plane, 1), to_home(far, farther, 0)],
        [to_home(far, farther, 1), to_home(near, nearer, 0)],
        [to_home(near, nearer, 1), to_home(far, middle, 0)],
        [to_home(far, middle, 1)],
    ]
    blocks, states = [], []
    state = jax.ShapeDtypeStruct((half, LANES), jnp.float32)
    for number, arrived in enumerate(stages):
        last = number == len(stages) - 1
        old, new = len(blocks), len(arrived)
        blocks = blocks + arrived
        count = 2 * len(blocks)
        outs = (jax.ShapeDtypeStruct((chain_len, rows), jnp.float32),) if last else (state,) * count
        states = pl.pallas_call(
            functools.partial(stage_kernel, run_slots, old, new, last),
            out_shape=outs,
            in_specs=[SMEM] * last + [VMEM] * (len(blocks) + len(states)),
            out_specs=(VMEM,) * len(outs),
            scratch_shapes=[pltpu.VMEM(state.shape, jnp.float32)] * (count if last else 0),
            compiler_params=pltpu.CompilerParams(vmem_limit_bytes=32 * 2**20),
            name="multiply_last" if last else "multiply_arrived",
        )(*([sizes] if last else []), *blocks, *states)
    found = lax.all_to_all(states[0], "chain", split_axis=0, concat_axis=0, tiled=True)
    return jnp.sum(found, axis=0, keepdims=True)


def solution(mesh):
    return jax.shard_map(
        local_home if mesh.shape["chain"] == mesh.shape["clus"] == 4 else local_plane,
        mesh=mesh,
        in_specs=(
            P(("groups", "chain", "clus"), None),
            P(("groups", "chain", "clus")),
            P("groups"),
        ),
        out_specs=P(("groups", "clus"), "chain"),
        check_vma=False,
    )
```

```python
import functools

import jax
import jax.numpy as jnp
from jax import lax
from jax.experimental import pallas as pl
from jax.experimental.pallas import tpu as pltpu
from jax.sharding import PartitionSpec as P

TILE = 8
LANES = 128
PIECE = 16
VMEM = pl.BlockSpec(memory_space=pltpu.VMEM)
SMEM = pl.BlockSpec(memory_space=pltpu.SMEM)


def as_bf16(mask):
    return mask.astype(jnp.float32).astype(jnp.bfloat16)


def sort_kernel(run_slots, dest_ref, rows_ref, units_ref, slots_ref):
    rows = rows_ref.shape[0]
    runs = rows // PIECE
    dest = dest_ref[...]
    run = dest // run_slots
    within = dest % run_slots
    member = lax.broadcasted_iota(jnp.int32, (runs, rows), 0) == run
    before = lax.broadcasted_iota(jnp.int32, (rows, rows), 0) < lax.broadcasted_iota(
        jnp.int32, (rows, rows), 1
    )
    earlier = jnp.dot(
        member.astype(jnp.float32).astype(jnp.bfloat16),
        before.astype(jnp.float32).astype(jnp.bfloat16),
        preferred_element_type=jnp.float32,
    )
    rank = jnp.sum(jnp.where(member, earlier, 0.0), axis=0, keepdims=True).astype(jnp.int32)
    placed = run * PIECE + rank
    hot = (lax.broadcasted_iota(jnp.int32, (rows, rows), 0) == placed).astype(jnp.float32)
    hot = hot.astype(jnp.bfloat16)
    x = rows_ref[...].astype(jnp.float32)
    units = (x * lax.rsqrt(jnp.sum(x * x, axis=1, keepdims=True) + 1e-06)).astype(jnp.bfloat16)
    units_ref[...] = jnp.dot(hot, units, preferred_element_type=jnp.float32).astype(jnp.bfloat16)
    halves = jnp.concatenate(
        [jnp.broadcast_to(within // 256, (8, rows)), jnp.broadcast_to(within % 256, (8, rows))], axis=0
    )
    moved = lax.dot_general(
        halves.astype(jnp.float32).astype(jnp.bfloat16),
        hot,
        (((1,), (1,)), ((), ())),
        preferred_element_type=jnp.float32,
    )
    slots_ref[...] = (moved[0:1, :] * 256.0 + moved[8:9, :]).astype(jnp.int32)


def best_kernel(info_ref, slots_ref, keys_ref, out_ref, query_ref):
    shards, depth, width = keys_ref.shape
    queries = out_ref.shape[1]
    run_slots = shards * PIECE
    unit = min(run_slots, queries)
    first = info_ref[0]
    members = info_ref[1]
    first_run = first // run_slots

    def run_rows(run):
        start = pl.multiple_of(run * PIECE, PIECE)
        return keys_ref[:, pl.ds(start, PIECE), :].reshape(run_slots, width)

    def run_positions(run):
        start = pl.multiple_of(run * PIECE, PIECE)
        tile = slots_ref[pl.ds(start, PIECE), :]
        wide = jnp.broadcast_to(tile[None], (shards, PIECE, shards)).reshape(run_slots, shards)
        lane = lax.broadcasted_iota(jnp.int32, (run_slots, shards), 1)
        row = lax.broadcasted_iota(jnp.int32, (run_slots, shards), 0)
        picked = jnp.sum(jnp.where(lane == row // PIECE, wide, 0), axis=1, keepdims=True)
        return picked + run * run_slots

    for index in range(queries // unit):
        run = first_run + index
        lanes = lax.broadcasted_iota(jnp.int32, (run_slots, unit), 1) + (first + index * unit)
        hot = (run_positions(run) == lanes).astype(jnp.float32).astype(jnp.bfloat16)
        query_ref[:, index * unit : (index + 1) * unit] = lax.dot_general(
            run_rows(run), hot, (((0,), (0,)), ((), ())), preferred_element_type=jnp.float32
        ).astype(jnp.bfloat16)

    def fold(scores):
        return jnp.max(scores.reshape(run_slots // 8, 8, queries), axis=0)

    def step(run, running):
        scores = jnp.dot(run_rows(run), query_ref[...], preferred_element_type=jnp.float32)
        return jnp.maximum(running, fold(scores))

    running = lax.fori_loop(0, first_run, step, jnp.full((8, queries), -1.0, jnp.float32))
    position = first + lax.broadcasted_iota(jnp.int32, (1, queries), 1)
    for index in range(queries // unit):
        run = first_run + index
        scores = jnp.dot(run_rows(run), query_ref[...], preferred_element_type=jnp.float32)
        masked = jnp.where(run_positions(run) < position, scores, -2.0)
        running = jnp.maximum(running, fold(masked))
    found = jnp.max(running, axis=0, keepdims=True)
    out_ref[...] = jnp.where(position < members, found, 0.0)


def local_plane(embeddings, dest, sizes):
    chain_len = lax.axis_size("chain")
    clus_len = lax.axis_size("clus")
    shards = chain_len * clus_len
    rows, width = embeddings.shape
    clusters = sizes.shape[0]
    parts = chain_len // clusters
    run_slots = shards * PIECE
    depth = rows // chain_len
    my_chain = lax.axis_index("chain")
    my_clus = lax.axis_index("clus")
    cluster = my_chain // parts
    part = my_chain % parts

    units, slots = pl.pallas_call(
        functools.partial(sort_kernel, run_slots),
        out_shape=(
            jax.ShapeDtypeStruct((rows, width), jnp.bfloat16),
            jax.ShapeDtypeStruct((1, rows), jnp.int32),
        ),
        in_specs=[VMEM, VMEM],
        out_specs=(VMEM, VMEM),
        compiler_params=pltpu.CompilerParams(vmem_limit_bytes=32 * 2**20),
        name="sort_units",
    )(dest.reshape(1, rows), embeddings)

    slots = lax.all_gather(slots, ("chain", "clus"), axis=0, tiled=True)
    slots = slots.reshape(chain_len, clus_len, clusters, -1, PIECE)
    slots = lax.dynamic_index_in_dim(slots, cluster, 2, keepdims=False)
    slots = slots.transpose(2, 3, 1, 0).reshape(-1, shards)

    got = lax.all_to_all(units, "chain", split_axis=0, concat_axis=0, tiled=True)
    keys = lax.all_gather(got, "clus", axis=0, tiled=True).reshape(shards, depth, width)
    if parts > 1:
        pieces = []
        for wanted in range(parts):
            block = keys
            for other in range(parts):
                if other != wanted:
                    pairs = [(c * parts + wanted, c * parts + other) for c in range(clusters)]
                    came = lax.ppermute(keys, "chain", pairs)
                    block = jnp.where(part == other, came, block)
            pieces.append(block)
        keys = jnp.concatenate(pieces, axis=1)

    first = (part * clus_len + my_clus) * rows
    ids = jnp.arange(clusters, dtype=jnp.int32)
    members = jnp.sum(jnp.where(ids == cluster, sizes, 0))
    info = jnp.stack([first, members]).astype(jnp.int32)
    found = pl.pallas_call(
        best_kernel,
        out_shape=jax.ShapeDtypeStruct((1, rows), jnp.float32),
        in_specs=[SMEM, VMEM, VMEM],
        out_specs=VMEM,
        scratch_shapes=[pltpu.VMEM((width, rows), jnp.bfloat16)],
        compiler_params=pltpu.CompilerParams(vmem_limit_bytes=48 * 2**20),
        name="best_of_earlier",
    )(info, slots, keys)

    pairs = []
    for z in range(chain_len):
        for k in range(clus_len):
            pairs.append((z * clus_len + k, ((z % parts) * clus_len + k) * clus_len + z // parts))
    return lax.ppermute(found, ("chain", "clus"), pairs)


def send_kernel(run_slots, cluster_runs, dest_ref, rows_ref, kept_ref, slots_ref, given_ref):
    rows, width = rows_ref.shape
    runs = rows // PIECE
    half = rows // 2
    depth = half // 2
    clus = lax.axis_index("clus")
    upper = (lax.axis_index("chain") >= lax.axis_size("chain") // 2).astype(jnp.int32)
    code = (clus // 2 ^ clus % 2 ^ upper) * 2 + upper
    before = lax.broadcasted_iota(jnp.int32, (rows, rows), 0) < lax.broadcasted_iota(
        jnp.int32, (rows, rows), 1
    )
    dest = dest_ref[...]
    run = lax.div(dest, run_slots)
    within = lax.rem(dest, run_slots)
    run = (lax.div(run, cluster_runs) ^ code) * cluster_runs + lax.rem(run, cluster_runs)
    member = lax.broadcasted_iota(jnp.int32, (runs, rows), 0) == run
    earlier = jnp.dot(as_bf16(member), as_bf16(before), preferred_element_type=jnp.float32)
    rank = jnp.sum(jnp.where(member, earlier, 0.0), axis=0, keepdims=True).astype(jnp.int32)
    hot = as_bf16(lax.broadcasted_iota(jnp.int32, (rows, rows), 0) == run * PIECE + rank)
    moved = lax.dot_general(
        jnp.broadcast_to(within, (TILE, rows)).astype(jnp.float32).astype(jnp.bfloat16),
        hot,
        (((1,), (1,)), ((), ())),
        preferred_element_type=jnp.float32,
    )
    x = rows_ref[...].astype(jnp.float32)
    units = (x * lax.rsqrt(jnp.sum(x * x, axis=1, keepdims=True) + 1e-06)).astype(jnp.bfloat16)
    for low, ref in ((0, kept_ref), (half, given_ref)):
        ref[0:half, :] = jnp.dot(
            hot[low : low + half], units, preferred_element_type=jnp.float32
        ).astype(jnp.bfloat16)
    line = lax.broadcasted_iota(jnp.int32, (TILE, half), 0)
    slots_ref[...] = jnp.where(line == 0, moved[:, 0:half], 0.0)
    given_ref[half : half + TILE, :] = jnp.zeros((TILE, width), jnp.bfloat16)
    given_ref[half : half + TILE, 0:half] = jnp.where(line == 1, moved[:, half:rows], 0.0).astype(
        jnp.bfloat16
    )


def merge_kernel(kept_ref, slots_ref, came_ref, near_ref, far_ref):
    half, width = kept_ref.shape
    depth = half // 2
    slots = slots_ref[...] + came_ref[half : half + TILE, 0:half].astype(jnp.float32)
    for low, ref in ((0, near_ref), (depth, far_ref)):
        ref[0:depth, :] = kept_ref[low : low + depth, :]
        ref[depth:half, :] = came_ref[low : low + depth, :]
        ref[half : half + TILE, :] = jnp.zeros((TILE, width), jnp.bfloat16)
        ref[half : half + TILE, 0:depth] = slots[:, low : low + depth].astype(jnp.bfloat16)


def home_chain():
    return lax.axis_size("chain") // 2 - 1 + lax.axis_index("clus") % 2


def stage_kernel(run_slots, old, new, last, *rest):
    first = old == 0
    count_ref, rest = (rest[0], rest[1:]) if first or last else (None, rest)
    refs, rest = rest[: old + new], rest[old + new :]
    old_states, rest = rest[: 2 * old], rest[2 * old :]
    if last:
        chunk_refs = rest[: -1 - 2 * (old + new)]
        states, found_ref = rest[len(chunk_refs) : -1], rest[-1]
    else:
        states = rest[: 2 * (old + new)]
    rows = refs[0].shape[0] - TILE
    depth = rows // 2
    runs = depth // PIECE
    is_home = lax.axis_index("chain") == home_chain()

    def halves(value):
        best = value[:, 0:LANES]
        for low in range(LANES, value.shape[1], LANES):
            best = jnp.maximum(best, value[:, low : low + LANES])
        return best

    if first:
        members = count_ref[lax.axis_index("clus")].astype(jnp.float32)
        rest[-1][...] = jnp.full_like(rest[-1], members)

    @pl.when(is_home)
    def _():
        for index in range(old):
            states[2 * index][...] = old_states[2 * index][...]
            states[2 * index + 1][...] = old_states[2 * index + 1][...]
        diagonal = lax.broadcasted_iota(jnp.int32, (rows, rows), 0) == lax.broadcasted_iota(
            jnp.int32, (rows, rows), 1
        )
        run_of = lax.broadcasted_iota(jnp.int32, (1, depth), 1) // PIECE
        for index in range(old, old + new):
            slots = refs[index][rows : rows + TILE, 0:depth].astype(jnp.float32)
            start = (run_of * run_slots).astype(jnp.float32)
            line = jnp.concatenate([slots[0:1] + start, slots[1:2] + start], axis=1)
            column = jnp.sum(jnp.where(diagonal, line, 0.0), axis=1, keepdims=True)
            states[2 * index][...] = jnp.broadcast_to(column, (rows, LANES))
            block = refs[index][0:rows, :]
            best = jnp.full((8, rows), -1.0, jnp.float32)
            for other in range(index + 1):
                scores = lax.dot_general(
                    refs[other][0:rows, :],
                    block,
                    (((1,), (1,)), ((), ())),
                    preferred_element_type=jnp.float32,
                )
                place = states[2 * other][...]
                earlier = jnp.concatenate([place] * (rows // LANES), axis=1) < line
                kept = jnp.where(earlier, scores, -2.0)
                best = jnp.maximum(best, jnp.max(kept.reshape(rows // 8, 8, rows), axis=0))
                if other < index:
                    given = halves(jnp.where(earlier, -2.0, scores))
                    states[2 * other + 1][...] = jnp.maximum(states[2 * other + 1][...], given)
            best = jnp.max(best, axis=0, keepdims=True)
            states[2 * index + 1][...] = halves(jnp.where(diagonal, best, -2.0))

    if last:
        chunk = found_ref.shape[1]

        @pl.when(jnp.logical_not(is_home))
        def _():
            for ref in chunk_refs:
                ref[...] = jnp.zeros_like(ref)

        @pl.when(is_home)
        def _():
            members = jnp.concatenate([count_ref[0:1, :]] * (run_slots // LANES), axis=1)
            lane = lax.broadcasted_iota(jnp.int32, (run_slots, run_slots), 1)
            for run in range(runs):
                where = [
                    (index, low + run * PIECE) for index in range(old + new) for low in (0, depth)
                ]
                place, best = (
                    jnp.concatenate([states[2 * n + kind][at : at + PIECE, :] for n, at in where])
                    for kind in range(2)
                )
                best = jnp.max(best, axis=1, keepdims=True)
                place = jnp.concatenate([place] * (run_slots // LANES), axis=1)
                base = run * run_slots
                position = (lane + base).astype(jnp.float32)
                found = jnp.sum(jnp.where(place == position, best, 0.0), axis=0, keepdims=True)
                found = jnp.where(position[0:1] < members, found, 0.0)
                row, low = base // chunk, base % chunk
                found_ref[row : row + 1, low : low + run_slots] = found

        chain_len = len(chunk_refs)
        for home in (chain_len // 2 - 1, chain_len // 2):
            @pl.when(lax.axis_index("chain") == home)
            def _():
                for step, ref in enumerate(chunk_refs):
                    row = (home + step) % chain_len
                    ref[...] = jnp.where(is_home, found_ref[row : row + 1, :], 0.0)


def local_home(embeddings, dest, sizes):
    chain_len = lax.axis_size("chain")
    clus_len = lax.axis_size("clus")
    rows, width = embeddings.shape
    half = rows // 2
    run_slots = chain_len * clus_len * PIECE
    block = jax.ShapeDtypeStruct((half + TILE, width), jnp.bfloat16)
    kept, slots, given = pl.pallas_call(
        functools.partial(send_kernel, run_slots, rows // clus_len // PIECE),
        out_shape=(
            jax.ShapeDtypeStruct((half, width), jnp.bfloat16),
            jax.ShapeDtypeStruct((TILE, half), jnp.float32),
            block,
        ),
        in_specs=[VMEM, VMEM],
        out_specs=(VMEM, VMEM, VMEM),
        compiler_params=pltpu.CompilerParams(vmem_limit_bytes=32 * 2**20),
        name="send_blocks",
    )(dest.reshape(1, rows), embeddings)

    def permute(value, moves):
        pairs = [(a * clus_len + b, c * clus_len + d) for a, b, c, d in moves]
        return lax.ppermute(value, ("chain", "clus"), pairs)

    low, high, top = chain_len // 2 - 1, chain_len // 2, chain_len - 1
    swap = [(z, k, z, k ^ 1) for z in range(chain_len) for k in range(clus_len)]
    near, far = pl.pallas_call(
        merge_kernel,
        out_shape=(block, block),
        in_specs=[VMEM, VMEM, VMEM],
        out_specs=(VMEM, VMEM),
        compiler_params=pltpu.CompilerParams(vmem_limit_bytes=16 * 2**20),
        name="merge_blocks",
    )(kept, slots, permute(given, swap))

    def to_home(value, moves, across):
        pairs = []
        for a, b in moves:
            for x in range(clus_len // 2):
                source = 2 * x + (across ^ (a >= high))
                pairs.append((a, source, b, 2 * (x ^ across) + (b - low)))
        return permute(value, pairs)

    nearer, farther = [(0, low), (top, high)], [(0, high), (top, low)]
    middle, plane = [(low, high), (high, low)], [(low, low), (high, high)]
    stages = [
        [near, to_home(far, farther, 0), to_home(near, nearer, 0)],
        [to_home(far, farther, 1), to_home(near, nearer, 1)],
        [to_home(far, middle, 0), to_home(near, plane, 1)],
        [to_home(far, middle, 1)],
    ]
    blocks, states = [], []
    state = jax.ShapeDtypeStruct((half, LANES), jnp.float32)
    chunk = jax.ShapeDtypeStruct((1, rows), jnp.float32)
    for number, arrived in enumerate(stages):
        first, last = number == 0, number == len(stages) - 1
        old, new = len(blocks), len(arrived)
        blocks = blocks + arrived
        outs = (chunk,) * chain_len if last else (state,) * (2 * len(blocks))
        outs += (jax.ShapeDtypeStruct((TILE, LANES), jnp.float32),) * first
        scratch = [pltpu.VMEM(state.shape, state.dtype)] * (2 * len(blocks))
        scratch.append(pltpu.VMEM((chain_len, rows), jnp.float32))
        count = [sizes] if first else [members] if last else []
        states = pl.pallas_call(
            functools.partial(stage_kernel, run_slots, old, new, last),
            out_shape=outs,
            in_specs=[SMEM] * first + [VMEM] * (last + len(blocks) + len(states)),
            out_specs=(VMEM,) * len(outs),
            scratch_shapes=scratch * last,
            compiler_params=pltpu.CompilerParams(vmem_limit_bytes=32 * 2**20),
            name="multiply_last" if last else "multiply_arrived",
        )(*count, *blocks, *states)
        if first:
            *states, members = states
    found = states[0]
    for step in range(1, chain_len):
        moves = []
        for k in range(clus_len):
            home = low + k % 2
            moves.append((home, k, (home + step) % chain_len, k))
        found = found + permute(states[step], moves)
    return found


def solution(mesh):
    return jax.shard_map(
        local_home if mesh.shape["chain"] == mesh.shape["clus"] == 4 else local_plane,
        mesh=mesh,
        in_specs=(
            P(("groups", "chain", "clus"), None),
            P(("groups", "chain", "clus")),
            P("groups"),
        ),
        out_specs=P(("groups", "clus"), "chain"),
        check_vma=False,
    )
```

```python
import functools

import jax
import jax.numpy as jnp
from jax import lax
from jax.experimental import pallas as pl
from jax.experimental.pallas import tpu as pltpu
from jax.sharding import PartitionSpec as P

TILE = 8
LANES = 128
PIECE = 16
VMEM = pl.BlockSpec(memory_space=pltpu.VMEM)
SMEM = pl.BlockSpec(memory_space=pltpu.SMEM)


def as_bf16(mask):
    return mask.astype(jnp.float32).astype(jnp.bfloat16)


def sort_kernel(run_slots, dest_ref, rows_ref, units_ref, slots_ref):
    rows = rows_ref.shape[0]
    runs = rows // PIECE
    dest = dest_ref[...]
    run = dest // run_slots
    within = dest % run_slots
    member = lax.broadcasted_iota(jnp.int32, (runs, rows), 0) == run
    before = lax.broadcasted_iota(jnp.int32, (rows, rows), 0) < lax.broadcasted_iota(
        jnp.int32, (rows, rows), 1
    )
    earlier = jnp.dot(
        member.astype(jnp.float32).astype(jnp.bfloat16),
        before.astype(jnp.float32).astype(jnp.bfloat16),
        preferred_element_type=jnp.float32,
    )
    rank = jnp.sum(jnp.where(member, earlier, 0.0), axis=0, keepdims=True).astype(jnp.int32)
    placed = run * PIECE + rank
    hot = (lax.broadcasted_iota(jnp.int32, (rows, rows), 0) == placed).astype(jnp.float32)
    hot = hot.astype(jnp.bfloat16)
    x = rows_ref[...].astype(jnp.float32)
    units = (x * lax.rsqrt(jnp.sum(x * x, axis=1, keepdims=True) + 1e-06)).astype(jnp.bfloat16)
    units_ref[...] = jnp.dot(hot, units, preferred_element_type=jnp.float32).astype(jnp.bfloat16)
    halves = jnp.concatenate(
        [jnp.broadcast_to(within // 256, (8, rows)), jnp.broadcast_to(within % 256, (8, rows))], axis=0
    )
    moved = lax.dot_general(
        halves.astype(jnp.float32).astype(jnp.bfloat16),
        hot,
        (((1,), (1,)), ((), ())),
        preferred_element_type=jnp.float32,
    )
    slots_ref[...] = (moved[0:1, :] * 256.0 + moved[8:9, :]).astype(jnp.int32)


def best_kernel(info_ref, slots_ref, keys_ref, out_ref, query_ref):
    shards, depth, width = keys_ref.shape
    queries = out_ref.shape[1]
    run_slots = shards * PIECE
    unit = min(run_slots, queries)
    first = info_ref[0]
    members = info_ref[1]
    first_run = first // run_slots

    def run_rows(run):
        start = pl.multiple_of(run * PIECE, PIECE)
        return keys_ref[:, pl.ds(start, PIECE), :].reshape(run_slots, width)

    def run_positions(run):
        start = pl.multiple_of(run * PIECE, PIECE)
        tile = slots_ref[pl.ds(start, PIECE), :]
        wide = jnp.broadcast_to(tile[None], (shards, PIECE, shards)).reshape(run_slots, shards)
        lane = lax.broadcasted_iota(jnp.int32, (run_slots, shards), 1)
        row = lax.broadcasted_iota(jnp.int32, (run_slots, shards), 0)
        picked = jnp.sum(jnp.where(lane == row // PIECE, wide, 0), axis=1, keepdims=True)
        return picked + run * run_slots

    for index in range(queries // unit):
        run = first_run + index
        lanes = lax.broadcasted_iota(jnp.int32, (run_slots, unit), 1) + (first + index * unit)
        hot = (run_positions(run) == lanes).astype(jnp.float32).astype(jnp.bfloat16)
        query_ref[:, index * unit : (index + 1) * unit] = lax.dot_general(
            run_rows(run), hot, (((0,), (0,)), ((), ())), preferred_element_type=jnp.float32
        ).astype(jnp.bfloat16)

    def fold(scores):
        return jnp.max(scores.reshape(run_slots // 8, 8, queries), axis=0)

    def step(run, running):
        scores = jnp.dot(run_rows(run), query_ref[...], preferred_element_type=jnp.float32)
        return jnp.maximum(running, fold(scores))

    running = lax.fori_loop(0, first_run, step, jnp.full((8, queries), -1.0, jnp.float32))
    position = first + lax.broadcasted_iota(jnp.int32, (1, queries), 1)
    for index in range(queries // unit):
        run = first_run + index
        scores = jnp.dot(run_rows(run), query_ref[...], preferred_element_type=jnp.float32)
        masked = jnp.where(run_positions(run) < position, scores, -2.0)
        running = jnp.maximum(running, fold(masked))
    found = jnp.max(running, axis=0, keepdims=True)
    out_ref[...] = jnp.where(position < members, found, 0.0)


def local_plane(embeddings, dest, sizes):
    chain_len = lax.axis_size("chain")
    clus_len = lax.axis_size("clus")
    shards = chain_len * clus_len
    rows, width = embeddings.shape
    clusters = sizes.shape[0]
    parts = chain_len // clusters
    run_slots = shards * PIECE
    depth = rows // chain_len
    my_chain = lax.axis_index("chain")
    my_clus = lax.axis_index("clus")
    cluster = my_chain // parts
    part = my_chain % parts

    units, slots = pl.pallas_call(
        functools.partial(sort_kernel, run_slots),
        out_shape=(
            jax.ShapeDtypeStruct((rows, width), jnp.bfloat16),
            jax.ShapeDtypeStruct((1, rows), jnp.int32),
        ),
        in_specs=[VMEM, VMEM],
        out_specs=(VMEM, VMEM),
        compiler_params=pltpu.CompilerParams(vmem_limit_bytes=32 * 2**20),
        name="sort_units",
    )(dest.reshape(1, rows), embeddings)

    slots = lax.all_gather(slots, ("chain", "clus"), axis=0, tiled=True)
    slots = slots.reshape(chain_len, clus_len, clusters, -1, PIECE)
    slots = lax.dynamic_index_in_dim(slots, cluster, 2, keepdims=False)
    slots = slots.transpose(2, 3, 1, 0).reshape(-1, shards)

    got = lax.all_to_all(units, "chain", split_axis=0, concat_axis=0, tiled=True)
    keys = lax.all_gather(got, "clus", axis=0, tiled=True).reshape(shards, depth, width)
    if parts > 1:
        pieces = []
        for wanted in range(parts):
            block = keys
            for other in range(parts):
                if other != wanted:
                    pairs = [(c * parts + wanted, c * parts + other) for c in range(clusters)]
                    came = lax.ppermute(keys, "chain", pairs)
                    block = jnp.where(part == other, came, block)
            pieces.append(block)
        keys = jnp.concatenate(pieces, axis=1)

    first = (part * clus_len + my_clus) * rows
    ids = jnp.arange(clusters, dtype=jnp.int32)
    members = jnp.sum(jnp.where(ids == cluster, sizes, 0))
    info = jnp.stack([first, members]).astype(jnp.int32)
    found = pl.pallas_call(
        best_kernel,
        out_shape=jax.ShapeDtypeStruct((1, rows), jnp.float32),
        in_specs=[SMEM, VMEM, VMEM],
        out_specs=VMEM,
        scratch_shapes=[pltpu.VMEM((width, rows), jnp.bfloat16)],
        compiler_params=pltpu.CompilerParams(vmem_limit_bytes=48 * 2**20),
        name="best_of_earlier",
    )(info, slots, keys)

    pairs = []
    for z in range(chain_len):
        for k in range(clus_len):
            pairs.append((z * clus_len + k, ((z % parts) * clus_len + k) * clus_len + z // parts))
    return lax.ppermute(found, ("chain", "clus"), pairs)


def send_kernel(run_slots, cluster_runs, dest_ref, rows_ref, kept_ref, slots_ref, given_ref):
    rows, width = rows_ref.shape
    runs = rows // PIECE
    half = rows // 2
    depth = half // 2
    clus = lax.axis_index("clus")
    upper = (lax.axis_index("chain") >= lax.axis_size("chain") // 2).astype(jnp.int32)
    code = (clus // 2 ^ clus % 2 ^ upper) * 2 + upper
    before = lax.broadcasted_iota(jnp.int32, (rows, rows), 0) < lax.broadcasted_iota(
        jnp.int32, (rows, rows), 1
    )
    dest = dest_ref[...]
    run = lax.div(dest, run_slots)
    within = lax.rem(dest, run_slots)
    run = (lax.div(run, cluster_runs) ^ code) * cluster_runs + lax.rem(run, cluster_runs)
    member = lax.broadcasted_iota(jnp.int32, (runs, rows), 0) == run
    earlier = jnp.dot(as_bf16(member), as_bf16(before), preferred_element_type=jnp.float32)
    rank = jnp.sum(jnp.where(member, earlier, 0.0), axis=0, keepdims=True).astype(jnp.int32)
    hot = as_bf16(lax.broadcasted_iota(jnp.int32, (rows, rows), 0) == run * PIECE + rank)
    moved = lax.dot_general(
        jnp.broadcast_to(within, (TILE, rows)).astype(jnp.float32).astype(jnp.bfloat16),
        hot,
        (((1,), (1,)), ((), ())),
        preferred_element_type=jnp.float32,
    )
    x = rows_ref[...].astype(jnp.float32)
    units = (x * lax.rsqrt(jnp.sum(x * x, axis=1, keepdims=True) + 1e-06)).astype(jnp.bfloat16)
    for low, ref in ((0, kept_ref), (half, given_ref)):
        ref[0:half, :] = jnp.dot(
            hot[low : low + half], units, preferred_element_type=jnp.float32
        ).astype(jnp.bfloat16)
    line = lax.broadcasted_iota(jnp.int32, (TILE, half), 0)
    slots_ref[...] = jnp.where(line == 0, moved[:, 0:half], 0.0)
    given_ref[half : half + TILE, :] = jnp.zeros((TILE, width), jnp.bfloat16)
    given_ref[half : half + TILE, 0:half] = jnp.where(line == 1, moved[:, half:rows], 0.0).astype(
        jnp.bfloat16
    )


def merge_kernel(kept_ref, slots_ref, came_ref, near_ref, far_ref):
    half, width = kept_ref.shape
    depth = half // 2
    slots = slots_ref[...] + came_ref[half : half + TILE, 0:half].astype(jnp.float32)
    for low, ref in ((0, near_ref), (depth, far_ref)):
        ref[0:depth, :] = kept_ref[low : low + depth, :]
        ref[depth:half, :] = came_ref[low : low + depth, :]
        ref[half : half + TILE, :] = jnp.zeros((TILE, width), jnp.bfloat16)
        ref[half : half + TILE, 0:depth] = slots[:, low : low + depth].astype(jnp.bfloat16)


def home_chain():
    return lax.axis_size("chain") // 2 - 1 + lax.axis_index("clus") % 2


def stage_kernel(run_slots, height, count, old, new, last, *rest):
    first = old == 0
    count_ref, rest = (rest[0], rest[1:]) if first or last else (None, rest)
    refs = []
    for ref in rest[:count]:
        refs += [ref.at[pl.ds(low, height)] for low in range(0, ref.shape[0], height)]
    rest = rest[count:]
    old_states, rest = rest[: 2 * old], rest[2 * old :]
    if last:
        chunk_refs = rest[: -1 - 2 * (old + new)]
        states, found_ref = rest[len(chunk_refs) : -1], rest[-1]
    else:
        states = rest[: 2 * (old + new)]
    rows = refs[0].shape[0] - TILE
    depth = rows // 2
    runs = depth // PIECE
    is_home = lax.axis_index("chain") == home_chain()

    def halves(value):
        best = value[:, 0:LANES]
        for low in range(LANES, value.shape[1], LANES):
            best = jnp.maximum(best, value[:, low : low + LANES])
        return best

    if first:
        members = count_ref[lax.axis_index("clus")].astype(jnp.float32)
        rest[-1][...] = jnp.full_like(rest[-1], members)

    @pl.when(is_home)
    def _():
        for index in range(old):
            states[2 * index][...] = old_states[2 * index][...]
            states[2 * index + 1][...] = old_states[2 * index + 1][...]
        diagonal = lax.broadcasted_iota(jnp.int32, (rows, rows), 0) == lax.broadcasted_iota(
            jnp.int32, (rows, rows), 1
        )
        run_of = lax.broadcasted_iota(jnp.int32, (1, depth), 1) // PIECE
        for index in range(old, old + new):
            slots = refs[index][rows : rows + TILE, 0:depth].astype(jnp.float32)
            start = (run_of * run_slots).astype(jnp.float32)
            line = jnp.concatenate([slots[0:1] + start, slots[1:2] + start], axis=1)
            column = jnp.sum(jnp.where(diagonal, line, 0.0), axis=1, keepdims=True)
            states[2 * index][...] = jnp.broadcast_to(column, (rows, LANES))
            block = refs[index][0:rows, :]
            best = jnp.full((8, rows), -1.0, jnp.float32)
            for other in range(index + 1):
                scores = lax.dot_general(
                    refs[other][0:rows, :],
                    block,
                    (((1,), (1,)), ((), ())),
                    preferred_element_type=jnp.float32,
                )
                place = states[2 * other][...]
                earlier = jnp.concatenate([place] * (rows // LANES), axis=1) < line
                kept = jnp.where(earlier, scores, -2.0)
                best = jnp.maximum(best, jnp.max(kept.reshape(rows // 8, 8, rows), axis=0))
                if other < index:
                    given = halves(jnp.where(earlier, -2.0, scores))
                    states[2 * other + 1][...] = jnp.maximum(states[2 * other + 1][...], given)
            best = jnp.max(best, axis=0, keepdims=True)
            states[2 * index + 1][...] = halves(jnp.where(diagonal, best, -2.0))

    if last:
        chunk = found_ref.shape[1]

        @pl.when(jnp.logical_not(is_home))
        def _():
            for ref in chunk_refs:
                ref[...] = jnp.zeros_like(ref)

        @pl.when(is_home)
        def _():
            members = jnp.concatenate([count_ref[0:1, :]] * (run_slots // LANES), axis=1)
            lane = lax.broadcasted_iota(jnp.int32, (run_slots, run_slots), 1)
            for run in range(runs):
                where = [
                    (index, low + run * PIECE) for index in range(old + new) for low in (0, depth)
                ]
                place, best = (
                    jnp.concatenate([states[2 * n + kind][at : at + PIECE, :] for n, at in where])
                    for kind in range(2)
                )
                best = jnp.max(best, axis=1, keepdims=True)
                place = jnp.concatenate([place] * (run_slots // LANES), axis=1)
                base = run * run_slots
                position = (lane + base).astype(jnp.float32)
                found = jnp.sum(jnp.where(place == position, best, 0.0), axis=0, keepdims=True)
                found = jnp.where(position[0:1] < members, found, 0.0)
                row, low = base // chunk, base % chunk
                found_ref[row : row + 1, low : low + run_slots] = found

        chain_len = len(chunk_refs)
        for home in (chain_len // 2 - 1, chain_len // 2):
            @pl.when(lax.axis_index("chain") == home)
            def _():
                for step, ref in enumerate(chunk_refs):
                    row = (home + step) % chain_len
                    ref[...] = jnp.where(is_home, found_ref[row : row + 1, :], 0.0)


def local_home(embeddings, dest, sizes):
    chain_len = lax.axis_size("chain")
    clus_len = lax.axis_size("clus")
    rows, width = embeddings.shape
    half = rows // 2
    run_slots = chain_len * clus_len * PIECE
    block = jax.ShapeDtypeStruct((half + TILE, width), jnp.bfloat16)
    kept, slots, given = pl.pallas_call(
        functools.partial(send_kernel, run_slots, rows // clus_len // PIECE),
        out_shape=(
            jax.ShapeDtypeStruct((half, width), jnp.bfloat16),
            jax.ShapeDtypeStruct((TILE, half), jnp.float32),
            block,
        ),
        in_specs=[VMEM, VMEM],
        out_specs=(VMEM, VMEM, VMEM),
        compiler_params=pltpu.CompilerParams(vmem_limit_bytes=32 * 2**20),
        name="send_blocks",
    )(dest.reshape(1, rows), embeddings)

    def permute(value, moves):
        pairs = [(a * clus_len + b, c * clus_len + d) for a, b, c, d in moves]
        return lax.ppermute(value, ("chain", "clus"), pairs)

    low, high, top = chain_len // 2 - 1, chain_len // 2, chain_len - 1
    swap = [(z, k, z, k ^ 1) for z in range(chain_len) for k in range(clus_len)]
    near, far = pl.pallas_call(
        merge_kernel,
        out_shape=(block, block),
        in_specs=[VMEM, VMEM, VMEM],
        out_specs=(VMEM, VMEM),
        compiler_params=pltpu.CompilerParams(vmem_limit_bytes=16 * 2**20),
        name="merge_blocks",
    )(kept, slots, permute(given, swap))

    def flow(a, b, across, helper):
        return [
            (a, 2 * x + (across ^ (a >= high)), b, 2 * (x ^ across) + ((b - low) ^ helper))
            for x in range(clus_len // 2)
        ]

    both = ((0, low, high, top), (top, high, low, 0))
    from_far, from_near, across_near, from_middle, across_middle = [], [], [], [], []
    for end, close, distant, _ in both:
        from_far += flow(end, distant, 0, 0) + flow(end, distant, 1, 1)
        from_near += flow(end, close, 0, 0) + flow(close, close, 1, 1)
        across_near += flow(end, close, 1, 0)
        from_middle += flow(close, distant, 0, 0)
        across_middle += flow(close, distant, 1, 0)
    from_far, from_near = permute(far, from_far), permute(near, from_near)
    across_near = permute(near, across_near)
    from_middle, across_middle = permute(far, from_middle), permute(far, across_middle)
    forward = [(z, k ^ 1, z, k) for k in range(clus_len) for z in [low + k % 2]]
    helped = [permute(from_near, forward), permute(from_far, forward)]
    stages = [[near, from_far, from_near], [across_near, from_middle], [across_middle, helped[0]], [helped[1]]]
    blocks, states, held = [], [], 0
    state = jax.ShapeDtypeStruct((half, LANES), jnp.float32)
    chunk = jax.ShapeDtypeStruct((1, rows), jnp.float32)
    for number, arrived in enumerate(stages):
        first, last = number == 0, number == len(stages) - 1
        old, blocks = held, blocks + arrived
        held = sum(value.shape[0] for value in blocks) // (half + TILE)
        outs = (chunk,) * chain_len if last else (state,) * (2 * held)
        outs += (jax.ShapeDtypeStruct((TILE, LANES), jnp.float32),) * first
        scratch = [pltpu.VMEM(state.shape, state.dtype)] * (2 * held)
        scratch.append(pltpu.VMEM((chain_len, rows), jnp.float32))
        count = [sizes] if first else [members] if last else []
        states = pl.pallas_call(
            functools.partial(stage_kernel, run_slots, half + TILE, len(blocks), old, held - old, last),
            out_shape=outs,
            in_specs=[SMEM] * first + [VMEM] * (last + len(blocks) + len(states)),
            out_specs=(VMEM,) * len(outs),
            scratch_shapes=scratch * last,
            compiler_params=pltpu.CompilerParams(vmem_limit_bytes=32 * 2**20),
            name="multiply_last" if last else "multiply_arrived",
        )(*count, *blocks, *states)
        if first:
            *states, members = states
    found = states[0]
    for step in range(1, chain_len):
        moves = [
            (z, k, (z + step) % chain_len, k) for z in range(chain_len) for k in range(clus_len)
        ]
        found = found + permute(states[step], moves)
    return found


def solution(mesh):
    return jax.shard_map(
        local_home if mesh.shape["chain"] == mesh.shape["clus"] == 4 else local_plane,
        mesh=mesh,
        in_specs=(
            P(("groups", "chain", "clus"), None),
            P(("groups", "chain", "clus")),
            P("groups"),
        ),
        out_specs=P(("groups", "clus"), "chain"),
        check_vma=False,
    )
```

```python
import functools

import jax
import jax.numpy as jnp
from jax import lax
from jax.experimental import pallas as pl
from jax.experimental.pallas import tpu as pltpu
from jax.sharding import PartitionSpec as P

TILE = 8
LANES = 128
PIECE = 16
VMEM = pl.BlockSpec(memory_space=pltpu.VMEM)
SMEM = pl.BlockSpec(memory_space=pltpu.SMEM)


def as_bf16(mask):
    return mask.astype(jnp.float32).astype(jnp.bfloat16)


def sort_kernel(run_slots, dest_ref, rows_ref, units_ref, slots_ref):
    rows = rows_ref.shape[0]
    runs = rows // PIECE
    dest = dest_ref[...]
    run = dest // run_slots
    within = dest % run_slots
    member = lax.broadcasted_iota(jnp.int32, (runs, rows), 0) == run
    before = lax.broadcasted_iota(jnp.int32, (rows, rows), 0) < lax.broadcasted_iota(
        jnp.int32, (rows, rows), 1
    )
    earlier = jnp.dot(
        member.astype(jnp.float32).astype(jnp.bfloat16),
        before.astype(jnp.float32).astype(jnp.bfloat16),
        preferred_element_type=jnp.float32,
    )
    rank = jnp.sum(jnp.where(member, earlier, 0.0), axis=0, keepdims=True).astype(jnp.int32)
    placed = run * PIECE + rank
    hot = (lax.broadcasted_iota(jnp.int32, (rows, rows), 0) == placed).astype(jnp.float32)
    hot = hot.astype(jnp.bfloat16)
    x = rows_ref[...].astype(jnp.float32)
    units = (x * lax.rsqrt(jnp.sum(x * x, axis=1, keepdims=True) + 1e-06)).astype(jnp.bfloat16)
    units_ref[...] = jnp.dot(hot, units, preferred_element_type=jnp.float32).astype(jnp.bfloat16)
    halves = jnp.concatenate(
        [jnp.broadcast_to(within // 256, (8, rows)), jnp.broadcast_to(within % 256, (8, rows))], axis=0
    )
    moved = lax.dot_general(
        halves.astype(jnp.float32).astype(jnp.bfloat16),
        hot,
        (((1,), (1,)), ((), ())),
        preferred_element_type=jnp.float32,
    )
    slots_ref[...] = (moved[0:1, :] * 256.0 + moved[8:9, :]).astype(jnp.int32)


def best_kernel(info_ref, slots_ref, keys_ref, out_ref, query_ref):
    shards, depth, width = keys_ref.shape
    queries = out_ref.shape[1]
    run_slots = shards * PIECE
    unit = min(run_slots, queries)
    first = info_ref[0]
    members = info_ref[1]
    first_run = first // run_slots

    def run_rows(run):
        start = pl.multiple_of(run * PIECE, PIECE)
        return keys_ref[:, pl.ds(start, PIECE), :].reshape(run_slots, width)

    def run_positions(run):
        start = pl.multiple_of(run * PIECE, PIECE)
        tile = slots_ref[pl.ds(start, PIECE), :]
        wide = jnp.broadcast_to(tile[None], (shards, PIECE, shards)).reshape(run_slots, shards)
        lane = lax.broadcasted_iota(jnp.int32, (run_slots, shards), 1)
        row = lax.broadcasted_iota(jnp.int32, (run_slots, shards), 0)
        picked = jnp.sum(jnp.where(lane == row // PIECE, wide, 0), axis=1, keepdims=True)
        return picked + run * run_slots

    for index in range(queries // unit):
        run = first_run + index
        lanes = lax.broadcasted_iota(jnp.int32, (run_slots, unit), 1) + (first + index * unit)
        hot = (run_positions(run) == lanes).astype(jnp.float32).astype(jnp.bfloat16)
        query_ref[:, index * unit : (index + 1) * unit] = lax.dot_general(
            run_rows(run), hot, (((0,), (0,)), ((), ())), preferred_element_type=jnp.float32
        ).astype(jnp.bfloat16)

    def fold(scores):
        return jnp.max(scores.reshape(run_slots // 8, 8, queries), axis=0)

    def step(run, running):
        scores = jnp.dot(run_rows(run), query_ref[...], preferred_element_type=jnp.float32)
        return jnp.maximum(running, fold(scores))

    running = lax.fori_loop(0, first_run, step, jnp.full((8, queries), -1.0, jnp.float32))
    position = first + lax.broadcasted_iota(jnp.int32, (1, queries), 1)
    for index in range(queries // unit):
        run = first_run + index
        scores = jnp.dot(run_rows(run), query_ref[...], preferred_element_type=jnp.float32)
        masked = jnp.where(run_positions(run) < position, scores, -2.0)
        running = jnp.maximum(running, fold(masked))
    found = jnp.max(running, axis=0, keepdims=True)
    out_ref[...] = jnp.where(position < members, found, 0.0)


def local_plane(embeddings, dest, sizes):
    chain_len = lax.axis_size("chain")
    clus_len = lax.axis_size("clus")
    shards = chain_len * clus_len
    rows, width = embeddings.shape
    clusters = sizes.shape[0]
    parts = chain_len // clusters
    run_slots = shards * PIECE
    depth = rows // chain_len
    my_chain = lax.axis_index("chain")
    my_clus = lax.axis_index("clus")
    cluster = my_chain // parts
    part = my_chain % parts

    units, slots = pl.pallas_call(
        functools.partial(sort_kernel, run_slots),
        out_shape=(
            jax.ShapeDtypeStruct((rows, width), jnp.bfloat16),
            jax.ShapeDtypeStruct((1, rows), jnp.int32),
        ),
        in_specs=[VMEM, VMEM],
        out_specs=(VMEM, VMEM),
        compiler_params=pltpu.CompilerParams(vmem_limit_bytes=32 * 2**20),
        name="sort_units",
    )(dest.reshape(1, rows), embeddings)

    slots = lax.all_gather(slots, ("chain", "clus"), axis=0, tiled=True)
    slots = slots.reshape(chain_len, clus_len, clusters, -1, PIECE)
    slots = lax.dynamic_index_in_dim(slots, cluster, 2, keepdims=False)
    slots = slots.transpose(2, 3, 1, 0).reshape(-1, shards)

    got = lax.all_to_all(units, "chain", split_axis=0, concat_axis=0, tiled=True)
    keys = lax.all_gather(got, "clus", axis=0, tiled=True).reshape(shards, depth, width)
    if parts > 1:
        pieces = []
        for wanted in range(parts):
            block = keys
            for other in range(parts):
                if other != wanted:
                    pairs = [(c * parts + wanted, c * parts + other) for c in range(clusters)]
                    came = lax.ppermute(keys, "chain", pairs)
                    block = jnp.where(part == other, came, block)
            pieces.append(block)
        keys = jnp.concatenate(pieces, axis=1)

    first = (part * clus_len + my_clus) * rows
    ids = jnp.arange(clusters, dtype=jnp.int32)
    members = jnp.sum(jnp.where(ids == cluster, sizes, 0))
    info = jnp.stack([first, members]).astype(jnp.int32)
    found = pl.pallas_call(
        best_kernel,
        out_shape=jax.ShapeDtypeStruct((1, rows), jnp.float32),
        in_specs=[SMEM, VMEM, VMEM],
        out_specs=VMEM,
        scratch_shapes=[pltpu.VMEM((width, rows), jnp.bfloat16)],
        compiler_params=pltpu.CompilerParams(vmem_limit_bytes=48 * 2**20),
        name="best_of_earlier",
    )(info, slots, keys)

    pairs = []
    for z in range(chain_len):
        for k in range(clus_len):
            pairs.append((z * clus_len + k, ((z % parts) * clus_len + k) * clus_len + z // parts))
    return lax.ppermute(found, ("chain", "clus"), pairs)


def send_kernel(run_slots, cluster_runs, dest_ref, rows_ref, kept_ref, slots_ref, given_ref):
    rows, width = rows_ref.shape
    runs = rows // PIECE
    half = rows // 2
    depth = half // 2
    clus = lax.axis_index("clus")
    upper = (lax.axis_index("chain") >= lax.axis_size("chain") // 2).astype(jnp.int32)
    code = (clus // 2 ^ clus % 2 ^ upper) * 2 + upper
    before = lax.broadcasted_iota(jnp.int32, (rows, rows), 0) < lax.broadcasted_iota(
        jnp.int32, (rows, rows), 1
    )
    dest = dest_ref[...]
    run = lax.div(dest, run_slots)
    within = lax.rem(dest, run_slots)
    run = (lax.div(run, cluster_runs) ^ code) * cluster_runs + lax.rem(run, cluster_runs)
    member = lax.broadcasted_iota(jnp.int32, (runs, rows), 0) == run
    earlier = jnp.dot(as_bf16(member), as_bf16(before), preferred_element_type=jnp.float32)
    rank = jnp.sum(jnp.where(member, earlier, 0.0), axis=0, keepdims=True).astype(jnp.int32)
    hot = as_bf16(lax.broadcasted_iota(jnp.int32, (rows, rows), 0) == run * PIECE + rank)
    moved = lax.dot_general(
        jnp.broadcast_to(within, (TILE, rows)).astype(jnp.float32).astype(jnp.bfloat16),
        hot,
        (((1,), (1,)), ((), ())),
        preferred_element_type=jnp.float32,
    )
    x = rows_ref[...].astype(jnp.float32)
    units = (x * lax.rsqrt(jnp.sum(x * x, axis=1, keepdims=True) + 1e-06)).astype(jnp.bfloat16)
    for low, ref in ((0, kept_ref), (half, given_ref)):
        ref[0:half, :] = jnp.dot(
            hot[low : low + half], units, preferred_element_type=jnp.float32
        ).astype(jnp.bfloat16)
    line = lax.broadcasted_iota(jnp.int32, (TILE, half), 0)
    slots_ref[...] = jnp.where(line == 0, moved[:, 0:half], 0.0)
    given_ref[half : half + TILE, :] = jnp.zeros((TILE, width), jnp.bfloat16)
    given_ref[half : half + TILE, 0:half] = jnp.where(line == 1, moved[:, half:rows], 0.0).astype(
        jnp.bfloat16
    )


def merge_kernel(kept_ref, slots_ref, came_ref, near_ref, far_ref):
    half, width = kept_ref.shape
    depth = half // 2
    slots = slots_ref[...] + came_ref[half : half + TILE, 0:half].astype(jnp.float32)
    for low, ref in ((0, near_ref), (depth, far_ref)):
        ref[0:depth, :] = kept_ref[low : low + depth, :]
        ref[depth:half, :] = came_ref[low : low + depth, :]
        ref[half : half + TILE, :] = jnp.zeros((TILE, width), jnp.bfloat16)
        ref[half : half + TILE, 0:depth] = slots[:, low : low + depth].astype(jnp.bfloat16)


def home_chain():
    return lax.axis_size("chain") // 2 - 1 + lax.axis_index("clus") % 2


def stage_kernel(run_slots, height, count, old, new, last, *rest):
    first = old == 0
    count_ref, rest = (rest[0], rest[1:]) if first or last else (None, rest)
    refs = []
    for ref in rest[:count]:
        refs += [ref.at[pl.ds(low, height)] for low in range(0, ref.shape[0], height)]
    rest = rest[count:]
    old_states, rest = rest[: 2 * old], rest[2 * old :]
    if last:
        chunk_refs = rest[: -1 - 2 * (old + new)]
        states, found_ref = rest[len(chunk_refs) : -1], rest[-1]
    else:
        states = rest[: 2 * (old + new)]
    rows = refs[0].shape[0] - TILE
    depth = rows // 2
    runs = depth // PIECE
    is_home = lax.axis_index("chain") == home_chain()

    def halves(value):
        best = value[:, 0:LANES]
        for low in range(LANES, value.shape[1], LANES):
            best = jnp.maximum(best, value[:, low : low + LANES])
        return best

    if first:
        members = count_ref[lax.axis_index("clus")].astype(jnp.float32)
        rest[-1][...] = jnp.full_like(rest[-1], members)

    @pl.when(is_home)
    def _():
        for index in range(old):
            states[2 * index][...] = old_states[2 * index][...]
            states[2 * index + 1][...] = old_states[2 * index + 1][...]
        diagonal = lax.broadcasted_iota(jnp.int32, (rows, rows), 0) == lax.broadcasted_iota(
            jnp.int32, (rows, rows), 1
        )
        run_of = lax.broadcasted_iota(jnp.int32, (1, depth), 1) // PIECE
        for index in range(old, old + new):
            slots = refs[index][rows : rows + TILE, 0:depth].astype(jnp.float32)
            start = (run_of * run_slots).astype(jnp.float32)
            line = jnp.concatenate([slots[0:1] + start, slots[1:2] + start], axis=1)
            column = jnp.sum(jnp.where(diagonal, line, 0.0), axis=1, keepdims=True)
            states[2 * index][...] = jnp.broadcast_to(column, (rows, LANES))
            block = refs[index][0:rows, :]
            best = jnp.full((8, rows), -1.0, jnp.float32)
            for other in range(index + 1):
                scores = lax.dot_general(
                    refs[other][0:rows, :],
                    block,
                    (((1,), (1,)), ((), ())),
                    preferred_element_type=jnp.float32,
                )
                place = states[2 * other][...]
                earlier = jnp.concatenate([place] * (rows // LANES), axis=1) < line
                kept = jnp.where(earlier, scores, -2.0)
                best = jnp.maximum(best, jnp.max(kept.reshape(rows // 8, 8, rows), axis=0))
                if other < index:
                    given = halves(jnp.where(earlier, -2.0, scores))
                    states[2 * other + 1][...] = jnp.maximum(states[2 * other + 1][...], given)
            best = jnp.max(best, axis=0, keepdims=True)
            states[2 * index + 1][...] = halves(jnp.where(diagonal, best, -2.0))

    if last:
        chunk = found_ref.shape[1]

        @pl.when(jnp.logical_not(is_home))
        def _():
            for ref in chunk_refs:
                ref[...] = jnp.zeros_like(ref)

        @pl.when(is_home)
        def _():
            members = jnp.concatenate([count_ref[0:1, :]] * (run_slots // LANES), axis=1)
            lane = lax.broadcasted_iota(jnp.int32, (run_slots, run_slots), 1)
            for run in range(runs):
                where = [
                    (index, low + run * PIECE) for index in range(old + new) for low in (0, depth)
                ]
                place, best = (
                    jnp.concatenate([states[2 * n + kind][at : at + PIECE, :] for n, at in where])
                    for kind in range(2)
                )
                best = jnp.max(best, axis=1, keepdims=True)
                place = jnp.concatenate([place] * (run_slots // LANES), axis=1)
                base = run * run_slots
                position = (lane + base).astype(jnp.float32)
                found = jnp.sum(jnp.where(place == position, best, 0.0), axis=0, keepdims=True)
                found = jnp.where(position[0:1] < members, found, 0.0)
                row, low = base // chunk, base % chunk
                found_ref[row : row + 1, low : low + run_slots] = found

        chain_len = len(chunk_refs)
        for home in (chain_len // 2 - 1, chain_len // 2):
            @pl.when(lax.axis_index("chain") == home)
            def _():
                for step, ref in enumerate(chunk_refs):
                    row = (home + step) % chain_len
                    ref[...] = jnp.where(is_home, found_ref[row : row + 1, :], 0.0)


def local_home(embeddings, dest, sizes):
    chain_len = lax.axis_size("chain")
    clus_len = lax.axis_size("clus")
    rows, width = embeddings.shape
    half = rows // 2
    run_slots = chain_len * clus_len * PIECE
    block = jax.ShapeDtypeStruct((half + TILE, width), jnp.bfloat16)
    kept, slots, given = pl.pallas_call(
        functools.partial(send_kernel, run_slots, rows // clus_len // PIECE),
        out_shape=(
            jax.ShapeDtypeStruct((half, width), jnp.bfloat16),
            jax.ShapeDtypeStruct((TILE, half), jnp.float32),
            block,
        ),
        in_specs=[VMEM, VMEM],
        out_specs=(VMEM, VMEM, VMEM),
        compiler_params=pltpu.CompilerParams(vmem_limit_bytes=32 * 2**20),
        name="send_blocks",
    )(dest.reshape(1, rows), embeddings)

    def permute(value, moves):
        pairs = [(a * clus_len + b, c * clus_len + d) for a, b, c, d in moves]
        return lax.ppermute(value, ("chain", "clus"), pairs)

    low, high, top = chain_len // 2 - 1, chain_len // 2, chain_len - 1
    swap = [(z, k, z, k ^ 1) for z in range(chain_len) for k in range(clus_len)]
    near, far = pl.pallas_call(
        merge_kernel,
        out_shape=(block, block),
        in_specs=[VMEM, VMEM, VMEM],
        out_specs=(VMEM, VMEM),
        compiler_params=pltpu.CompilerParams(vmem_limit_bytes=16 * 2**20),
        name="merge_blocks",
    )(kept, slots, permute(given, swap))

    def serving(z, across):
        return across ^ (z >= high)

    def to_home(value, moves):
        columns = range(clus_len // 2)
        return permute(
            value, [(a, 2 * x + serving(a, 0), b, 2 * x + serving(b, 0)) for a, b in moves for x in columns]
        )

    def across(value):
        return permute(
            value,
            [
                (z, 2 * x + serving(z, 1), z, 2 * (x ^ 1) + serving(z, 0))
                for z in range(chain_len)
                for x in range(clus_len // 2)
            ],
        )

    from_far = [(0, high), (top, low)]
    from_near = [(0, low), (top, high)]
    from_middle = [(low, high), (high, low)]
    far_crossed, near_crossed = across(far), across(near)
    stages = [[near, to_home(far, from_far), to_home(near, from_near), to_home(far, from_middle), near_crossed], [to_home(far_crossed, from_far)], [to_home(near_crossed, from_near), to_home(far_crossed, from_middle)]]
    blocks, states, held = [], [], 0
    state = jax.ShapeDtypeStruct((half, LANES), jnp.float32)
    chunk = jax.ShapeDtypeStruct((1, rows), jnp.float32)
    for number, arrived in enumerate(stages):
        first, last = number == 0, number == len(stages) - 1
        old, blocks = held, blocks + arrived
        held = sum(value.shape[0] for value in blocks) // (half + TILE)
        outs = (chunk,) * chain_len if last else (state,) * (2 * held)
        outs += (jax.ShapeDtypeStruct((TILE, LANES), jnp.float32),) * first
        scratch = [pltpu.VMEM(state.shape, state.dtype)] * (2 * held)
        scratch.append(pltpu.VMEM((chain_len, rows), jnp.float32))
        count = [sizes] if first else [members] if last else []
        states = pl.pallas_call(
            functools.partial(stage_kernel, run_slots, half + TILE, len(blocks), old, held - old, last),
            out_shape=outs,
            in_specs=[SMEM] * first + [VMEM] * (last + len(blocks) + len(states)),
            out_specs=(VMEM,) * len(outs),
            scratch_shapes=scratch * last,
            compiler_params=pltpu.CompilerParams(vmem_limit_bytes=32 * 2**20),
            name="multiply_last" if last else "multiply_arrived",
        )(*count, *blocks, *states)
        if first:
            *states, members = states
    found = states[0]
    for step in range(1, chain_len):
        homes = [(low + k % 2, k) for k in range(clus_len)]
        moves = [(home, k, (home + step) % chain_len, k) for home, k in homes]
        found = found + permute(states[step], moves)
    return found


def solution(mesh):
    return jax.shard_map(
        local_home if mesh.shape["chain"] == mesh.shape["clus"] == 4 else local_plane,
        mesh=mesh,
        in_specs=(
            P(("groups", "chain", "clus"), None),
            P(("groups", "chain", "clus")),
            P("groups"),
        ),
        out_specs=P(("groups", "clus"), "chain"),
        check_vma=False,
    )
```

```python
import functools

import jax
import jax.numpy as jnp
from jax import lax
from jax.experimental import pallas as pl
from jax.experimental.pallas import tpu as pltpu
from jax.sharding import PartitionSpec as P

TILE = 8
LANES = 128
PIECE = 16
VMEM = pl.BlockSpec(memory_space=pltpu.VMEM)
SMEM = pl.BlockSpec(memory_space=pltpu.SMEM)


def as_bf16(mask):
    return mask.astype(jnp.float32).astype(jnp.bfloat16)


def sort_kernel(run_slots, dest_ref, rows_ref, units_ref, slots_ref):
    rows = rows_ref.shape[0]
    runs = rows // PIECE
    dest = dest_ref[...]
    run = dest // run_slots
    within = dest % run_slots
    member = lax.broadcasted_iota(jnp.int32, (runs, rows), 0) == run
    before = lax.broadcasted_iota(jnp.int32, (rows, rows), 0) < lax.broadcasted_iota(
        jnp.int32, (rows, rows), 1
    )
    earlier = jnp.dot(
        member.astype(jnp.float32).astype(jnp.bfloat16),
        before.astype(jnp.float32).astype(jnp.bfloat16),
        preferred_element_type=jnp.float32,
    )
    rank = jnp.sum(jnp.where(member, earlier, 0.0), axis=0, keepdims=True).astype(jnp.int32)
    placed = run * PIECE + rank
    hot = (lax.broadcasted_iota(jnp.int32, (rows, rows), 0) == placed).astype(jnp.float32)
    hot = hot.astype(jnp.bfloat16)
    x = rows_ref[...].astype(jnp.float32)
    units = (x * lax.rsqrt(jnp.sum(x * x, axis=1, keepdims=True) + 1e-06)).astype(jnp.bfloat16)
    units_ref[...] = jnp.dot(hot, units, preferred_element_type=jnp.float32).astype(jnp.bfloat16)
    halves = jnp.concatenate(
        [jnp.broadcast_to(within // 256, (8, rows)), jnp.broadcast_to(within % 256, (8, rows))], axis=0
    )
    moved = lax.dot_general(
        halves.astype(jnp.float32).astype(jnp.bfloat16),
        hot,
        (((1,), (1,)), ((), ())),
        preferred_element_type=jnp.float32,
    )
    slots_ref[...] = (moved[0:1, :] * 256.0 + moved[8:9, :]).astype(jnp.int32)


def best_kernel(info_ref, slots_ref, keys_ref, out_ref, query_ref):
    shards, depth, width = keys_ref.shape
    queries = out_ref.shape[1]
    run_slots = shards * PIECE
    unit = min(run_slots, queries)
    first = info_ref[0]
    members = info_ref[1]
    first_run = first // run_slots

    def run_rows(run):
        start = pl.multiple_of(run * PIECE, PIECE)
        return keys_ref[:, pl.ds(start, PIECE), :].reshape(run_slots, width)

    def run_positions(run):
        start = pl.multiple_of(run * PIECE, PIECE)
        tile = slots_ref[pl.ds(start, PIECE), :]
        wide = jnp.broadcast_to(tile[None], (shards, PIECE, shards)).reshape(run_slots, shards)
        lane = lax.broadcasted_iota(jnp.int32, (run_slots, shards), 1)
        row = lax.broadcasted_iota(jnp.int32, (run_slots, shards), 0)
        picked = jnp.sum(jnp.where(lane == row // PIECE, wide, 0), axis=1, keepdims=True)
        return picked + run * run_slots

    for index in range(queries // unit):
        run = first_run + index
        lanes = lax.broadcasted_iota(jnp.int32, (run_slots, unit), 1) + (first + index * unit)
        hot = (run_positions(run) == lanes).astype(jnp.float32).astype(jnp.bfloat16)
        query_ref[:, index * unit : (index + 1) * unit] = lax.dot_general(
            run_rows(run), hot, (((0,), (0,)), ((), ())), preferred_element_type=jnp.float32
        ).astype(jnp.bfloat16)

    def fold(scores):
        return jnp.max(scores.reshape(run_slots // 8, 8, queries), axis=0)

    def step(run, running):
        scores = jnp.dot(run_rows(run), query_ref[...], preferred_element_type=jnp.float32)
        return jnp.maximum(running, fold(scores))

    running = lax.fori_loop(0, first_run, step, jnp.full((8, queries), -1.0, jnp.float32))
    position = first + lax.broadcasted_iota(jnp.int32, (1, queries), 1)
    for index in range(queries // unit):
        run = first_run + index
        scores = jnp.dot(run_rows(run), query_ref[...], preferred_element_type=jnp.float32)
        masked = jnp.where(run_positions(run) < position, scores, -2.0)
        running = jnp.maximum(running, fold(masked))
    found = jnp.max(running, axis=0, keepdims=True)
    out_ref[...] = jnp.where(position < members, found, 0.0)


def local_plane(embeddings, dest, sizes):
    chain_len = lax.axis_size("chain")
    clus_len = lax.axis_size("clus")
    shards = chain_len * clus_len
    rows, width = embeddings.shape
    clusters = sizes.shape[0]
    parts = chain_len // clusters
    run_slots = shards * PIECE
    depth = rows // chain_len
    my_chain = lax.axis_index("chain")
    my_clus = lax.axis_index("clus")
    cluster = my_chain // parts
    part = my_chain % parts

    units, slots = pl.pallas_call(
        functools.partial(sort_kernel, run_slots),
        out_shape=(
            jax.ShapeDtypeStruct((rows, width), jnp.bfloat16),
            jax.ShapeDtypeStruct((1, rows), jnp.int32),
        ),
        in_specs=[VMEM, VMEM],
        out_specs=(VMEM, VMEM),
        compiler_params=pltpu.CompilerParams(vmem_limit_bytes=32 * 2**20),
        name="sort_units",
    )(dest.reshape(1, rows), embeddings)

    slots = lax.all_gather(slots, ("chain", "clus"), axis=0, tiled=True)
    slots = slots.reshape(chain_len, clus_len, clusters, -1, PIECE)
    slots = lax.dynamic_index_in_dim(slots, cluster, 2, keepdims=False)
    slots = slots.transpose(2, 3, 1, 0).reshape(-1, shards)

    got = lax.all_to_all(units, "chain", split_axis=0, concat_axis=0, tiled=True)
    keys = lax.all_gather(got, "clus", axis=0, tiled=True).reshape(shards, depth, width)
    if parts > 1:
        pieces = []
        for wanted in range(parts):
            block = keys
            for other in range(parts):
                if other != wanted:
                    pairs = [(c * parts + wanted, c * parts + other) for c in range(clusters)]
                    came = lax.ppermute(keys, "chain", pairs)
                    block = jnp.where(part == other, came, block)
            pieces.append(block)
        keys = jnp.concatenate(pieces, axis=1)

    first = (part * clus_len + my_clus) * rows
    ids = jnp.arange(clusters, dtype=jnp.int32)
    members = jnp.sum(jnp.where(ids == cluster, sizes, 0))
    info = jnp.stack([first, members]).astype(jnp.int32)
    found = pl.pallas_call(
        best_kernel,
        out_shape=jax.ShapeDtypeStruct((1, rows), jnp.float32),
        in_specs=[SMEM, VMEM, VMEM],
        out_specs=VMEM,
        scratch_shapes=[pltpu.VMEM((width, rows), jnp.bfloat16)],
        compiler_params=pltpu.CompilerParams(vmem_limit_bytes=48 * 2**20),
        name="best_of_earlier",
    )(info, slots, keys)

    pairs = []
    for z in range(chain_len):
        for k in range(clus_len):
            pairs.append((z * clus_len + k, ((z % parts) * clus_len + k) * clus_len + z // parts))
    return lax.ppermute(found, ("chain", "clus"), pairs)


def place_kernel(run_slots, cluster_runs, dest_ref, hot_ref, kept_slots_ref, given_slots_ref):
    rows = dest_ref.shape[1]
    runs = rows // PIECE
    half = rows // 2
    clus = lax.axis_index("clus")
    upper = (lax.axis_index("chain") >= lax.axis_size("chain") // 2).astype(jnp.int32)
    code = (clus // 2 ^ clus % 2 ^ upper) * 2 + upper
    before = lax.broadcasted_iota(jnp.int32, (rows, rows), 0) < lax.broadcasted_iota(
        jnp.int32, (rows, rows), 1
    )
    dest = dest_ref[...]
    run = lax.div(dest, run_slots)
    within = lax.rem(dest, run_slots)
    run = (lax.div(run, cluster_runs) ^ code) * cluster_runs + lax.rem(run, cluster_runs)
    member = lax.broadcasted_iota(jnp.int32, (runs, rows), 0) == run
    earlier = jnp.dot(as_bf16(member), as_bf16(before), preferred_element_type=jnp.float32)
    rank = jnp.sum(jnp.where(member, earlier, 0.0), axis=0, keepdims=True).astype(jnp.int32)
    hot = as_bf16(lax.broadcasted_iota(jnp.int32, (rows, rows), 0) == run * PIECE + rank)
    hot_ref[...] = hot
    moved = lax.dot_general(
        jnp.broadcast_to(within, (TILE, rows)).astype(jnp.float32).astype(jnp.bfloat16),
        hot,
        (((1,), (1,)), ((), ())),
        preferred_element_type=jnp.float32,
    )
    line = lax.broadcasted_iota(jnp.int32, (TILE, half), 0)
    kept_slots_ref[...] = jnp.where(line == 0, moved[:, 0:half], 0.0)
    given_slots_ref[...] = jnp.where(line == 1, moved[:, half:rows], 0.0)


def send_kernel(hot_ref, slots_ref, rows_ref, kept_ref, given_ref):
    rows, width = rows_ref.shape
    half = rows // 2
    x = rows_ref[...].astype(jnp.float32)
    units = (x * lax.rsqrt(jnp.sum(x * x, axis=1, keepdims=True) + 1e-06)).astype(jnp.bfloat16)
    for low, ref in ((0, kept_ref), (half, given_ref)):
        ref[0:half, :] = jnp.dot(
            hot_ref[low : low + half, :], units, preferred_element_type=jnp.float32
        ).astype(jnp.bfloat16)
    given_ref[half : half + TILE, :] = jnp.zeros((TILE, width), jnp.bfloat16)
    given_ref[half : half + TILE, 0:half] = slots_ref[...].astype(jnp.bfloat16)


def merge_kernel(kept_ref, slots_ref, came_ref, near_ref, far_ref):
    half, width = kept_ref.shape
    depth = half // 2
    slots = slots_ref[...] + came_ref[half : half + TILE, 0:half].astype(jnp.float32)
    for low, ref in ((0, near_ref), (depth, far_ref)):
        ref[0:depth, :] = kept_ref[low : low + depth, :]
        ref[depth:half, :] = came_ref[low : low + depth, :]
        ref[half : half + TILE, :] = jnp.zeros((TILE, width), jnp.bfloat16)
        ref[half : half + TILE, 0:depth] = slots[:, low : low + depth].astype(jnp.bfloat16)


def home_chain():
    return lax.axis_size("chain") // 2 - 1 + lax.axis_index("clus") % 2


def stage_kernel(run_slots, height, count, old, new, last, *rest):
    first = old == 0
    count_ref, rest = (rest[0], rest[1:]) if first or last else (None, rest)
    refs = []
    for ref in rest[:count]:
        refs += [ref.at[pl.ds(low, height)] for low in range(0, ref.shape[0], height)]
    rest = rest[count:]
    old_states, rest = rest[: 2 * old], rest[2 * old :]
    if last:
        chunk_refs = rest[: -1 - 2 * (old + new)]
        states, found_ref = rest[len(chunk_refs) : -1], rest[-1]
    else:
        states = rest[: 2 * (old + new)]
    rows = refs[0].shape[0] - TILE
    depth = rows // 2
    runs = depth // PIECE
    is_home = lax.axis_index("chain") == home_chain()

    def halves(value):
        best = value[:, 0:LANES]
        for low in range(LANES, value.shape[1], LANES):
            best = jnp.maximum(best, value[:, low : low + LANES])
        return best

    if first:
        members = count_ref[lax.axis_index("clus")].astype(jnp.float32)
        rest[-1][...] = jnp.full_like(rest[-1], members)

    @pl.when(is_home)
    def _():
        for index in range(old):
            states[2 * index][...] = old_states[2 * index][...]
            states[2 * index + 1][...] = old_states[2 * index + 1][...]
        diagonal = lax.broadcasted_iota(jnp.int32, (rows, rows), 0) == lax.broadcasted_iota(
            jnp.int32, (rows, rows), 1
        )
        run_of = lax.broadcasted_iota(jnp.int32, (1, depth), 1) // PIECE
        for index in range(old, old + new):
            slots = refs[index][rows : rows + TILE, 0:depth].astype(jnp.float32)
            start = (run_of * run_slots).astype(jnp.float32)
            line = jnp.concatenate([slots[0:1] + start, slots[1:2] + start], axis=1)
            column = jnp.sum(jnp.where(diagonal, line, 0.0), axis=1, keepdims=True)
            states[2 * index][...] = jnp.broadcast_to(column, (rows, LANES))
            block = refs[index][0:rows, :]
            best = jnp.full((8, rows), -1.0, jnp.float32)
            for other in range(index + 1):
                scores = lax.dot_general(
                    refs[other][0:rows, :],
                    block,
                    (((1,), (1,)), ((), ())),
                    preferred_element_type=jnp.float32,
                )
                place = states[2 * other][...]
                earlier = jnp.concatenate([place] * (rows // LANES), axis=1) < line
                kept = jnp.where(earlier, scores, -2.0)
                best = jnp.maximum(best, jnp.max(kept.reshape(rows // 8, 8, rows), axis=0))
                if other < index:
                    given = halves(jnp.where(earlier, -2.0, scores))
                    states[2 * other + 1][...] = jnp.maximum(states[2 * other + 1][...], given)
            best = jnp.max(best, axis=0, keepdims=True)
            states[2 * index + 1][...] = halves(jnp.where(diagonal, best, -2.0))

    if last:
        chunk = found_ref.shape[1]

        @pl.when(jnp.logical_not(is_home))
        def _():
            for ref in chunk_refs:
                ref[...] = jnp.zeros_like(ref)

        @pl.when(is_home)
        def _():
            members = jnp.concatenate([count_ref[0:1, :]] * (run_slots // LANES), axis=1)
            lane = lax.broadcasted_iota(jnp.int32, (run_slots, run_slots), 1)
            for run in range(runs):
                where = [
                    (index, low + run * PIECE) for index in range(old + new) for low in (0, depth)
                ]
                place, best = (
                    jnp.concatenate([states[2 * n + kind][at : at + PIECE, :] for n, at in where])
                    for kind in range(2)
                )
                best = jnp.max(best, axis=1, keepdims=True)
                place = jnp.concatenate([place] * (run_slots // LANES), axis=1)
                base = run * run_slots
                position = (lane + base).astype(jnp.float32)
                found = jnp.sum(jnp.where(place == position, best, 0.0), axis=0, keepdims=True)
                found = jnp.where(position[0:1] < members, found, 0.0)
                row, low = base // chunk, base % chunk
                found_ref[row : row + 1, low : low + run_slots] = found

        chain_len = len(chunk_refs)
        for home in (chain_len // 2 - 1, chain_len // 2):
            @pl.when(lax.axis_index("chain") == home)
            def _():
                for step, ref in enumerate(chunk_refs):
                    row = (home + step) % chain_len
                    ref[...] = jnp.where(is_home, found_ref[row : row + 1, :], 0.0)


def local_home(embeddings, dest, sizes):
    chain_len = lax.axis_size("chain")
    clus_len = lax.axis_size("clus")
    rows, width = embeddings.shape
    half = rows // 2
    run_slots = chain_len * clus_len * PIECE
    block = jax.ShapeDtypeStruct((half + TILE, width), jnp.bfloat16)
    slots = jax.ShapeDtypeStruct((TILE, half), jnp.float32)
    hot, slots, given_slots = pl.pallas_call(
        functools.partial(place_kernel, run_slots, rows // clus_len // PIECE),
        out_shape=(jax.ShapeDtypeStruct((rows, rows), jnp.bfloat16), slots, slots),
        in_specs=[VMEM],
        out_specs=(VMEM,) * 3,
        cost_estimate=pl.CostEstimate(flops=0, bytes_accessed=8 * rows * width, transcendentals=0),
        compiler_params=pltpu.CompilerParams(vmem_limit_bytes=16 * 2**20),
        name="place_rows",
    )(dest.reshape(1, rows))
    kept, given = pl.pallas_call(
        send_kernel,
        out_shape=(jax.ShapeDtypeStruct((half, width), jnp.bfloat16), block),
        in_specs=[VMEM] * 3,
        out_specs=(VMEM, VMEM),
        compiler_params=pltpu.CompilerParams(vmem_limit_bytes=16 * 2**20),
        name="send_blocks",
    )(hot, given_slots, embeddings)

    def permute(value, moves):
        pairs = [(a * clus_len + b, c * clus_len + d) for a, b, c, d in moves]
        return lax.ppermute(value, ("chain", "clus"), pairs)

    low, high, top = chain_len // 2 - 1, chain_len // 2, chain_len - 1
    swap = [(z, k, z, k ^ 1) for z in range(chain_len) for k in range(clus_len)]
    near, far = pl.pallas_call(
        merge_kernel,
        out_shape=(block, block),
        in_specs=[VMEM, VMEM, VMEM],
        out_specs=(VMEM, VMEM),
        compiler_params=pltpu.CompilerParams(vmem_limit_bytes=16 * 2**20),
        name="merge_blocks",
    )(kept, slots, permute(given, swap))

    def serving(z, across):
        return across ^ (z >= high)

    def to_home(value, moves):
        columns = range(clus_len // 2)
        pairs = [(a, 2 * x + serving(a, 0), b, 2 * x + serving(b, 0)) for a, b in moves for x in columns]
        if {a for a, _ in moves} == {b for _, b in moves}:
            taken = {pair[:2] for pair in pairs}
            everyone = [(z, k) for z in range(chain_len) for k in range(clus_len)]
            pairs += [place + place for place in everyone if place not in taken]
        return permute(value, pairs)

    def across(value):
        pairs = []
        for z in range(chain_len):
            for x in range(clus_len // 2):
                own, other = serving(z, 0), serving(z, 1)
                pairs.append((z, 2 * x + other, z, 2 * (x ^ 1) + own))
                pairs.append((z, 2 * x + own, z, 2 * x + other))
        return permute(value, pairs)

    from_far = [(0, high), (top, low)]
    from_near = [(0, low), (top, high)]
    from_middle = [(low, high), (high, low)]
    far_crossed, near_crossed = across(far), across(near)
    far_along, near_along = to_home(far, from_far), to_home(near, from_near)
    middle_along = to_home(far, from_middle)
    far_after, near_after = to_home(far_crossed, from_far), to_home(near_crossed, from_near)
    middle_after = to_home(far_crossed, from_middle)
    stages = [[near, near_crossed, near_along, far_along], [far_after, middle_along], [near_after, middle_after]]
    blocks, states, held = [], [], 0
    state = jax.ShapeDtypeStruct((half, LANES), jnp.float32)
    chunk = jax.ShapeDtypeStruct((1, rows), jnp.float32)
    for number, arrived in enumerate(stages):
        first, last = number == 0, number == len(stages) - 1
        old, blocks = held, blocks + arrived
        held = sum(value.shape[0] for value in blocks) // (half + TILE)
        outs = (chunk,) * chain_len if last else (state,) * (2 * held)
        outs += (jax.ShapeDtypeStruct((TILE, LANES), jnp.float32),) * first
        scratch = [pltpu.VMEM(state.shape, state.dtype)] * (2 * held)
        scratch.append(pltpu.VMEM((chain_len, rows), jnp.float32))
        count = [sizes] if first else [members] if last else []
        states = pl.pallas_call(
            functools.partial(stage_kernel, run_slots, half + TILE, len(blocks), old, held - old, last),
            out_shape=outs,
            in_specs=[SMEM] * first + [VMEM] * (last + len(blocks) + len(states)),
            out_specs=(VMEM,) * len(outs),
            scratch_shapes=scratch * last,
            compiler_params=pltpu.CompilerParams(vmem_limit_bytes=32 * 2**20),
            name="multiply_last" if last else "multiply_arrived",
        )(*count, *blocks, *states)
        if first:
            *states, members = states
    found = states[0]
    for step in range(1, chain_len):
        homes = [(low + k % 2, k) for k in range(clus_len)]
        moves = [(home, k, (home + step) % chain_len, k) for home, k in homes]
        found = found + permute(states[step], moves)
    return found


def solution(mesh):
    return jax.shard_map(
        local_home if mesh.shape["chain"] == mesh.shape["clus"] == 4 else local_plane,
        mesh=mesh,
        in_specs=(
            P(("groups", "chain", "clus"), None),
            P(("groups", "chain", "clus")),
            P("groups"),
        ),
        out_specs=P(("groups", "clus"), "chain"),
        check_vma=False,
    )
```

```python
import functools

import jax
import jax.numpy as jnp
from jax import lax
from jax.experimental import pallas as pl
from jax.experimental.pallas import tpu as pltpu
from jax.sharding import PartitionSpec as P

TILE = 8
LANES = 128
PIECE = 16
VMEM = pl.BlockSpec(memory_space=pltpu.VMEM)
SMEM = pl.BlockSpec(memory_space=pltpu.SMEM)


def as_bf16(mask):
    return mask.astype(jnp.float32).astype(jnp.bfloat16)


def sort_kernel(run_slots, dest_ref, rows_ref, units_ref, slots_ref):
    rows = rows_ref.shape[0]
    runs = rows // PIECE
    dest = dest_ref[...]
    run = dest // run_slots
    within = dest % run_slots
    member = lax.broadcasted_iota(jnp.int32, (runs, rows), 0) == run
    before = lax.broadcasted_iota(jnp.int32, (rows, rows), 0) < lax.broadcasted_iota(
        jnp.int32, (rows, rows), 1
    )
    earlier = jnp.dot(
        member.astype(jnp.float32).astype(jnp.bfloat16),
        before.astype(jnp.float32).astype(jnp.bfloat16),
        preferred_element_type=jnp.float32,
    )
    rank = jnp.sum(jnp.where(member, earlier, 0.0), axis=0, keepdims=True).astype(jnp.int32)
    placed = run * PIECE + rank
    hot = (lax.broadcasted_iota(jnp.int32, (rows, rows), 0) == placed).astype(jnp.float32)
    hot = hot.astype(jnp.bfloat16)
    x = rows_ref[...].astype(jnp.float32)
    units = (x * lax.rsqrt(jnp.sum(x * x, axis=1, keepdims=True) + 1e-06)).astype(jnp.bfloat16)
    units_ref[...] = jnp.dot(hot, units, preferred_element_type=jnp.float32).astype(jnp.bfloat16)
    halves = jnp.concatenate(
        [jnp.broadcast_to(within // 256, (8, rows)), jnp.broadcast_to(within % 256, (8, rows))], axis=0
    )
    moved = lax.dot_general(
        halves.astype(jnp.float32).astype(jnp.bfloat16),
        hot,
        (((1,), (1,)), ((), ())),
        preferred_element_type=jnp.float32,
    )
    slots_ref[...] = (moved[0:1, :] * 256.0 + moved[8:9, :]).astype(jnp.int32)


def best_kernel(info_ref, slots_ref, keys_ref, out_ref, query_ref):
    shards, depth, width = keys_ref.shape
    queries = out_ref.shape[1]
    run_slots = shards * PIECE
    unit = min(run_slots, queries)
    first = info_ref[0]
    members = info_ref[1]
    first_run = first // run_slots

    def run_rows(run):
        start = pl.multiple_of(run * PIECE, PIECE)
        return keys_ref[:, pl.ds(start, PIECE), :].reshape(run_slots, width)

    def run_positions(run):
        start = pl.multiple_of(run * PIECE, PIECE)
        tile = slots_ref[pl.ds(start, PIECE), :]
        wide = jnp.broadcast_to(tile[None], (shards, PIECE, shards)).reshape(run_slots, shards)
        lane = lax.broadcasted_iota(jnp.int32, (run_slots, shards), 1)
        row = lax.broadcasted_iota(jnp.int32, (run_slots, shards), 0)
        picked = jnp.sum(jnp.where(lane == row // PIECE, wide, 0), axis=1, keepdims=True)
        return picked + run * run_slots

    for index in range(queries // unit):
        run = first_run + index
        lanes = lax.broadcasted_iota(jnp.int32, (run_slots, unit), 1) + (first + index * unit)
        hot = (run_positions(run) == lanes).astype(jnp.float32).astype(jnp.bfloat16)
        query_ref[:, index * unit : (index + 1) * unit] = lax.dot_general(
            run_rows(run), hot, (((0,), (0,)), ((), ())), preferred_element_type=jnp.float32
        ).astype(jnp.bfloat16)

    def fold(scores):
        return jnp.max(scores.reshape(run_slots // 8, 8, queries), axis=0)

    def step(run, running):
        scores = jnp.dot(run_rows(run), query_ref[...], preferred_element_type=jnp.float32)
        return jnp.maximum(running, fold(scores))

    running = lax.fori_loop(0, first_run, step, jnp.full((8, queries), -1.0, jnp.float32))
    position = first + lax.broadcasted_iota(jnp.int32, (1, queries), 1)
    for index in range(queries // unit):
        run = first_run + index
        scores = jnp.dot(run_rows(run), query_ref[...], preferred_element_type=jnp.float32)
        masked = jnp.where(run_positions(run) < position, scores, -2.0)
        running = jnp.maximum(running, fold(masked))
    found = jnp.max(running, axis=0, keepdims=True)
    out_ref[...] = jnp.where(position < members, found, 0.0)


def local_plane(embeddings, dest, sizes):
    chain_len = lax.axis_size("chain")
    clus_len = lax.axis_size("clus")
    shards = chain_len * clus_len
    rows, width = embeddings.shape
    clusters = sizes.shape[0]
    parts = chain_len // clusters
    run_slots = shards * PIECE
    depth = rows // chain_len
    my_chain = lax.axis_index("chain")
    my_clus = lax.axis_index("clus")
    cluster = my_chain // parts
    part = my_chain % parts

    units, slots = pl.pallas_call(
        functools.partial(sort_kernel, run_slots),
        out_shape=(
            jax.ShapeDtypeStruct((rows, width), jnp.bfloat16),
            jax.ShapeDtypeStruct((1, rows), jnp.int32),
        ),
        in_specs=[VMEM, VMEM],
        out_specs=(VMEM, VMEM),
        compiler_params=pltpu.CompilerParams(vmem_limit_bytes=32 * 2**20),
        name="sort_units",
    )(dest.reshape(1, rows), embeddings)

    slots = lax.all_gather(slots, ("chain", "clus"), axis=0, tiled=True)
    slots = slots.reshape(chain_len, clus_len, clusters, -1, PIECE)
    slots = lax.dynamic_index_in_dim(slots, cluster, 2, keepdims=False)
    slots = slots.transpose(2, 3, 1, 0).reshape(-1, shards)

    got = lax.all_to_all(units, "chain", split_axis=0, concat_axis=0, tiled=True)
    keys = lax.all_gather(got, "clus", axis=0, tiled=True).reshape(shards, depth, width)
    if parts > 1:
        pieces = []
        for wanted in range(parts):
            block = keys
            for other in range(parts):
                if other != wanted:
                    pairs = [(c * parts + wanted, c * parts + other) for c in range(clusters)]
                    came = lax.ppermute(keys, "chain", pairs)
                    block = jnp.where(part == other, came, block)
            pieces.append(block)
        keys = jnp.concatenate(pieces, axis=1)

    first = (part * clus_len + my_clus) * rows
    ids = jnp.arange(clusters, dtype=jnp.int32)
    members = jnp.sum(jnp.where(ids == cluster, sizes, 0))
    info = jnp.stack([first, members]).astype(jnp.int32)
    found = pl.pallas_call(
        best_kernel,
        out_shape=jax.ShapeDtypeStruct((1, rows), jnp.float32),
        in_specs=[SMEM, VMEM, VMEM],
        out_specs=VMEM,
        scratch_shapes=[pltpu.VMEM((width, rows), jnp.bfloat16)],
        compiler_params=pltpu.CompilerParams(vmem_limit_bytes=48 * 2**20),
        name="best_of_earlier",
    )(info, slots, keys)

    pairs = []
    for z in range(chain_len):
        for k in range(clus_len):
            pairs.append((z * clus_len + k, ((z % parts) * clus_len + k) * clus_len + z // parts))
    return lax.ppermute(found, ("chain", "clus"), pairs)


def place_kernel(run_slots, cluster_runs, dest_ref, hot_ref, kept_slots_ref, given_slots_ref):
    rows = dest_ref.shape[1]
    runs = rows // PIECE
    half = rows // 2
    clus = lax.axis_index("clus")
    upper = (lax.axis_index("chain") >= lax.axis_size("chain") // 2).astype(jnp.int32)
    code = (clus // 2 ^ clus % 2 ^ upper) * 2 + upper
    before = lax.broadcasted_iota(jnp.int32, (rows, rows), 0) < lax.broadcasted_iota(
        jnp.int32, (rows, rows), 1
    )
    dest = dest_ref[...]
    run = lax.div(dest, run_slots)
    within = lax.rem(dest, run_slots)
    run = (lax.div(run, cluster_runs) ^ code) * cluster_runs + lax.rem(run, cluster_runs)
    member = lax.broadcasted_iota(jnp.int32, (runs, rows), 0) == run
    earlier = jnp.dot(as_bf16(member), as_bf16(before), preferred_element_type=jnp.float32)
    rank = jnp.sum(jnp.where(member, earlier, 0.0), axis=0, keepdims=True).astype(jnp.int32)
    hot = as_bf16(lax.broadcasted_iota(jnp.int32, (rows, rows), 0) == run * PIECE + rank)
    hot_ref[...] = hot
    moved = lax.dot_general(
        jnp.broadcast_to(within, (TILE, rows)).astype(jnp.float32).astype(jnp.bfloat16),
        hot,
        (((1,), (1,)), ((), ())),
        preferred_element_type=jnp.float32,
    )
    line = lax.broadcasted_iota(jnp.int32, (TILE, half), 0)
    kept_slots_ref[...] = jnp.where(line == 0, moved[:, 0:half], 0.0)
    given_slots_ref[...] = jnp.where(line == 1, moved[:, half:rows], 0.0)


def send_kernel(hot_ref, slots_ref, rows_ref, kept_ref, given_ref):
    rows, width = rows_ref.shape
    half = rows // 2
    x = rows_ref[...].astype(jnp.float32)
    units = (x * lax.rsqrt(jnp.sum(x * x, axis=1, keepdims=True) + 1e-06)).astype(jnp.bfloat16)
    for low, ref in ((0, kept_ref), (half, given_ref)):
        ref[0:half, :] = jnp.dot(
            hot_ref[low : low + half, :], units, preferred_element_type=jnp.float32
        ).astype(jnp.bfloat16)
    given_ref[half : half + TILE, :] = jnp.zeros((TILE, width), jnp.bfloat16)
    given_ref[half : half + TILE, 0:half] = slots_ref[...].astype(jnp.bfloat16)


def merge_kernel(kept_ref, slots_ref, came_ref, near_ref, far_ref):
    half, width = kept_ref.shape
    depth = half // 2
    slots = slots_ref[...] + came_ref[half : half + TILE, 0:half].astype(jnp.float32)
    for low, ref in ((0, near_ref), (depth, far_ref)):
        ref[0:depth, :] = kept_ref[low : low + depth, :]
        ref[depth:half, :] = came_ref[low : low + depth, :]
        ref[half : half + TILE, :] = jnp.zeros((TILE, width), jnp.bfloat16)
        ref[half : half + TILE, 0:depth] = slots[:, low : low + depth].astype(jnp.bfloat16)


def home_chain():
    return lax.axis_size("chain") // 2 - 1 + lax.axis_index("clus") % 2


def stage_kernel(run_slots, height, count, old, new, last, *rest):
    first = old == 0
    count_ref, rest = (rest[0], rest[1:]) if first or last else (None, rest)
    refs = []
    for ref in rest[:count]:
        refs += [ref.at[pl.ds(low, height)] for low in range(0, ref.shape[0], height)]
    rest = rest[count:]
    old_states, rest = rest[: 2 * old], rest[2 * old :]
    if last:
        chunk_refs = rest[: -1 - 2 * (old + new)]
        states, found_ref = rest[len(chunk_refs) : -1], rest[-1]
    else:
        states = rest[: 2 * (old + new)]
    rows = refs[0].shape[0] - TILE
    depth = rows // 2
    runs = depth // PIECE
    is_home = lax.axis_index("chain") == home_chain()

    def halves(value):
        best = value[:, 0:LANES]
        for low in range(LANES, value.shape[1], LANES):
            best = jnp.maximum(best, value[:, low : low + LANES])
        return best

    if first:
        members = count_ref[lax.axis_index("clus")].astype(jnp.float32)
        rest[-1][...] = jnp.full_like(rest[-1], members)

    @pl.when(is_home)
    def _():
        for index in range(old):
            states[2 * index][...] = old_states[2 * index][...]
            states[2 * index + 1][...] = old_states[2 * index + 1][...]
        diagonal = lax.broadcasted_iota(jnp.int32, (rows, rows), 0) == lax.broadcasted_iota(
            jnp.int32, (rows, rows), 1
        )
        run_of = lax.broadcasted_iota(jnp.int32, (1, depth), 1) // PIECE
        for index in range(old, old + new):
            slots = refs[index][rows : rows + TILE, 0:depth].astype(jnp.float32)
            start = (run_of * run_slots).astype(jnp.float32)
            line = jnp.concatenate([slots[0:1] + start, slots[1:2] + start], axis=1)
            column = jnp.sum(jnp.where(diagonal, line, 0.0), axis=1, keepdims=True)
            states[2 * index][...] = jnp.broadcast_to(column, (rows, LANES))
            block = refs[index][0:rows, :]
            best = jnp.full((8, rows), -1.0, jnp.float32)
            for other in range(index + 1):
                scores = lax.dot_general(
                    refs[other][0:rows, :],
                    block,
                    (((1,), (1,)), ((), ())),
                    preferred_element_type=jnp.float32,
                )
                place = states[2 * other][...]
                earlier = jnp.concatenate([place] * (rows // LANES), axis=1) < line
                kept = jnp.where(earlier, scores, -2.0)
                best = jnp.maximum(best, jnp.max(kept.reshape(rows // 8, 8, rows), axis=0))
                if other < index:
                    given = halves(jnp.where(earlier, -2.0, scores))
                    states[2 * other + 1][...] = jnp.maximum(states[2 * other + 1][...], given)
            best = jnp.max(best, axis=0, keepdims=True)
            states[2 * index + 1][...] = halves(jnp.where(diagonal, best, -2.0))

    if last:
        chunk = found_ref.shape[1]

        @pl.when(jnp.logical_not(is_home))
        def _():
            for ref in chunk_refs:
                ref[...] = jnp.zeros_like(ref)

        @pl.when(is_home)
        def _():
            members = jnp.concatenate([count_ref[0:1, :]] * (run_slots // LANES), axis=1)
            lane = lax.broadcasted_iota(jnp.int32, (run_slots, run_slots), 1)
            for run in range(runs):
                where = [
                    (index, low + run * PIECE) for index in range(old + new) for low in (0, depth)
                ]
                place, best = (
                    jnp.concatenate([states[2 * n + kind][at : at + PIECE, :] for n, at in where])
                    for kind in range(2)
                )
                best = jnp.max(best, axis=1, keepdims=True)
                place = jnp.concatenate([place] * (run_slots // LANES), axis=1)
                base = run * run_slots
                position = (lane + base).astype(jnp.float32)
                found = jnp.sum(jnp.where(place == position, best, 0.0), axis=0, keepdims=True)
                found = jnp.where(position[0:1] < members, found, 0.0)
                row, low = base // chunk, base % chunk
                found_ref[row : row + 1, low : low + run_slots] = found

        chain_len = len(chunk_refs)
        for home in (chain_len // 2 - 1, chain_len // 2):
            @pl.when(lax.axis_index("chain") == home)
            def _():
                for step, ref in enumerate(chunk_refs):
                    row = (home + step) % chain_len
                    ref[...] = jnp.where(is_home, found_ref[row : row + 1, :], 0.0)


def local_home(embeddings, dest, sizes):
    chain_len = lax.axis_size("chain")
    clus_len = lax.axis_size("clus")
    rows, width = embeddings.shape
    half = rows // 2
    run_slots = chain_len * clus_len * PIECE
    block = jax.ShapeDtypeStruct((half + TILE, width), jnp.bfloat16)
    slots = jax.ShapeDtypeStruct((TILE, half), jnp.float32)
    hot, slots, given_slots = pl.pallas_call(
        functools.partial(place_kernel, run_slots, rows // clus_len // PIECE),
        out_shape=(jax.ShapeDtypeStruct((rows, rows), jnp.bfloat16), slots, slots),
        in_specs=[VMEM],
        out_specs=(VMEM,) * 3,
        cost_estimate=pl.CostEstimate(flops=0, bytes_accessed=8 * rows * width, transcendentals=0),
        compiler_params=pltpu.CompilerParams(vmem_limit_bytes=16 * 2**20),
        name="place_rows",
    )(dest.reshape(1, rows))
    kept, given = pl.pallas_call(
        send_kernel,
        out_shape=(jax.ShapeDtypeStruct((half, width), jnp.bfloat16), block),
        in_specs=[VMEM] * 3,
        out_specs=(VMEM, VMEM),
        compiler_params=pltpu.CompilerParams(vmem_limit_bytes=16 * 2**20),
        name="send_blocks",
    )(hot, given_slots, embeddings)

    def permute(value, moves):
        pairs = [(a * clus_len + b, c * clus_len + d) for a, b, c, d in moves]
        return lax.ppermute(value, ("chain", "clus"), pairs)

    low, high, top = chain_len // 2 - 1, chain_len // 2, chain_len - 1
    swap = [(z, k, z, k ^ 1) for z in range(chain_len) for k in range(clus_len)]
    near, far = pl.pallas_call(
        merge_kernel,
        out_shape=(block, block),
        in_specs=[VMEM, VMEM, VMEM],
        out_specs=(VMEM, VMEM),
        compiler_params=pltpu.CompilerParams(vmem_limit_bytes=16 * 2**20),
        name="merge_blocks",
    )(kept, slots, permute(given, swap))

    def serving(z, across):
        return across ^ (z >= high)

    def to_home(value, moves):
        columns = range(clus_len // 2)
        pairs = [(a, 2 * x + serving(a, 0), b, 2 * x + serving(b, 0)) for a, b in moves for x in columns]
        if {a for a, _ in moves} == {b for _, b in moves}:
            taken = {pair[:2] for pair in pairs}
            everyone = [(z, k) for z in range(chain_len) for k in range(clus_len)]
            pairs += [place + place for place in everyone if place not in taken]
        return permute(value, pairs)

    def across(value):
        pairs = []
        for z in range(chain_len):
            for x in range(clus_len // 2):
                own, other = serving(z, 0), serving(z, 1)
                pairs.append((z, 2 * x + other, z, 2 * (x ^ 1) + own))
                pairs.append((z, 2 * x + own, z, 2 * x + other))
        return permute(value, pairs)

    from_far = [(0, high), (top, low)]
    from_near = [(0, low), (top, high)]
    from_middle = [(low, high), (high, low)]
    far_crossed, near_crossed = across(far), across(near)
    far_along, near_along = to_home(far, from_far), to_home(near, from_near)
    middle_along = to_home(far, from_middle)
    far_after, near_after = to_home(far_crossed, from_far), to_home(near_crossed, from_near)
    middle_after = to_home(far_crossed, from_middle)
    stages = [[near, near_crossed, near_along, far_along], [far_after, middle_along], [near_after], [middle_after]]
    blocks, states, held = [], [], 0
    state = jax.ShapeDtypeStruct((half, LANES), jnp.float32)
    chunk = jax.ShapeDtypeStruct((1, rows), jnp.float32)
    for number, arrived in enumerate(stages):
        first, last = number == 0, number == len(stages) - 1
        old, blocks = held, blocks + arrived
        held = sum(value.shape[0] for value in blocks) // (half + TILE)
        outs = (chunk,) * chain_len if last else (state,) * (2 * held)
        outs += (jax.ShapeDtypeStruct((TILE, LANES), jnp.float32),) * first
        scratch = [pltpu.VMEM(state.shape, state.dtype)] * (2 * held)
        scratch.append(pltpu.VMEM((chain_len, rows), jnp.float32))
        count = [sizes] if first else [members] if last else []
        states = pl.pallas_call(
            functools.partial(stage_kernel, run_slots, half + TILE, len(blocks), old, held - old, last),
            out_shape=outs,
            in_specs=[SMEM] * first + [VMEM] * (last + len(blocks) + len(states)),
            out_specs=(VMEM,) * len(outs),
            scratch_shapes=scratch * last,
            compiler_params=pltpu.CompilerParams(vmem_limit_bytes=32 * 2**20),
            name="multiply_last" if last else "multiply_arrived",
        )(*count, *blocks, *states)
        if first:
            *states, members = states
    found = states[0]
    for step in range(1, chain_len):
        moves = []
        for k in range(clus_len):
            pair = (low + k % 2, (low + k % 2 + step) % chain_len)
            for z in range(chain_len):
                moves.append((z, k, pair[1 - pair.index(z)] if z in pair else z, k))
        found = found + permute(states[step], moves)
    return found


def solution(mesh):
    return jax.shard_map(
        local_home if mesh.shape["chain"] == mesh.shape["clus"] == 4 else local_plane,
        mesh=mesh,
        in_specs=(
            P(("groups", "chain", "clus"), None),
            P(("groups", "chain", "clus")),
            P("groups"),
        ),
        out_specs=P(("groups", "clus"), "chain"),
        check_vma=False,
    )
```

```python
import functools

import jax
import jax.numpy as jnp
from jax import lax
from jax.experimental import pallas as pl
from jax.experimental.pallas import tpu as pltpu
from jax.sharding import PartitionSpec as P

TILE = 8
LANES = 128
PIECE = 16
VMEM = pl.BlockSpec(memory_space=pltpu.VMEM)
SMEM = pl.BlockSpec(memory_space=pltpu.SMEM)


def as_bf16(mask):
    return mask.astype(jnp.float32).astype(jnp.bfloat16)


def sort_kernel(run_slots, dest_ref, rows_ref, units_ref, slots_ref):
    rows = rows_ref.shape[0]
    runs = rows // PIECE
    dest = dest_ref[...]
    run = dest // run_slots
    within = dest % run_slots
    member = lax.broadcasted_iota(jnp.int32, (runs, rows), 0) == run
    before = lax.broadcasted_iota(jnp.int32, (rows, rows), 0) < lax.broadcasted_iota(
        jnp.int32, (rows, rows), 1
    )
    earlier = jnp.dot(
        member.astype(jnp.float32).astype(jnp.bfloat16),
        before.astype(jnp.float32).astype(jnp.bfloat16),
        preferred_element_type=jnp.float32,
    )
    rank = jnp.sum(jnp.where(member, earlier, 0.0), axis=0, keepdims=True).astype(jnp.int32)
    placed = run * PIECE + rank
    hot = (lax.broadcasted_iota(jnp.int32, (rows, rows), 0) == placed).astype(jnp.float32)
    hot = hot.astype(jnp.bfloat16)
    x = rows_ref[...].astype(jnp.float32)
    units = (x * lax.rsqrt(jnp.sum(x * x, axis=1, keepdims=True) + 1e-06)).astype(jnp.bfloat16)
    units_ref[...] = jnp.dot(hot, units, preferred_element_type=jnp.float32).astype(jnp.bfloat16)
    halves = jnp.concatenate(
        [jnp.broadcast_to(within // 256, (8, rows)), jnp.broadcast_to(within % 256, (8, rows))], axis=0
    )
    moved = lax.dot_general(
        halves.astype(jnp.float32).astype(jnp.bfloat16),
        hot,
        (((1,), (1,)), ((), ())),
        preferred_element_type=jnp.float32,
    )
    slots_ref[...] = (moved[0:1, :] * 256.0 + moved[8:9, :]).astype(jnp.int32)


def best_kernel(info_ref, slots_ref, keys_ref, out_ref, query_ref):
    shards, depth, width = keys_ref.shape
    queries = out_ref.shape[1]
    run_slots = shards * PIECE
    unit = min(run_slots, queries)
    first = info_ref[0]
    members = info_ref[1]
    first_run = first // run_slots

    def run_rows(run):
        start = pl.multiple_of(run * PIECE, PIECE)
        return keys_ref[:, pl.ds(start, PIECE), :].reshape(run_slots, width)

    def run_positions(run):
        start = pl.multiple_of(run * PIECE, PIECE)
        tile = slots_ref[pl.ds(start, PIECE), :]
        wide = jnp.broadcast_to(tile[None], (shards, PIECE, shards)).reshape(run_slots, shards)
        lane = lax.broadcasted_iota(jnp.int32, (run_slots, shards), 1)
        row = lax.broadcasted_iota(jnp.int32, (run_slots, shards), 0)
        picked = jnp.sum(jnp.where(lane == row // PIECE, wide, 0), axis=1, keepdims=True)
        return picked + run * run_slots

    for index in range(queries // unit):
        run = first_run + index
        lanes = lax.broadcasted_iota(jnp.int32, (run_slots, unit), 1) + (first + index * unit)
        hot = (run_positions(run) == lanes).astype(jnp.float32).astype(jnp.bfloat16)
        query_ref[:, index * unit : (index + 1) * unit] = lax.dot_general(
            run_rows(run), hot, (((0,), (0,)), ((), ())), preferred_element_type=jnp.float32
        ).astype(jnp.bfloat16)

    def fold(scores):
        return jnp.max(scores.reshape(run_slots // 8, 8, queries), axis=0)

    def step(run, running):
        scores = jnp.dot(run_rows(run), query_ref[...], preferred_element_type=jnp.float32)
        return jnp.maximum(running, fold(scores))

    running = lax.fori_loop(0, first_run, step, jnp.full((8, queries), -1.0, jnp.float32))
    position = first + lax.broadcasted_iota(jnp.int32, (1, queries), 1)
    for index in range(queries // unit):
        run = first_run + index
        scores = jnp.dot(run_rows(run), query_ref[...], preferred_element_type=jnp.float32)
        masked = jnp.where(run_positions(run) < position, scores, -2.0)
        running = jnp.maximum(running, fold(masked))
    found = jnp.max(running, axis=0, keepdims=True)
    out_ref[...] = jnp.where(position < members, found, 0.0)


def local_plane(embeddings, dest, sizes):
    chain_len = lax.axis_size("chain")
    clus_len = lax.axis_size("clus")
    shards = chain_len * clus_len
    rows, width = embeddings.shape
    clusters = sizes.shape[0]
    parts = chain_len // clusters
    run_slots = shards * PIECE
    depth = rows // chain_len
    my_chain = lax.axis_index("chain")
    my_clus = lax.axis_index("clus")
    cluster = my_chain // parts
    part = my_chain % parts

    units, slots = pl.pallas_call(
        functools.partial(sort_kernel, run_slots),
        out_shape=(
            jax.ShapeDtypeStruct((rows, width), jnp.bfloat16),
            jax.ShapeDtypeStruct((1, rows), jnp.int32),
        ),
        in_specs=[VMEM, VMEM],
        out_specs=(VMEM, VMEM),
        compiler_params=pltpu.CompilerParams(vmem_limit_bytes=32 * 2**20),
        name="sort_units",
    )(dest.reshape(1, rows), embeddings)

    slots = lax.all_gather(slots, ("chain", "clus"), axis=0, tiled=True)
    slots = slots.reshape(chain_len, clus_len, clusters, -1, PIECE)
    slots = lax.dynamic_index_in_dim(slots, cluster, 2, keepdims=False)
    slots = slots.transpose(2, 3, 1, 0).reshape(-1, shards)

    got = lax.all_to_all(units, "chain", split_axis=0, concat_axis=0, tiled=True)
    keys = lax.all_gather(got, "clus", axis=0, tiled=True).reshape(shards, depth, width)
    if parts > 1:
        pieces = []
        for wanted in range(parts):
            block = keys
            for other in range(parts):
                if other != wanted:
                    pairs = [(c * parts + wanted, c * parts + other) for c in range(clusters)]
                    came = lax.ppermute(keys, "chain", pairs)
                    block = jnp.where(part == other, came, block)
            pieces.append(block)
        keys = jnp.concatenate(pieces, axis=1)

    first = (part * clus_len + my_clus) * rows
    ids = jnp.arange(clusters, dtype=jnp.int32)
    members = jnp.sum(jnp.where(ids == cluster, sizes, 0))
    info = jnp.stack([first, members]).astype(jnp.int32)
    found = pl.pallas_call(
        best_kernel,
        out_shape=jax.ShapeDtypeStruct((1, rows), jnp.float32),
        in_specs=[SMEM, VMEM, VMEM],
        out_specs=VMEM,
        scratch_shapes=[pltpu.VMEM((width, rows), jnp.bfloat16)],
        compiler_params=pltpu.CompilerParams(vmem_limit_bytes=48 * 2**20),
        name="best_of_earlier",
    )(info, slots, keys)

    pairs = []
    for z in range(chain_len):
        for k in range(clus_len):
            pairs.append((z * clus_len + k, ((z % parts) * clus_len + k) * clus_len + z // parts))
    return lax.ppermute(found, ("chain", "clus"), pairs)


def place_kernel(run_slots, cluster_runs, dest_ref, hot_ref, kept_slots_ref, given_slots_ref):
    rows = dest_ref.shape[1]
    runs = rows // PIECE
    half = rows // 2
    clus = lax.axis_index("clus")
    upper = (lax.axis_index("chain") >= lax.axis_size("chain") // 2).astype(jnp.int32)
    code = (clus // 2 ^ clus % 2 ^ upper) * 2 + upper
    before = lax.broadcasted_iota(jnp.int32, (rows, rows), 0) < lax.broadcasted_iota(
        jnp.int32, (rows, rows), 1
    )
    dest = dest_ref[...]
    run = lax.div(dest, run_slots)
    within = lax.rem(dest, run_slots)
    run = (lax.div(run, cluster_runs) ^ code) * cluster_runs + lax.rem(run, cluster_runs)
    member = lax.broadcasted_iota(jnp.int32, (runs, rows), 0) == run
    earlier = jnp.dot(as_bf16(member), as_bf16(before), preferred_element_type=jnp.float32)
    rank = jnp.sum(jnp.where(member, earlier, 0.0), axis=0, keepdims=True).astype(jnp.int32)
    hot = as_bf16(lax.broadcasted_iota(jnp.int32, (rows, rows), 0) == run * PIECE + rank)
    hot_ref[...] = hot
    moved = lax.dot_general(
        jnp.broadcast_to(within, (TILE, rows)).astype(jnp.float32).astype(jnp.bfloat16),
        hot,
        (((1,), (1,)), ((), ())),
        preferred_element_type=jnp.float32,
    )
    line = lax.broadcasted_iota(jnp.int32, (TILE, half), 0)
    kept_slots_ref[...] = jnp.where(line == 0, moved[:, 0:half], 0.0)
    given_slots_ref[...] = jnp.where(line == 1, moved[:, half:rows], 0.0)


def send_kernel(hot_ref, slots_ref, rows_ref, kept_ref, given_ref):
    rows, width = rows_ref.shape
    half = rows // 2
    x = rows_ref[...].astype(jnp.float32)
    units = (x * lax.rsqrt(jnp.sum(x * x, axis=1, keepdims=True) + 1e-06)).astype(jnp.bfloat16)
    for low, ref in ((0, kept_ref), (half, given_ref)):
        ref[0:half, :] = jnp.dot(
            hot_ref[low : low + half, :], units, preferred_element_type=jnp.float32
        ).astype(jnp.bfloat16)
    given_ref[half : half + TILE, :] = jnp.zeros((TILE, width), jnp.bfloat16)
    given_ref[half : half + TILE, 0:half] = slots_ref[...].astype(jnp.bfloat16)


def merge_kernel(kept_ref, slots_ref, came_ref, near_ref, far_ref):
    half, width = kept_ref.shape
    depth = half // 2
    slots = slots_ref[...] + came_ref[half : half + TILE, 0:half].astype(jnp.float32)
    for low, ref in ((0, near_ref), (depth, far_ref)):
        ref[0:depth, :] = kept_ref[low : low + depth, :]
        ref[depth:half, :] = came_ref[low : low + depth, :]
        ref[half : half + TILE, :] = jnp.zeros((TILE, width), jnp.bfloat16)
        ref[half : half + TILE, 0:depth] = slots[:, low : low + depth].astype(jnp.bfloat16)


def home_chain():
    return lax.axis_size("chain") // 2 - 1 + lax.axis_index("clus") % 2


def stage_kernel(run_slots, height, count, old, new, last, *rest):
    first = old == 0
    count_ref, rest = (rest[0], rest[1:]) if first or last else (None, rest)
    refs = []
    for ref in rest[:count]:
        refs += [ref.at[pl.ds(low, height)] for low in range(0, ref.shape[0], height)]
    rest = rest[count:]
    old_states, rest = rest[: 2 * old], rest[2 * old :]
    if last:
        chunk_refs = rest[: -1 - 2 * (old + new)]
        states, found_ref = rest[len(chunk_refs) : -1], rest[-1]
    else:
        states = rest[: 2 * (old + new)]
    rows = refs[0].shape[0] - TILE
    depth = rows // 2
    runs = depth // PIECE
    is_home = lax.axis_index("chain") == home_chain()

    def halves(value):
        best = value[:, 0:LANES]
        for low in range(LANES, value.shape[1], LANES):
            best = jnp.maximum(best, value[:, low : low + LANES])
        return best

    if first:
        members = count_ref[lax.axis_index("clus")].astype(jnp.float32)
        rest[-1][...] = jnp.full_like(rest[-1], members)

    @pl.when(is_home)
    def _():
        for index in range(old):
            states[2 * index][...] = old_states[2 * index][...]
            states[2 * index + 1][...] = old_states[2 * index + 1][...]
        diagonal = lax.broadcasted_iota(jnp.int32, (rows, rows), 0) == lax.broadcasted_iota(
            jnp.int32, (rows, rows), 1
        )
        run_of = lax.broadcasted_iota(jnp.int32, (1, depth), 1) // PIECE
        for index in range(old, old + new):
            slots = refs[index][rows : rows + TILE, 0:depth].astype(jnp.float32)
            start = (run_of * run_slots).astype(jnp.float32)
            line = jnp.concatenate([slots[0:1] + start, slots[1:2] + start], axis=1)
            column = jnp.sum(jnp.where(diagonal, line, 0.0), axis=1, keepdims=True)
            states[2 * index][...] = jnp.broadcast_to(column, (rows, LANES))
            block = refs[index][0:rows, :]
            best = jnp.full((8, rows), -1.0, jnp.float32)
            for other in range(index + 1):
                scores = lax.dot_general(
                    refs[other][0:rows, :],
                    block,
                    (((1,), (1,)), ((), ())),
                    preferred_element_type=jnp.float32,
                )
                place = states[2 * other][...]
                earlier = jnp.concatenate([place] * (rows // LANES), axis=1) < line
                kept = jnp.where(earlier, scores, -2.0)
                best = jnp.maximum(best, jnp.max(kept.reshape(rows // 8, 8, rows), axis=0))
                if other < index:
                    given = halves(jnp.where(earlier, -2.0, scores))
                    states[2 * other + 1][...] = jnp.maximum(states[2 * other + 1][...], given)
            best = jnp.max(best, axis=0, keepdims=True)
            states[2 * index + 1][...] = halves(jnp.where(diagonal, best, -2.0))

    if last:
        chunk = found_ref.shape[1]

        @pl.when(jnp.logical_not(is_home))
        def _():
            for ref in chunk_refs:
                ref[...] = jnp.zeros_like(ref)

        @pl.when(is_home)
        def _():
            members = jnp.concatenate([count_ref[0:1, :]] * (run_slots // LANES), axis=1)
            lane = lax.broadcasted_iota(jnp.int32, (run_slots, run_slots), 1)
            for run in range(runs):
                where = [
                    (index, low + run * PIECE) for index in range(old + new) for low in (0, depth)
                ]
                place, best = (
                    jnp.concatenate([states[2 * n + kind][at : at + PIECE, :] for n, at in where])
                    for kind in range(2)
                )
                best = jnp.max(best, axis=1, keepdims=True)
                place = jnp.concatenate([place] * (run_slots // LANES), axis=1)
                base = run * run_slots
                position = (lane + base).astype(jnp.float32)
                found = jnp.sum(jnp.where(place == position, best, 0.0), axis=0, keepdims=True)
                found = jnp.where(position[0:1] < members, found, 0.0)
                row, low = base // chunk, base % chunk
                found_ref[row : row + 1, low : low + run_slots] = found

        chain_len = len(chunk_refs)
        for home in (chain_len // 2 - 1, chain_len // 2):
            @pl.when(lax.axis_index("chain") == home)
            def _():
                for step, ref in enumerate(chunk_refs):
                    row = (home + step) % chain_len
                    ref[...] = jnp.where(is_home, found_ref[row : row + 1, :], 0.0)


def local_home(embeddings, dest, sizes):
    chain_len = lax.axis_size("chain")
    clus_len = lax.axis_size("clus")
    rows, width = embeddings.shape
    half = rows // 2
    run_slots = chain_len * clus_len * PIECE
    block = jax.ShapeDtypeStruct((half + TILE, width), jnp.bfloat16)
    slots = jax.ShapeDtypeStruct((TILE, half), jnp.float32)
    hot, slots, given_slots = pl.pallas_call(
        functools.partial(place_kernel, run_slots, rows // clus_len // PIECE),
        out_shape=(jax.ShapeDtypeStruct((rows, rows), jnp.bfloat16), slots, slots),
        in_specs=[VMEM],
        out_specs=(VMEM,) * 3,
        cost_estimate=pl.CostEstimate(flops=0, bytes_accessed=8 * rows * width, transcendentals=0),
        compiler_params=pltpu.CompilerParams(vmem_limit_bytes=16 * 2**20),
        name="place_rows",
    )(dest.reshape(1, rows))
    kept, given = pl.pallas_call(
        send_kernel,
        out_shape=(jax.ShapeDtypeStruct((half, width), jnp.bfloat16), block),
        in_specs=[VMEM] * 3,
        out_specs=(VMEM, VMEM),
        compiler_params=pltpu.CompilerParams(vmem_limit_bytes=16 * 2**20),
        name="send_blocks",
    )(hot, given_slots, embeddings)

    def permute(value, moves):
        pairs = [(a * clus_len + b, c * clus_len + d) for a, b, c, d in moves]
        return lax.ppermute(value, ("chain", "clus"), pairs)

    low, high, top = chain_len // 2 - 1, chain_len // 2, chain_len - 1
    swap = [(z, k, z, k ^ 1) for z in range(chain_len) for k in range(clus_len)]
    near, far = pl.pallas_call(
        merge_kernel,
        out_shape=(block, block),
        in_specs=[VMEM, VMEM, VMEM],
        out_specs=(VMEM, VMEM),
        compiler_params=pltpu.CompilerParams(vmem_limit_bytes=16 * 2**20),
        name="merge_blocks",
    )(kept, slots, permute(given, swap))

    def serving(z, across):
        return across ^ (z >= high)

    def to_home(value, moves):
        columns = range(clus_len // 2)
        pairs = [(a, 2 * x + serving(a, 0), b, 2 * x + serving(b, 0)) for a, b in moves for x in columns]
        if {a for a, _ in moves} == {b for _, b in moves}:
            taken = {pair[:2] for pair in pairs}
            everyone = [(z, k) for z in range(chain_len) for k in range(clus_len)]
            pairs += [place + place for place in everyone if place not in taken]
        return permute(value, pairs)

    def across(value):
        pairs = []
        for z in range(chain_len):
            for x in range(clus_len // 2):
                own, other = serving(z, 0), serving(z, 1)
                pairs.append((z, 2 * x + other, z, 2 * (x ^ 1) + own))
                pairs.append((z, 2 * x + own, z, 2 * x + other))
        return permute(value, pairs)

    from_far = [(0, high), (top, low)]
    from_near = [(0, low), (top, high)]
    from_middle = [(low, high), (high, low)]
    far_crossed, near_crossed = across(far), across(near)
    far_along, near_along = to_home(far, from_far), to_home(near, from_near)
    middle_along = to_home(far, from_middle)
    far_after, near_after = to_home(far_crossed, from_far), to_home(near_crossed, from_near)
    middle_after = to_home(far_crossed, from_middle)
    stages = [[near, near_crossed, near_along, far_along], [far_after, middle_along], [near_after], [middle_after]]
    blocks, states, held = [], [], 0
    state = jax.ShapeDtypeStruct((half, LANES), jnp.float32)
    chunk = jax.ShapeDtypeStruct((1, rows), jnp.float32)
    for number, arrived in enumerate(stages):
        first, last = number == 0, number == len(stages) - 1
        old, blocks = held, blocks + arrived
        held = sum(value.shape[0] for value in blocks) // (half + TILE)
        outs = (chunk,) * chain_len if last else (state,) * (2 * held)
        outs += (jax.ShapeDtypeStruct((TILE, LANES), jnp.float32),) * first
        scratch = [pltpu.VMEM(state.shape, state.dtype)] * (2 * held)
        scratch.append(pltpu.VMEM((chain_len, rows), jnp.float32))
        count = [sizes] if first else [members] if last else []
        states = pl.pallas_call(
            functools.partial(stage_kernel, run_slots, half + TILE, len(blocks), old, held - old, last),
            out_shape=outs,
            in_specs=[SMEM] * first + [VMEM] * (last + len(blocks) + len(states)),
            out_specs=(VMEM,) * len(outs),
            scratch_shapes=scratch * last,
            compiler_params=pltpu.CompilerParams(vmem_limit_bytes=32 * 2**20),
            name="multiply_last" if last else "multiply_arrived",
        )(*count, *blocks, *states)
        if first:
            *states, members = states
    found = states[0]
    for step in range(1, chain_len):
        homes = [(low + k % 2, k) for k in range(clus_len)]
        moves = [(home, k, (home + step) % chain_len, k) for home, k in homes]
        found = found + permute(states[step], moves)
    return found


def solution(mesh):
    return jax.shard_map(
        local_home if mesh.shape["chain"] == mesh.shape["clus"] == 4 else local_plane,
        mesh=mesh,
        in_specs=(
            P(("groups", "chain", "clus"), None),
            P(("groups", "chain", "clus")),
            P("groups"),
        ),
        out_specs=P(("groups", "clus"), "chain"),
        check_vma=False,
    )
```

```python
import functools

import jax
import jax.numpy as jnp
from jax import lax
from jax.experimental import pallas as pl
from jax.experimental.pallas import tpu as pltpu
from jax.sharding import PartitionSpec as P

TILE = 8
LANES = 128
PIECE = 16
VMEM = pl.BlockSpec(memory_space=pltpu.VMEM)
SMEM = pl.BlockSpec(memory_space=pltpu.SMEM)


def as_bf16(mask):
    return mask.astype(jnp.float32).astype(jnp.bfloat16)


def sort_kernel(run_slots, dest_ref, rows_ref, units_ref, slots_ref):
    rows = rows_ref.shape[0]
    runs = rows // PIECE
    dest = dest_ref[...]
    run = dest // run_slots
    within = dest % run_slots
    member = lax.broadcasted_iota(jnp.int32, (runs, rows), 0) == run
    before = lax.broadcasted_iota(jnp.int32, (rows, rows), 0) < lax.broadcasted_iota(
        jnp.int32, (rows, rows), 1
    )
    earlier = jnp.dot(
        member.astype(jnp.float32).astype(jnp.bfloat16),
        before.astype(jnp.float32).astype(jnp.bfloat16),
        preferred_element_type=jnp.float32,
    )
    rank = jnp.sum(jnp.where(member, earlier, 0.0), axis=0, keepdims=True).astype(jnp.int32)
    placed = run * PIECE + rank
    hot = (lax.broadcasted_iota(jnp.int32, (rows, rows), 0) == placed).astype(jnp.float32)
    hot = hot.astype(jnp.bfloat16)
    x = rows_ref[...].astype(jnp.float32)
    units = (x * lax.rsqrt(jnp.sum(x * x, axis=1, keepdims=True) + 1e-06)).astype(jnp.bfloat16)
    units_ref[...] = jnp.dot(hot, units, preferred_element_type=jnp.float32).astype(jnp.bfloat16)
    halves = jnp.concatenate(
        [jnp.broadcast_to(within // 256, (8, rows)), jnp.broadcast_to(within % 256, (8, rows))], axis=0
    )
    moved = lax.dot_general(
        halves.astype(jnp.float32).astype(jnp.bfloat16),
        hot,
        (((1,), (1,)), ((), ())),
        preferred_element_type=jnp.float32,
    )
    slots_ref[...] = (moved[0:1, :] * 256.0 + moved[8:9, :]).astype(jnp.int32)


def best_kernel(info_ref, slots_ref, keys_ref, out_ref, query_ref):
    shards, depth, width = keys_ref.shape
    queries = out_ref.shape[1]
    run_slots = shards * PIECE
    unit = min(run_slots, queries)
    first = info_ref[0]
    members = info_ref[1]
    first_run = first // run_slots

    def run_rows(run):
        start = pl.multiple_of(run * PIECE, PIECE)
        return keys_ref[:, pl.ds(start, PIECE), :].reshape(run_slots, width)

    def run_positions(run):
        start = pl.multiple_of(run * PIECE, PIECE)
        tile = slots_ref[pl.ds(start, PIECE), :]
        wide = jnp.broadcast_to(tile[None], (shards, PIECE, shards)).reshape(run_slots, shards)
        lane = lax.broadcasted_iota(jnp.int32, (run_slots, shards), 1)
        row = lax.broadcasted_iota(jnp.int32, (run_slots, shards), 0)
        picked = jnp.sum(jnp.where(lane == row // PIECE, wide, 0), axis=1, keepdims=True)
        return picked + run * run_slots

    for index in range(queries // unit):
        run = first_run + index
        lanes = lax.broadcasted_iota(jnp.int32, (run_slots, unit), 1) + (first + index * unit)
        hot = (run_positions(run) == lanes).astype(jnp.float32).astype(jnp.bfloat16)
        query_ref[:, index * unit : (index + 1) * unit] = lax.dot_general(
            run_rows(run), hot, (((0,), (0,)), ((), ())), preferred_element_type=jnp.float32
        ).astype(jnp.bfloat16)

    def fold(scores):
        return jnp.max(scores.reshape(run_slots // 8, 8, queries), axis=0)

    def step(run, running):
        scores = jnp.dot(run_rows(run), query_ref[...], preferred_element_type=jnp.float32)
        return jnp.maximum(running, fold(scores))

    running = lax.fori_loop(0, first_run, step, jnp.full((8, queries), -1.0, jnp.float32))
    position = first + lax.broadcasted_iota(jnp.int32, (1, queries), 1)
    for index in range(queries // unit):
        run = first_run + index
        scores = jnp.dot(run_rows(run), query_ref[...], preferred_element_type=jnp.float32)
        masked = jnp.where(run_positions(run) < position, scores, -2.0)
        running = jnp.maximum(running, fold(masked))
    found = jnp.max(running, axis=0, keepdims=True)
    out_ref[...] = jnp.where(position < members, found, 0.0)


def local_plane(embeddings, dest, sizes):
    chain_len = lax.axis_size("chain")
    clus_len = lax.axis_size("clus")
    shards = chain_len * clus_len
    rows, width = embeddings.shape
    clusters = sizes.shape[0]
    parts = chain_len // clusters
    run_slots = shards * PIECE
    depth = rows // chain_len
    my_chain = lax.axis_index("chain")
    my_clus = lax.axis_index("clus")
    cluster = my_chain // parts
    part = my_chain % parts

    units, slots = pl.pallas_call(
        functools.partial(sort_kernel, run_slots),
        out_shape=(
            jax.ShapeDtypeStruct((rows, width), jnp.bfloat16),
            jax.ShapeDtypeStruct((1, rows), jnp.int32),
        ),
        in_specs=[VMEM, VMEM],
        out_specs=(VMEM, VMEM),
        compiler_params=pltpu.CompilerParams(vmem_limit_bytes=32 * 2**20),
        name="sort_units",
    )(dest.reshape(1, rows), embeddings)

    slots = lax.all_gather(slots, ("chain", "clus"), axis=0, tiled=True)
    slots = slots.reshape(chain_len, clus_len, clusters, -1, PIECE)
    slots = lax.dynamic_index_in_dim(slots, cluster, 2, keepdims=False)
    slots = slots.transpose(2, 3, 1, 0).reshape(-1, shards)

    got = lax.all_to_all(units, "chain", split_axis=0, concat_axis=0, tiled=True)
    keys = lax.all_gather(got, "clus", axis=0, tiled=True).reshape(shards, depth, width)
    if parts > 1:
        pieces = []
        for wanted in range(parts):
            block = keys
            for other in range(parts):
                if other != wanted:
                    pairs = [(c * parts + wanted, c * parts + other) for c in range(clusters)]
                    came = lax.ppermute(keys, "chain", pairs)
                    block = jnp.where(part == other, came, block)
            pieces.append(block)
        keys = jnp.concatenate(pieces, axis=1)

    first = (part * clus_len + my_clus) * rows
    ids = jnp.arange(clusters, dtype=jnp.int32)
    members = jnp.sum(jnp.where(ids == cluster, sizes, 0))
    info = jnp.stack([first, members]).astype(jnp.int32)
    found = pl.pallas_call(
        best_kernel,
        out_shape=jax.ShapeDtypeStruct((1, rows), jnp.float32),
        in_specs=[SMEM, VMEM, VMEM],
        out_specs=VMEM,
        scratch_shapes=[pltpu.VMEM((width, rows), jnp.bfloat16)],
        compiler_params=pltpu.CompilerParams(vmem_limit_bytes=48 * 2**20),
        name="best_of_earlier",
    )(info, slots, keys)

    pairs = []
    for z in range(chain_len):
        for k in range(clus_len):
            pairs.append((z * clus_len + k, ((z % parts) * clus_len + k) * clus_len + z // parts))
    return lax.ppermute(found, ("chain", "clus"), pairs)


def place_kernel(run_slots, cluster_runs, dest_ref, hot_ref, slots_ref):
    rows = dest_ref.shape[1]
    runs = rows // PIECE
    upper = (lax.axis_index("chain") >= lax.axis_size("chain") // 2).astype(jnp.int32)
    code = lax.axis_index("clus") // 2 * 2 + upper
    before = lax.broadcasted_iota(jnp.int32, (rows, rows), 0) < lax.broadcasted_iota(
        jnp.int32, (rows, rows), 1
    )
    dest = dest_ref[...]
    run = lax.div(dest, run_slots)
    within = lax.rem(dest, run_slots)
    run = (lax.div(run, cluster_runs) ^ code) * cluster_runs + lax.rem(run, cluster_runs)
    member = lax.broadcasted_iota(jnp.int32, (runs, rows), 0) == run
    earlier = jnp.dot(as_bf16(member), as_bf16(before), preferred_element_type=jnp.float32)
    rank = jnp.sum(jnp.where(member, earlier, 0.0), axis=0, keepdims=True).astype(jnp.int32)
    hot = as_bf16(lax.broadcasted_iota(jnp.int32, (rows, rows), 0) == run * PIECE + rank)
    hot_ref[...] = hot
    slots_ref[...] = lax.dot_general(
        jnp.broadcast_to(within, (TILE, rows)).astype(jnp.float32).astype(jnp.bfloat16),
        hot,
        (((1,), (1,)), ((), ())),
        preferred_element_type=jnp.float32,
    )


def send_kernel(hot_ref, slots_ref, rows_ref, *block_refs):
    rows, width = rows_ref.shape
    depth = rows // len(block_refs)
    x = rows_ref[...].astype(jnp.float32)
    units = (x * lax.rsqrt(jnp.sum(x * x, axis=1, keepdims=True) + 1e-06)).astype(jnp.bfloat16)
    for index, ref in enumerate(block_refs):
        low = index * depth
        ref[0:depth, :] = jnp.dot(
            hot_ref[low : low + depth, :], units, preferred_element_type=jnp.float32
        ).astype(jnp.bfloat16)
        ref[depth : depth + TILE, :] = jnp.zeros((TILE, width), jnp.bfloat16)
        ref[depth : depth + TILE, 0:depth] = slots_ref[:, low : low + depth].astype(jnp.bfloat16)


def merge_kernel(mine_ref, came_ref, out_ref):
    depth = mine_ref.shape[0] - TILE
    out_ref[0:depth, :] = mine_ref[0:depth, :]
    out_ref[depth : 2 * depth, :] = came_ref[0:depth, :]
    line = lax.broadcasted_iota(jnp.int32, (TILE, out_ref.shape[1]), 0)
    mine, came = (ref[depth : depth + TILE, :].astype(jnp.float32) for ref in (mine_ref, came_ref))
    out_ref[2 * depth :, :] = jnp.where(line == 0, mine, came).astype(jnp.bfloat16)


def helper_kernel(count, *refs):
    out_ref = refs[-1]
    depth = refs[0].shape[0] - TILE
    for index, ref in enumerate(refs[:count]):
        out_ref[index * depth : (index + 1) * depth, :] = ref[0:depth, :]
        low = count * depth + index * TILE
        out_ref[low : low + TILE, :] = ref[depth : depth + TILE, :]


def home_chain():
    return lax.axis_size("chain") // 2 - 1 + lax.axis_index("clus") % 2


def stage_kernel(run_slots, height, count, old, new, last, *rest):
    first = old == 0
    count_ref, rest = (rest[0], rest[1:]) if first or last else (None, rest)
    depth = (height - TILE) // 2
    parts = []
    for ref in rest[:count]:
        size = ref.shape[0] // depth
        if ref.shape[0] == height:
            parts += [(ref, 0, 2 * depth, TILE, 0), (ref, depth, 2 * depth, TILE, 1)]
        elif size == 1:
            parts.append((ref, 0, depth, TILE, 0))
        else:
            for at in range(size):
                tile = size * depth + at // 2 * 2 * TILE
                parts.append((ref, at * depth, tile, 2 * TILE, at % 2 * TILE))
    refs = [parts[at : at + 2] for at in range(0, len(parts), 2)]
    rest = rest[count:]
    old_states, rest = rest[: 2 * old], rest[2 * old :]
    if last:
        chunk_refs = rest[: -1 - 2 * (old + new)]
        states, found_ref = rest[len(chunk_refs) : -1], rest[-1]
    else:
        states = rest[: 2 * (old + new)]
    rows = 2 * depth
    runs = depth // PIECE
    is_home = lax.axis_index("chain") == home_chain()

    def halves(value):
        best = value[:, 0:LANES]
        for low in range(LANES, value.shape[1], LANES):
            best = jnp.maximum(best, value[:, low : low + LANES])
        return best

    if first:
        members = count_ref[lax.axis_index("clus")].astype(jnp.float32)
        rest[-1][...] = jnp.full_like(rest[-1], members)

    def load(index):
        (ref, low, *_), (other, _, *_) = refs[index]
        if ref is other:
            return ref[low : low + rows, :]
        return jnp.concatenate([part[0][0:depth, :] for part in refs[index]], axis=0)

    @pl.when(is_home)
    def _():
        for index in range(old):
            states[2 * index][...] = old_states[2 * index][...]
            states[2 * index + 1][...] = old_states[2 * index + 1][...]
        diagonal = lax.broadcasted_iota(jnp.int32, (rows, rows), 0) == lax.broadcasted_iota(
            jnp.int32, (rows, rows), 1
        )
        run_of = lax.broadcasted_iota(jnp.int32, (1, depth), 1) // PIECE
        for index in range(old, old + new):
            start = (run_of * run_slots).astype(jnp.float32)
            line = jnp.concatenate(
                [
                    ref[at : at + size, 0:depth].astype(jnp.float32)[row : row + 1] + start
                    for ref, _, at, size, row in refs[index]
                ],
                axis=1,
            )
            column = jnp.sum(jnp.where(diagonal, line, 0.0), axis=1, keepdims=True)
            states[2 * index][...] = jnp.broadcast_to(column, (rows, LANES))
            block = load(index)
            best = jnp.full((8, rows), -1.0, jnp.float32)
            for other in range(index + 1):
                scores = lax.dot_general(
                    load(other),
                    block,
                    (((1,), (1,)), ((), ())),
                    preferred_element_type=jnp.float32,
                )
                place = states[2 * other][...]
                earlier = jnp.concatenate([place] * (rows // LANES), axis=1) < line
                kept = jnp.where(earlier, scores, -2.0)
                best = jnp.maximum(best, jnp.max(kept.reshape(rows // 8, 8, rows), axis=0))
                if other < index:
                    given = halves(jnp.where(earlier, -2.0, scores))
                    states[2 * other + 1][...] = jnp.maximum(states[2 * other + 1][...], given)
            best = jnp.max(best, axis=0, keepdims=True)
            states[2 * index + 1][...] = halves(jnp.where(diagonal, best, -2.0))

    if last:
        chunk = found_ref.shape[1]

        @pl.when(jnp.logical_not(is_home))
        def _():
            for ref in chunk_refs:
                ref[...] = jnp.zeros_like(ref)

        @pl.when(is_home)
        def _():
            members = jnp.concatenate([count_ref[0:1, :]] * (run_slots // LANES), axis=1)
            lane = lax.broadcasted_iota(jnp.int32, (run_slots, run_slots), 1)
            for run in range(runs):
                where = [
                    (index, low + run * PIECE) for index in range(old + new) for low in (0, depth)
                ]
                place, best = (
                    jnp.concatenate([states[2 * n + kind][at : at + PIECE, :] for n, at in where])
                    for kind in range(2)
                )
                best = jnp.max(best, axis=1, keepdims=True)
                place = jnp.concatenate([place] * (run_slots // LANES), axis=1)
                base = run * run_slots
                position = (lane + base).astype(jnp.float32)
                found = jnp.sum(jnp.where(place == position, best, 0.0), axis=0, keepdims=True)
                found = jnp.where(position[0:1] < members, found, 0.0)
                row, low = base // chunk, base % chunk
                found_ref[row : row + 1, low : low + run_slots] = found

        chain_len = len(chunk_refs)
        for home in (chain_len // 2 - 1, chain_len // 2):
            @pl.when(lax.axis_index("chain") == home)
            def _():
                for step, ref in enumerate(chunk_refs):
                    row = home ^ step
                    ref[...] = jnp.where(is_home, found_ref[row : row + 1, :], 0.0)


def local_home(embeddings, dest, sizes):
    chain_len = lax.axis_size("chain")
    clus_len = lax.axis_size("clus")
    rows, width = embeddings.shape
    half = rows // 2
    run_slots = chain_len * clus_len * PIECE
    block = jax.ShapeDtypeStruct((half + TILE, width), jnp.bfloat16)
    depth = rows // clus_len
    hot, slots = pl.pallas_call(
        functools.partial(place_kernel, run_slots, depth // PIECE),
        out_shape=(
            jax.ShapeDtypeStruct((rows, rows), jnp.bfloat16),
            jax.ShapeDtypeStruct((TILE, rows), jnp.float32),
        ),
        in_specs=[VMEM],
        out_specs=(VMEM, VMEM),
        compiler_params=pltpu.CompilerParams(vmem_limit_bytes=16 * 2**20),
        name="place_rows",
    )(dest.reshape(1, rows))
    near, far, near_other, far_other = pl.pallas_call(
        send_kernel,
        out_shape=(jax.ShapeDtypeStruct((depth + TILE, width), jnp.bfloat16),) * clus_len,
        in_specs=[VMEM] * 3,
        out_specs=(VMEM,) * clus_len,
        compiler_params=pltpu.CompilerParams(vmem_limit_bytes=16 * 2**20),
        name="send_blocks",
    )(hot, slots, embeddings)

    def permute(value, moves):
        pairs = [(a * clus_len + b, c * clus_len + d) for a, b, c, d in moves]
        return lax.ppermute(value, ("chain", "clus"), pairs)

    low, high, top = chain_len // 2 - 1, chain_len // 2, chain_len - 1
    places = [(z, k) for z in range(chain_len) for k in range(clus_len)]

    def swap(value):
        return permute(value, [(z, k, z, k ^ 1) for z, k in places])

    def along(value, steps):
        return permute(value, [(z, k, steps[z], k) if z in steps else (z, k, z, k ^ 1) for z, k in places])

    def crossed(value):
        came = permute(value, [(z, k, z, k ^ 2) for z, k in places])
        return pl.pallas_call(
            merge_kernel,
            out_shape=block,
            in_specs=[VMEM, VMEM],
            out_specs=VMEM,
            compiler_params=pltpu.CompilerParams(vmem_limit_bytes=16 * 2**20),
            name="merge_blocks",
        )(came, swap(came)), came

    def to_home(value, moves):
        pairs = []
        for a, b in moves:
            pairs += [(a, k ^ (a >= high), b, k ^ (b >= high)) for k in range(0, clus_len, 2)]
        return permute(value, pairs)

    far_crossed, far_came = crossed(far_other)
    near_crossed, near_came = crossed(near_other)
    from_far = along(far, {0: high, high: top, top: low, low: 0})
    from_middle = along(far, {low: high, high: low})
    from_near = along(near, {0: low, low: 0, top: high, high: top})
    own = (near, from_near, from_far, from_middle)
    helped = pl.pallas_call(
        functools.partial(helper_kernel, len(own)),
        out_shape=jax.ShapeDtypeStruct((len(own) * (depth + TILE), width), jnp.bfloat16),
        in_specs=[VMEM] * (len(own) + 2),
        out_specs=VMEM,
        compiler_params=pltpu.CompilerParams(vmem_limit_bytes=16 * 2**20),
        name="help_home",
    )(*own, far_came, near_came)
    helped = swap(helped)
    far_after = to_home(far_crossed, [(0, high), (top, low)])
    middle_after = to_home(far_crossed, [(low, high), (high, low)])
    near_after = to_home(near_crossed, [(0, low), (top, high)])
    stages = [[*own], [near_crossed, far_after], [helped], [near_after], [middle_after]]
    blocks, states, held = [], [], 0
    state = jax.ShapeDtypeStruct((half, LANES), jnp.float32)
    chunk = jax.ShapeDtypeStruct((1, rows), jnp.float32)
    for number, arrived in enumerate(stages):
        first, last = number == 0, number == len(stages) - 1
        old, blocks = held, blocks + arrived
        held = sum(value.shape[0] // depth for value in blocks) // 2
        outs = (chunk,) * chain_len if last else (state,) * (2 * held)
        outs += (jax.ShapeDtypeStruct((TILE, LANES), jnp.float32),) * first
        scratch = [pltpu.VMEM(state.shape, state.dtype)] * (2 * held)
        scratch.append(pltpu.VMEM((chain_len, rows), jnp.float32))
        count = [sizes] if first else [members] if last else []
        states = pl.pallas_call(
            functools.partial(stage_kernel, run_slots, half + TILE, len(blocks), old, held - old, last),
            out_shape=outs,
            in_specs=[SMEM] * first + [VMEM] * (last + len(blocks) + len(states)),
            out_specs=(VMEM,) * len(outs),
            scratch_shapes=scratch * last,
            compiler_params=pltpu.CompilerParams(vmem_limit_bytes=32 * 2**20),
            name="multiply_last" if last else "multiply_arrived",
        )(*count, *blocks, *states)
        if first:
            *states, members = states
    found = states[0]
    for step in range(1, chain_len):
        homes = [(low + k % 2, k) for k in range(clus_len)]
        found = found + permute(states[step], [(home, k, home ^ step, k) for home, k in homes])
    return found


def solution(mesh):
    return jax.shard_map(
        local_home if mesh.shape["chain"] == mesh.shape["clus"] == 4 else local_plane,
        mesh=mesh,
        in_specs=(
            P(("groups", "chain", "clus"), None),
            P(("groups", "chain", "clus")),
            P("groups"),
        ),
        out_specs=P(("groups", "clus"), "chain"),
        check_vma=False,
    )
```

```python
import functools

import jax
import jax.numpy as jnp
from jax import lax
from jax.experimental import pallas as pl
from jax.experimental.pallas import tpu as pltpu
from jax.sharding import PartitionSpec as P

TILE = 8
LANES = 128
PIECE = 16
VMEM = pl.BlockSpec(memory_space=pltpu.VMEM)
SMEM = pl.BlockSpec(memory_space=pltpu.SMEM)


def as_bf16(mask):
    return mask.astype(jnp.float32).astype(jnp.bfloat16)


def sort_kernel(run_slots, dest_ref, rows_ref, units_ref, slots_ref):
    rows = rows_ref.shape[0]
    runs = rows // PIECE
    dest = dest_ref[...]
    run = dest // run_slots
    within = dest % run_slots
    member = lax.broadcasted_iota(jnp.int32, (runs, rows), 0) == run
    before = lax.broadcasted_iota(jnp.int32, (rows, rows), 0) < lax.broadcasted_iota(
        jnp.int32, (rows, rows), 1
    )
    earlier = jnp.dot(
        member.astype(jnp.float32).astype(jnp.bfloat16),
        before.astype(jnp.float32).astype(jnp.bfloat16),
        preferred_element_type=jnp.float32,
    )
    rank = jnp.sum(jnp.where(member, earlier, 0.0), axis=0, keepdims=True).astype(jnp.int32)
    placed = run * PIECE + rank
    hot = (lax.broadcasted_iota(jnp.int32, (rows, rows), 0) == placed).astype(jnp.float32)
    hot = hot.astype(jnp.bfloat16)
    x = rows_ref[...].astype(jnp.float32)
    units = (x * lax.rsqrt(jnp.sum(x * x, axis=1, keepdims=True) + 1e-06)).astype(jnp.bfloat16)
    units_ref[...] = jnp.dot(hot, units, preferred_element_type=jnp.float32).astype(jnp.bfloat16)
    halves = jnp.concatenate(
        [jnp.broadcast_to(within // 256, (8, rows)), jnp.broadcast_to(within % 256, (8, rows))], axis=0
    )
    moved = lax.dot_general(
        halves.astype(jnp.float32).astype(jnp.bfloat16),
        hot,
        (((1,), (1,)), ((), ())),
        preferred_element_type=jnp.float32,
    )
    slots_ref[...] = (moved[0:1, :] * 256.0 + moved[8:9, :]).astype(jnp.int32)


def best_kernel(info_ref, slots_ref, keys_ref, out_ref, query_ref):
    shards, depth, width = keys_ref.shape
    queries = out_ref.shape[1]
    run_slots = shards * PIECE
    unit = min(run_slots, queries)
    first = info_ref[0]
    members = info_ref[1]
    first_run = first // run_slots

    def run_rows(run):
        start = pl.multiple_of(run * PIECE, PIECE)
        return keys_ref[:, pl.ds(start, PIECE), :].reshape(run_slots, width)

    def run_positions(run):
        start = pl.multiple_of(run * PIECE, PIECE)
        tile = slots_ref[pl.ds(start, PIECE), :]
        wide = jnp.broadcast_to(tile[None], (shards, PIECE, shards)).reshape(run_slots, shards)
        lane = lax.broadcasted_iota(jnp.int32, (run_slots, shards), 1)
        row = lax.broadcasted_iota(jnp.int32, (run_slots, shards), 0)
        picked = jnp.sum(jnp.where(lane == row // PIECE, wide, 0), axis=1, keepdims=True)
        return picked + run * run_slots

    for index in range(queries // unit):
        run = first_run + index
        lanes = lax.broadcasted_iota(jnp.int32, (run_slots, unit), 1) + (first + index * unit)
        hot = (run_positions(run) == lanes).astype(jnp.float32).astype(jnp.bfloat16)
        query_ref[:, index * unit : (index + 1) * unit] = lax.dot_general(
            run_rows(run), hot, (((0,), (0,)), ((), ())), preferred_element_type=jnp.float32
        ).astype(jnp.bfloat16)

    def fold(scores):
        return jnp.max(scores.reshape(run_slots // 8, 8, queries), axis=0)

    def step(run, running):
        scores = jnp.dot(run_rows(run), query_ref[...], preferred_element_type=jnp.float32)
        return jnp.maximum(running, fold(scores))

    running = lax.fori_loop(0, first_run, step, jnp.full((8, queries), -1.0, jnp.float32))
    position = first + lax.broadcasted_iota(jnp.int32, (1, queries), 1)
    for index in range(queries // unit):
        run = first_run + index
        scores = jnp.dot(run_rows(run), query_ref[...], preferred_element_type=jnp.float32)
        masked = jnp.where(run_positions(run) < position, scores, -2.0)
        running = jnp.maximum(running, fold(masked))
    found = jnp.max(running, axis=0, keepdims=True)
    out_ref[...] = jnp.where(position < members, found, 0.0)


def local_plane(embeddings, dest, sizes):
    chain_len = lax.axis_size("chain")
    clus_len = lax.axis_size("clus")
    shards = chain_len * clus_len
    rows, width = embeddings.shape
    clusters = sizes.shape[0]
    parts = chain_len // clusters
    run_slots = shards * PIECE
    depth = rows // chain_len
    my_chain = lax.axis_index("chain")
    my_clus = lax.axis_index("clus")
    cluster = my_chain // parts
    part = my_chain % parts

    units, slots = pl.pallas_call(
        functools.partial(sort_kernel, run_slots),
        out_shape=(
            jax.ShapeDtypeStruct((rows, width), jnp.bfloat16),
            jax.ShapeDtypeStruct((1, rows), jnp.int32),
        ),
        in_specs=[VMEM, VMEM],
        out_specs=(VMEM, VMEM),
        compiler_params=pltpu.CompilerParams(vmem_limit_bytes=32 * 2**20),
        name="sort_units",
    )(dest.reshape(1, rows), embeddings)

    slots = lax.all_gather(slots, ("chain", "clus"), axis=0, tiled=True)
    slots = slots.reshape(chain_len, clus_len, clusters, -1, PIECE)
    slots = lax.dynamic_index_in_dim(slots, cluster, 2, keepdims=False)
    slots = slots.transpose(2, 3, 1, 0).reshape(-1, shards)

    got = lax.all_to_all(units, "chain", split_axis=0, concat_axis=0, tiled=True)
    keys = lax.all_gather(got, "clus", axis=0, tiled=True).reshape(shards, depth, width)
    if parts > 1:
        pieces = []
        for wanted in range(parts):
            block = keys
            for other in range(parts):
                if other != wanted:
                    pairs = [(c * parts + wanted, c * parts + other) for c in range(clusters)]
                    came = lax.ppermute(keys, "chain", pairs)
                    block = jnp.where(part == other, came, block)
            pieces.append(block)
        keys = jnp.concatenate(pieces, axis=1)

    first = (part * clus_len + my_clus) * rows
    ids = jnp.arange(clusters, dtype=jnp.int32)
    members = jnp.sum(jnp.where(ids == cluster, sizes, 0))
    info = jnp.stack([first, members]).astype(jnp.int32)
    found = pl.pallas_call(
        best_kernel,
        out_shape=jax.ShapeDtypeStruct((1, rows), jnp.float32),
        in_specs=[SMEM, VMEM, VMEM],
        out_specs=VMEM,
        scratch_shapes=[pltpu.VMEM((width, rows), jnp.bfloat16)],
        compiler_params=pltpu.CompilerParams(vmem_limit_bytes=48 * 2**20),
        name="best_of_earlier",
    )(info, slots, keys)

    pairs = []
    for z in range(chain_len):
        for k in range(clus_len):
            pairs.append((z * clus_len + k, ((z % parts) * clus_len + k) * clus_len + z // parts))
    return lax.ppermute(found, ("chain", "clus"), pairs)


def send_kernel(run_slots, cluster_runs, dest_ref, rows_ref, kept_ref, slots_ref, given_ref):
    rows, width = rows_ref.shape
    runs = rows // PIECE
    half = rows // 2
    depth = half // 2
    clus = lax.axis_index("clus")
    upper = (lax.axis_index("chain") >= lax.axis_size("chain") // 2).astype(jnp.int32)
    code = (clus // 2 ^ clus % 2 ^ upper) * 2 + upper
    before = lax.broadcasted_iota(jnp.int32, (rows, rows), 0) < lax.broadcasted_iota(
        jnp.int32, (rows, rows), 1
    )
    dest = dest_ref[...]
    run = lax.div(dest, run_slots)
    within = lax.rem(dest, run_slots)
    run = (lax.div(run, cluster_runs) ^ code) * cluster_runs + lax.rem(run, cluster_runs)
    member = lax.broadcasted_iota(jnp.int32, (runs, rows), 0) == run
    earlier = jnp.dot(as_bf16(member), as_bf16(before), preferred_element_type=jnp.float32)
    rank = jnp.sum(jnp.where(member, earlier, 0.0), axis=0, keepdims=True).astype(jnp.int32)
    hot = as_bf16(lax.broadcasted_iota(jnp.int32, (rows, rows), 0) == run * PIECE + rank)
    moved = lax.dot_general(
        jnp.broadcast_to(within, (TILE, rows)).astype(jnp.float32).astype(jnp.bfloat16),
        hot,
        (((1,), (1,)), ((), ())),
        preferred_element_type=jnp.float32,
    )
    x = rows_ref[...].astype(jnp.float32)
    units = (x * lax.rsqrt(jnp.sum(x * x, axis=1, keepdims=True) + 1e-06)).astype(jnp.bfloat16)
    for low, ref in ((0, kept_ref), (half, given_ref)):
        ref[0:half, :] = jnp.dot(
            hot[low : low + half], units, preferred_element_type=jnp.float32
        ).astype(jnp.bfloat16)
    line = lax.broadcasted_iota(jnp.int32, (TILE, half), 0)
    slots_ref[...] = jnp.where(line == 0, moved[:, 0:half], 0.0)
    given_ref[half : half + TILE, :] = jnp.zeros((TILE, width), jnp.bfloat16)
    given_ref[half : half + TILE, 0:half] = jnp.where(line == 1, moved[:, half:rows], 0.0).astype(
        jnp.bfloat16
    )


def merge_kernel(kept_ref, slots_ref, came_ref, near_ref, far_ref):
    half, width = kept_ref.shape
    depth = half // 2
    slots = slots_ref[...] + came_ref[half : half + TILE, 0:half].astype(jnp.float32)
    for low, ref in ((0, near_ref), (depth, far_ref)):
        ref[0:depth, :] = kept_ref[low : low + depth, :]
        ref[depth:half, :] = came_ref[low : low + depth, :]
        ref[half : half + TILE, :] = jnp.zeros((TILE, width), jnp.bfloat16)
        ref[half : half + TILE, 0:depth] = slots[:, low : low + depth].astype(jnp.bfloat16)


def home_chain():
    return lax.axis_size("chain") // 2 - 1 + lax.axis_index("clus") % 2


def stage_kernel(run_slots, height, count, old, new, last, *rest):
    first = old == 0
    count_ref, rest = (rest[0], rest[1:]) if first or last else (None, rest)
    refs = []
    for ref in rest[:count]:
        refs += [ref.at[pl.ds(low, height)] for low in range(0, ref.shape[0], height)]
    rest = rest[count:]
    old_states, rest = rest[: 2 * old], rest[2 * old :]
    if last:
        chunk_refs = rest[: -1 - 2 * (old + new)]
        states, found_ref = rest[len(chunk_refs) : -1], rest[-1]
    else:
        states = rest[: 2 * (old + new)]
    rows = refs[0].shape[0] - TILE
    depth = rows // 2
    runs = depth // PIECE
    is_home = lax.axis_index("chain") == home_chain()

    def halves(value):
        best = value[:, 0:LANES]
        for low in range(LANES, value.shape[1], LANES):
            best = jnp.maximum(best, value[:, low : low + LANES])
        return best

    if first:
        members = count_ref[lax.axis_index("clus")].astype(jnp.float32)
        rest[-1][...] = jnp.full_like(rest[-1], members)

    @pl.when(is_home)
    def _():
        for index in range(old):
            states[2 * index][...] = old_states[2 * index][...]
            states[2 * index + 1][...] = old_states[2 * index + 1][...]
        diagonal = lax.broadcasted_iota(jnp.int32, (rows, rows), 0) == lax.broadcasted_iota(
            jnp.int32, (rows, rows), 1
        )
        run_of = lax.broadcasted_iota(jnp.int32, (1, depth), 1) // PIECE
        for index in range(old, old + new):
            slots = refs[index][rows : rows + TILE, 0:depth].astype(jnp.float32)
            start = (run_of * run_slots).astype(jnp.float32)
            line = jnp.concatenate([slots[0:1] + start, slots[1:2] + start], axis=1)
            column = jnp.sum(jnp.where(diagonal, line, 0.0), axis=1, keepdims=True)
            states[2 * index][...] = jnp.broadcast_to(column, (rows, LANES))
            block = refs[index][0:rows, :]
            best = jnp.full((8, rows), -1.0, jnp.float32)
            for other in range(index + 1):
                scores = lax.dot_general(
                    refs[other][0:rows, :],
                    block,
                    (((1,), (1,)), ((), ())),
                    preferred_element_type=jnp.float32,
                )
                place = states[2 * other][...]
                earlier = jnp.concatenate([place] * (rows // LANES), axis=1) < line
                kept = jnp.where(earlier, scores, -2.0)
                best = jnp.maximum(best, jnp.max(kept.reshape(rows // 8, 8, rows), axis=0))
                if other < index:
                    given = halves(jnp.where(earlier, -2.0, scores))
                    states[2 * other + 1][...] = jnp.maximum(states[2 * other + 1][...], given)
            best = jnp.max(best, axis=0, keepdims=True)
            states[2 * index + 1][...] = halves(jnp.where(diagonal, best, -2.0))

    if last:
        chunk = found_ref.shape[1]

        @pl.when(jnp.logical_not(is_home))
        def _():
            for ref in chunk_refs:
                ref[...] = jnp.zeros_like(ref)

        @pl.when(is_home)
        def _():
            members = jnp.concatenate([count_ref[0:1, :]] * (run_slots // LANES), axis=1)
            lane = lax.broadcasted_iota(jnp.int32, (run_slots, run_slots), 1)
            for run in range(runs):
                where = [
                    (index, low + run * PIECE) for index in range(old + new) for low in (0, depth)
                ]
                place, best = (
                    jnp.concatenate([states[2 * n + kind][at : at + PIECE, :] for n, at in where])
                    for kind in range(2)
                )
                best = jnp.max(best, axis=1, keepdims=True)
                place = jnp.concatenate([place] * (run_slots // LANES), axis=1)
                base = run * run_slots
                position = (lane + base).astype(jnp.float32)
                found = jnp.sum(jnp.where(place == position, best, 0.0), axis=0, keepdims=True)
                found = jnp.where(position[0:1] < members, found, 0.0)
                row, low = base // chunk, base % chunk
                found_ref[row : row + 1, low : low + run_slots] = found

        chain_len = len(chunk_refs)
        for home in (chain_len // 2 - 1, chain_len // 2):
            @pl.when(lax.axis_index("chain") == home)
            def _():
                for step, ref in enumerate(chunk_refs):
                    row = (home + step) % chain_len
                    ref[...] = jnp.where(is_home, found_ref[row : row + 1, :], 0.0)


def local_home(embeddings, dest, sizes):
    chain_len = lax.axis_size("chain")
    clus_len = lax.axis_size("clus")
    rows, width = embeddings.shape
    half = rows // 2
    run_slots = chain_len * clus_len * PIECE
    block = jax.ShapeDtypeStruct((half + TILE, width), jnp.bfloat16)
    kept, slots, given = pl.pallas_call(
        functools.partial(send_kernel, run_slots, rows // clus_len // PIECE),
        out_shape=(
            jax.ShapeDtypeStruct((half, width), jnp.bfloat16),
            jax.ShapeDtypeStruct((TILE, half), jnp.float32),
            block,
        ),
        in_specs=[VMEM, VMEM],
        out_specs=(VMEM, VMEM, VMEM),
        compiler_params=pltpu.CompilerParams(vmem_limit_bytes=32 * 2**20),
        name="send_blocks",
    )(dest.reshape(1, rows), embeddings)

    def permute(value, moves):
        pairs = [(a * clus_len + b, c * clus_len + d) for a, b, c, d in moves]
        return lax.ppermute(value, ("chain", "clus"), pairs)

    low, high, top = chain_len // 2 - 1, chain_len // 2, chain_len - 1
    swap = [(z, k, z, k ^ 1) for z in range(chain_len) for k in range(clus_len)]
    near, far = pl.pallas_call(
        merge_kernel,
        out_shape=(block, block),
        in_specs=[VMEM, VMEM, VMEM],
        out_specs=(VMEM, VMEM),
        compiler_params=pltpu.CompilerParams(vmem_limit_bytes=16 * 2**20),
        name="merge_blocks",
    )(kept, slots, permute(given, swap))

    def serving(z, across):
        return across ^ (z >= high)

    def to_home(value, moves):
        columns = range(clus_len // 2)
        return permute(
            value, [(a, 2 * x + serving(a, 0), b, 2 * x + serving(b, 0)) for a, b in moves for x in columns]
        )

    def across(value):
        pairs = []
        for z in range(chain_len):
            for x in range(clus_len // 2):
                own, other = serving(z, 0), serving(z, 1)
                pairs.append((z, 2 * x + other, z, 2 * (x ^ 1) + own))
                pairs.append((z, 2 * x + own, z, 2 * x + other))
        return permute(value, pairs)

    from_far = [(0, high), (top, low)]
    from_near = [(0, low), (top, high)]
    from_middle = [(low, high), (high, low)]
    far_crossed, near_crossed = across(far), across(near)
    far_along, near_along = to_home(far, from_far), to_home(near, from_near)
    middle_along = to_home(far, from_middle)
    far_after, near_after = to_home(far_crossed, from_far), to_home(near_crossed, from_near)
    middle_after = to_home(far_crossed, from_middle)
    stages = [
        [near, near_crossed, near_along, far_along],
        [far_after, middle_along],
        [near_after, middle_after],
    ]
    blocks, states, held = [], [], 0
    state = jax.ShapeDtypeStruct((half, LANES), jnp.float32)
    chunk = jax.ShapeDtypeStruct((1, rows), jnp.float32)
    for number, arrived in enumerate(stages):
        first, last = number == 0, number == len(stages) - 1
        old, blocks = held, blocks + arrived
        held = sum(value.shape[0] for value in blocks) // (half + TILE)
        outs = (chunk,) * chain_len if last else (state,) * (2 * held)
        outs += (jax.ShapeDtypeStruct((TILE, LANES), jnp.float32),) * first
        scratch = [pltpu.VMEM(state.shape, state.dtype)] * (2 * held)
        scratch.append(pltpu.VMEM((chain_len, rows), jnp.float32))
        count = [sizes] if first else [members] if last else []
        states = pl.pallas_call(
            functools.partial(stage_kernel, run_slots, half + TILE, len(blocks), old, held - old, last),
            out_shape=outs,
            in_specs=[SMEM] * first + [VMEM] * (last + len(blocks) + len(states)),
            out_specs=(VMEM,) * len(outs),
            scratch_shapes=scratch * last,
            compiler_params=pltpu.CompilerParams(vmem_limit_bytes=32 * 2**20),
            name="multiply_last" if last else "multiply_arrived",
        )(*count, *blocks, *states)
        if first:
            *states, members = states
    found = states[0]
    for step in range(1, chain_len):
        homes = [(low + k % 2, k) for k in range(clus_len)]
        moves = [(home, k, (home + step) % chain_len, k) for home, k in homes]
        found = found + permute(states[step], moves)
    return found


def solution(mesh):
    return jax.shard_map(
        local_home if mesh.shape["chain"] == mesh.shape["clus"] == 4 else local_plane,
        mesh=mesh,
        in_specs=(
            P(("groups", "chain", "clus"), None),
            P(("groups", "chain", "clus")),
            P("groups"),
        ),
        out_specs=P(("groups", "clus"), "chain"),
        check_vma=False,
    )
```
